32 devices in a mesh: batch: 16 (over z, y, x), pair: 2 (over core).
Axes of the slice: x: 2, y: 2, z: 4, core: 2. Of those that a mesh axis runs over, the one named last changes fastest.
Arguments:
- tokens: bfloat16 [64, 2, 160, 768], P('batch', 'pair'), may hold values from -6 to 6
- segment_ids: int32 [64, 2, 160], P('batch'), may hold values from -1 to 2, as said below
- query_weight: bfloat16 [768, 768], P(('batch', 'pair')), may hold values from -0.21875 to 0.21875
- query_bias: bfloat16 [768], P(('batch', 'pair')), may hold values from -3 to 3
- key_weight: bfloat16 [768, 768], P(('batch', 'pair')), may hold values from -0.21875 to 0.21875
- value_weight: bfloat16 [768, 768], P(('batch', 'pair')), may hold values from -0.21875 to 0.21875
- value_bias: bfloat16 [768], P(('batch', 'pair')), may hold values from -3 to 3
- out_weight: bfloat16 [768, 768], P(('batch', 'pair')), may hold values from -1.25 to 1.25
- out_bias: bfloat16 [768], P(('batch', 'pair')), may hold values from -3 to 3
- first_gain: bfloat16 [768], P(('batch', 'pair')), may hold values from 0.5 to 1.5
- first_shift: bfloat16 [768], P(('batch', 'pair')), may hold values from -2 to 2
- up_weight: bfloat16 [768, 3072], P(('batch', 'pair')), may hold values from -0.21875 to 0.21875
- up_bias: bfloat16 [3072], P(('batch', 'pair')), may hold values from -3 to 3
- down_weight: bfloat16 [3072, 768], P(('batch', 'pair')), may hold values from -0.109375 to 0.109375
- down_bias: bfloat16 [768], P(('batch', 'pair')), may hold values from -2 to 2
- second_gain: bfloat16 [768], P(('batch', 'pair')), may hold values from 0.5 to 1.5
- second_shift: bfloat16 [768], P(('batch', 'pair')), may hold values from -2 to 2
- cotangent: bfloat16 [64, 2, 160, 768], P('batch', 'pair'), may hold values from -6 to 6
Outputs:
- layer_output: bfloat16 [64, 2, 160, 768], P('batch', 'pair')
- tokens_gradient: bfloat16 [64, 2, 160, 768], P('batch', 'pair')
- query_weight_gradient: float32 [768, 768], P(('batch', 'pair'))
- query_bias_gradient: float32 [768], P(('batch', 'pair'))
- key_weight_gradient: float32 [768, 768], P(('batch', 'pair'))
- value_weight_gradient: float32 [768, 768], P(('batch', 'pair'))
- value_bias_gradient: float32 [768], P(('batch', 'pair'))
- out_weight_gradient: float32 [768, 768], P(('batch', 'pair'))
- out_bias_gradient: float32 [768], P(('batch', 'pair'))
- first_gain_gradient: float32 [768], P(('batch', 'pair'))
- first_shift_gradient: float32 [768], P(('batch', 'pair'))
- up_weight_gradient: float32 [768, 3072], P(('batch', 'pair'))
- up_bias_gradient: float32 [3072], P(('batch', 'pair'))
- down_weight_gradient: float32 [3072, 768], P(('batch', 'pair'))
- down_bias_gradient: float32 [768], P(('batch', 'pair'))
- second_gain_gradient: float32 [768], P(('batch', 'pair'))
- second_shift_gradient: float32 [768], P(('batch', 'pair'))
The draws below stay inside these ranges and needn't reach their ends.
Inputs may be any that keep to these rules, and one draw needn't show every extreme that they name: `segment_ids`: within each half of a sequence the ids never fall, pairs are numbered from 0 and each pair holds at least one word slot and one region slot; a sequence holds 2 or 3 pairs; -1 appears only after the last pair of a half, and word slots 96 and later are always -1.
All inputs are finite; a program needn't handle non-finite values.
Results may differ from the reference program's by a relative error of at most 0.014.
Values may be sent and summed in bfloat16 or wider, within the bound.
A program may use at most 192 MiB of HBM per device.

```python
import jax
import jax.numpy as jnp
from jax import lax

D = 768
HEADS = 12
HEAD_DIM = 64
FF = 3072
SLOT = 160
WORDS = 96
SEQS = 64


def half_labels(subkeys, number, length, triple):
    first_cut = jax.random.randint(subkeys[0], (number, 1), length // 5, 2 * length // 5)
    second_cut = jax.random.randint(subkeys[1], (number, 1), 3 * length // 5, 4 * length // 5)
    filled = jax.random.randint(subkeys[2], (number, 1), 4 * length // 5 + 1, length + 1)
    position = jnp.arange(SLOT, dtype=jnp.int32)[None, :]
    labels = (position >= first_cut).astype(jnp.int32) + triple[:, None] * (position >= second_cut).astype(jnp.int32)
    return jnp.where(position < filled, labels, -1).astype(jnp.int32)


def draw_segment_ids(key, part):
    key = jax.random.fold_in(key, 7)
    subkeys = jax.random.split(key, 7)
    number = SEQS
    triple = jax.random.randint(subkeys[0], (number,), 0, 2)
    triple = jnp.where(jnp.arange(number) == 0, 1, triple).astype(jnp.int32)
    word_labels = half_labels(subkeys[1:4], number, WORDS, triple)
    region_labels = half_labels(subkeys[4:7], number, SLOT, triple)
    return jnp.stack([word_labels, region_labels], 1)


def raised(array, own_key, source, target, shards_of, factor):
    def block_of(axis_at):
        return (jnp.arange(array.shape[axis_at]) // (array.shape[axis_at] // shards_of)).reshape((-1,) + (1,) * (array.ndim - 1 - axis_at))

    one_side = jax.random.permutation(own_key, shards_of)[block_of(target)]
    second = (block_of(target) + shards_of // 2) % shards_of
    return jnp.where((block_of(source) == one_side) | (block_of(source) == second), factor * array, array)


def levels(rng, shape, shards, smallest, high):
    level = 1.0
    for dim, parts in shards:
        draws = jax.random.uniform(jax.random.fold_in(jax.random.fold_in(rng, 6), dim), (parts,), jnp.float32, smallest / len(shards), high / len(shards))
        level = level * jnp.repeat(jnp.exp(draws), shape[dim] // parts).reshape((-1,) + (1,) * (len(shape) - 1 - dim))
    return level


def noise(key, dims, scale, reach, shards=(), held_as=jnp.bfloat16):
    level = levels(key, dims, shards, -0.22, 0.18) if shards else 1.0
    array = jax.random.normal(key, dims, jnp.float32) * scale * level
    return jnp.minimum(jnp.maximum(array, -reach), reach).astype(held_as)


def gaussian_with(own_key, dims, scale, most, cuts, heavy, kind=jnp.bfloat16):
    result = scale * jax.random.normal(own_key, dims, jnp.float32)
    if cuts:
        result = result * levels(own_key, dims, cuts, -0.22, 0.18)
    return jnp.clip(raised(result, jax.random.fold_in(own_key, 3), *heavy), -most, most).astype(kind)


def setup_inputs(seed: int = 0) -> dict:
    key_list = jax.random.split(jax.random.key(seed), 19)
    tokens = noise(key_list[0], (SEQS, 2, SLOT, D), 1.0, 6.0, ((0, 16), (1, 2)))
    segment_ids = draw_segment_ids(jax.random.fold_in(key_list[18], 71), 0)
    query_weight = noise(key_list[2], (D, D), D ** -0.5, 0.21875, ((0, 32),))
    query_bias = noise(key_list[3], (D,), 0.5, 3.0, ((0, 32),))
    key_weight = noise(key_list[4], (D, D), D ** -0.5, 0.21875, ((0, 32),))
    value_weight = noise(key_list[5], (D, D), D ** -0.5, 0.21875, ((0, 32),))
    value_bias = noise(key_list[6], (D,), 0.5, 3.0, ((0, 32),))
    out_weight = noise(key_list[7], (D, D), (D // 36) ** -0.5, 1.25, ((0, 32),))
    out_bias = noise(key_list[8], (D,), 0.5, 3.0, ((0, 32),))
    first_gain = jnp.clip(1.0 + 0.1 * jax.random.normal(key_list[9], (D,), jnp.float32), 0.5, 1.5).astype(jnp.bfloat16)
    first_shift = noise(key_list[10], (D,), 0.3, 2.0, ((0, 32),))
    up_weight = noise(key_list[11], (D, FF), D ** -0.5, 0.21875, ((0, 32),))
    up_bias = noise(key_list[12], (FF,), 0.5, 3.0, ((0, 32),))
    down_weight = noise(key_list[13], (FF, D), FF ** -0.5, 0.109375, ((0, 32),))
    down_bias = noise(key_list[14], (D,), 0.3, 2.0, ((0, 32),))
    second_gain = jnp.clip(1.0 + 0.1 * jax.random.normal(key_list[15], (D,), jnp.float32), 0.5, 1.5).astype(jnp.bfloat16)
    second_shift = noise(key_list[16], (D,), 0.3, 2.0, ((0, 32),))
    cotangent = gaussian_with(key_list[17], (SEQS, 2, SLOT, D), 1.0, 6.0, ((0, 16), (1, 2)), (0, 3, 16, 2.0))
    return dict(tokens=tokens, segment_ids=segment_ids, query_weight=query_weight, query_bias=query_bias, key_weight=key_weight, value_weight=value_weight, value_bias=value_bias, out_weight=out_weight, out_bias=out_bias, first_gain=first_gain, first_shift=first_shift, up_weight=up_weight, up_bias=up_bias, down_weight=down_weight, down_bias=down_bias, second_gain=second_gain, second_shift=second_shift, cotangent=cotangent)


HIGHEST = lax.Precision.HIGHEST
EPSILON = 1e-05
NEG_FILL = -1e+30

@jax.custom_vjp
def low(v):
    return lax.optimization_barrier(v.astype(jnp.bfloat16)).astype(jnp.float32)

@jax.custom_vjp
def low_back(v):
    return v

def low_keep(v):
    return (low(v), None)

def low_pass(kept, grad):
    return (grad,)

def back_keep(v):
    return (v, None)

def back_low(kept, grad):
    return (low(grad),)
low.defvjp(low_keep, low_pass)
low_back.defvjp(back_keep, back_low)

def both_low(value):
    return low_back(low(value))

def layer_norm(values, gain, shift):
    average = lax.optimization_barrier(jnp.mean(values, -1, keepdims=True))
    centred = values - average
    variance = lax.optimization_barrier(jnp.mean(centred * centred, -1, keepdims=True))
    return centred * lax.rsqrt(variance + EPSILON) * gain + shift

def product(left, right):
    return jnp.matmul(left, right, precision=HIGHEST)

def forward(weights, group_x, group_ids):
    query_weight, query_bias, key_weight, value_weight, value_bias, out_weight, out_bias, first_gain, first_shift, up_weight, up_bias, down_weight, down_bias, second_gain, second_shift = weights
    number = group_x.shape[0]
    row_count = group_x.shape[1] * group_x.shape[2]
    inputs = group_x.reshape(number, row_count, D)
    labels = group_ids.reshape(number, row_count)
    head_shape = (number, row_count, HEADS, HEAD_DIM)
    queries = both_low(product(inputs, query_weight) + query_bias).reshape(head_shape)
    keys_all = both_low(product(inputs, key_weight)).reshape(head_shape)
    values_all = both_low(product(inputs, value_weight) + value_bias).reshape(head_shape)
    allowed = (labels[:, :, None] == labels[:, None, :])[:, None]
    raw = jnp.einsum('gqhd,gkhd->ghqk', queries, keys_all, precision=HIGHEST) * HEAD_DIM ** (-0.5)
    scores = low_back(jnp.where(allowed, raw, NEG_FILL))
    row_max = lax.optimization_barrier(jnp.max(scores, -1, keepdims=True))
    log_total = row_max + jnp.log(lax.optimization_barrier(jnp.sum(jnp.exp(scores - row_max), -1, keepdims=True)))
    probs = low(jnp.exp(scores - log_total))
    mixed = jnp.einsum('ghqk,gkhd->gqhd', probs, values_all, precision=HIGHEST).reshape(number, row_count, D)
    mixed = both_low(mixed)
    first_resid = inputs + low_back(product(mixed, out_weight) + out_bias)
    normed = layer_norm(first_resid, first_gain, first_shift)
    pre_hidden = low_back(product(low(normed), up_weight) + up_bias)
    hidden = low(jax.nn.gelu(pre_hidden))
    second_resid = normed + low_back(product(hidden, down_weight) + down_bias)
    return layer_norm(second_resid, second_gain, second_shift).reshape(group_x.shape)

def reference(tokens, segment_ids, query_weight, query_bias, key_weight, value_weight, value_bias, out_weight, out_bias, first_gain, first_shift, up_weight, up_bias, down_weight, down_bias, second_gain, second_shift, cotangent):
    weights = tuple((weight_in.astype(jnp.float32) for weight_in in (query_weight, query_bias, key_weight, value_weight, value_bias, out_weight, out_bias, first_gain, first_shift, up_weight, up_bias, down_weight, down_bias, second_gain, second_shift)))
    blocks = SEQS // 8
    block_shape = (blocks, 8, 2, SLOT, D)
    token_blocks = tokens.astype(jnp.float32).reshape(block_shape)
    label_blocks = segment_ids.reshape(blocks, 8, 2, SLOT)
    cot_blocks = cotangent.astype(jnp.float32).reshape(block_shape)

    def advance(totals, block_in):
        group_x, group_ids, group_cot = block_in
        outcome, pullback = jax.vjp(lambda params, inputs: forward(params, inputs, group_ids), weights, group_x)
        weight_grads, input_grad = pullback(group_cot)
        totals = tuple((total + extra for total, extra in zip(totals, weight_grads)))
        return (totals, (outcome.astype(jnp.bfloat16), input_grad.astype(jnp.bfloat16)))
    start = tuple((jnp.zeros_like(weight_in) for weight_in in weights))
    grads, (outputs, input_grads) = lax.scan(advance, start, (token_blocks, label_blocks, cot_blocks))
    full_shape = (SEQS, 2, SLOT, D)
    return (outputs.reshape(full_shape), input_grads.reshape(full_shape), grads[0], grads[1], grads[2], grads[3], grads[4], grads[5], grads[6], grads[7], grads[8], grads[9], grads[10], grads[11], grads[12], grads[13], grads[14])
```

```python
import jax
import jax.numpy as jnp
from jax import lax
from jax.experimental import pallas as pl
from jax.experimental.pallas import tpu as pltpu
from jax.sharding import PartitionSpec as P

BATCH, PAIR = AXES = ("batch", "pair")
HEAD_DIM = 64


EPSILON = 1e-05
NEG_FILL = -1e30


def swapped(value, axis, stride):
    return lax.ppermute(value, axis, [(i, i ^ 1 << stride) for i in range(lax.axis_size(axis))])


def layer_norm(values, gain, shift):
    average = jnp.mean(values, -1, keepdims=True)
    centred = values - average
    variance = jnp.mean(centred * centred, -1, keepdims=True)
    return centred * lax.rsqrt(variance + EPSILON) * gain + shift


def matmul(left, right):
    return jnp.dot(left, right, preferred_element_type=jnp.float32)


def product_back(left, right):
    return lax.dot_general(
        left, right, (((left.ndim - 1,), (1,)), ((), ())), preferred_element_type=jnp.float32
    )


def outer_sum(left, right):
    flat_left = left.reshape(-1, left.shape[-1])
    flat_right = right.reshape(-1, right.shape[-1])
    return lax.dot_general(
        flat_left, flat_right, (((0,), (0,)), ((), ())), preferred_element_type=jnp.float32
    )


def row_total(values):
    return jnp.sum(values.astype(jnp.float32), (0, 1))


def scores_of(query_heads, key_rows, allowed, factor):
    raw = jnp.einsum("sqhd,skhd->shqk", query_heads, key_rows, preferred_element_type=jnp.float32)
    return jnp.where(allowed, raw * factor, NEG_FILL)


def local(
    tokens,
    segment_ids,
    query_weight,
    query_bias,
    key_weight,
    value_weight,
    value_bias,
    out_weight,
    out_bias,
    first_gain,
    first_shift,
    up_weight,
    up_bias,
    down_weight,
    down_bias,
    second_gain,
    second_shift,
    cotangent,
):
    seqs = tokens.shape[0]
    slots = tokens.shape[2]
    width = tokens.shape[3]
    heads = width // HEAD_DIM
    factor = HEAD_DIM ** (-0.5)
    token_rows = tokens.reshape(seqs, slots, width)
    attention_shards = (
        query_weight,
        query_bias,
        key_weight,
        value_weight,
        value_bias,
        out_weight,
        out_bias,
        first_gain,
        first_shift,
    )
    feedforward_shards = (up_weight, up_bias, down_weight, down_bias, second_gain, second_shift)
    attention_full = (
        lax.all_gather(attention_shards[0], AXES, axis=0, tiled=True),
        lax.all_gather(attention_shards[1], AXES, axis=0, tiled=True),
        lax.all_gather(attention_shards[2], AXES, axis=0, tiled=True),
        lax.all_gather(attention_shards[3], AXES, axis=0, tiled=True),
        lax.all_gather(attention_shards[4], AXES, axis=0, tiled=True),
        lax.all_gather(attention_shards[5], AXES, axis=0, tiled=True),
        lax.all_gather(attention_shards[6], AXES, axis=0, tiled=True),
        lax.all_gather(attention_shards[7], AXES, axis=0, tiled=True),
        lax.all_gather(attention_shards[8], AXES, axis=0, tiled=True),
    )
    feedforward_full = (
        lax.all_gather(feedforward_shards[0], AXES, axis=0, tiled=True),
        lax.all_gather(feedforward_shards[1], AXES, axis=0, tiled=True),
        lax.all_gather(feedforward_shards[2], AXES, axis=0, tiled=True),
        lax.all_gather(feedforward_shards[3], AXES, axis=0, tiled=True),
        lax.all_gather(feedforward_shards[4], AXES, axis=0, tiled=True),
        lax.all_gather(feedforward_shards[5], AXES, axis=0, tiled=True),
    )
    (
        query_mat,
        query_vec,
        key_mat,
        value_mat,
        value_vec,
        out_mat,
        out_vec,
        gain_first,
        shift_first,
    ) = attention_full
    up_mat, up_vec, down_mat, down_vec, gain_second, shift_second = feedforward_full
    pair_index = lax.axis_index(PAIR)
    own_ids = lax.dynamic_index_in_dim(segment_ids, pair_index, 1, keepdims=False)
    other_ids = lax.dynamic_index_in_dim(segment_ids, 1 - pair_index, 1, keepdims=False)
    key_ids = jnp.concatenate([own_ids, other_ids], 1)
    allowed = (own_ids[:, :, None] == key_ids[:, None, :])[:, None]
    queries = (matmul(token_rows, query_mat) + query_vec).astype(jnp.bfloat16)
    keys_own = matmul(token_rows, key_mat).astype(jnp.bfloat16)
    values_own = (matmul(token_rows, value_mat) + value_vec).astype(jnp.bfloat16)
    keys_other, values_other = swapped((keys_own, values_own), PAIR, 0)
    head_rows = (seqs, 2 * slots, heads, HEAD_DIM)
    key_rows = jnp.concatenate([keys_own, keys_other], 1).reshape(head_rows)
    value_rows = jnp.concatenate([values_own, values_other], 1).reshape(head_rows)
    query_heads = queries.reshape(seqs, slots, heads, HEAD_DIM)
    scores = scores_of(query_heads, key_rows, allowed, factor)
    row_max = jnp.max(scores, -1, keepdims=True)
    log_total = row_max + jnp.log(jnp.sum(jnp.exp(scores - row_max), -1, keepdims=True))
    probs_low = jnp.exp(scores - log_total).astype(jnp.bfloat16)
    mixed = jnp.einsum("shqk,skhd->sqhd", probs_low, value_rows, preferred_element_type=jnp.float32)
    mixed = mixed.reshape(seqs, slots, width).astype(jnp.bfloat16)
    first_resid = token_rows.astype(jnp.float32) + matmul(mixed, out_mat) + out_vec
    normed, first_pull = jax.vjp(
        layer_norm, first_resid, gain_first.astype(jnp.float32), shift_first.astype(jnp.float32)
    )
    normed_low = normed.astype(jnp.bfloat16)
    pre_hidden = matmul(normed_low, up_mat) + up_vec
    hidden, gelu_pull = jax.vjp(jax.nn.gelu, pre_hidden)
    hidden_low = hidden.astype(jnp.bfloat16)
    second_resid = normed + matmul(hidden_low, down_mat) + down_vec
    final, second_pull = jax.vjp(
        layer_norm, second_resid, gain_second.astype(jnp.float32), shift_second.astype(jnp.float32)
    )
    layer_output = final.astype(jnp.bfloat16).reshape(tokens.shape)
    out_grad = cotangent.reshape(seqs, slots, width).astype(jnp.float32)
    second_grad, gain_second_grad, shift_second_grad = second_pull(out_grad)
    down_in = second_grad.astype(jnp.bfloat16)
    down_weight_grad = outer_sum(hidden_low, down_in)
    down_bias_grad = row_total(down_in)
    hidden_grad = product_back(down_in, down_mat)
    (pre_grad,) = gelu_pull(hidden_grad)
    pre_low = pre_grad.astype(jnp.bfloat16)
    up_weight_grad = outer_sum(normed_low, pre_low)
    up_bias_grad = row_total(pre_low)
    normed_grad = product_back(pre_low, up_mat) + second_grad
    first_grad, gain_first_grad, shift_first_grad = first_pull(normed_grad)
    feedforward_terms = (
        up_weight_grad,
        up_bias_grad,
        down_weight_grad,
        down_bias_grad,
        gain_second_grad,
        shift_second_grad,
    )
    feedforward_parts = (
        lax.psum_scatter(feedforward_terms[0], AXES, scatter_dimension=0, tiled=True),
        lax.psum_scatter(feedforward_terms[1], AXES, scatter_dimension=0, tiled=True),
        lax.psum_scatter(feedforward_terms[2], AXES, scatter_dimension=0, tiled=True),
        lax.psum_scatter(feedforward_terms[3], AXES, scatter_dimension=0, tiled=True),
        lax.psum_scatter(feedforward_terms[4], AXES, scatter_dimension=0, tiled=True),
        lax.psum_scatter(feedforward_terms[5], AXES, scatter_dimension=0, tiled=True),
    )
    branch_low = first_grad.astype(jnp.bfloat16)
    out_weight_grad = outer_sum(mixed, branch_low)
    out_bias_grad = row_total(branch_low)
    mixed_grad = (
        product_back(branch_low, out_mat).astype(jnp.bfloat16).reshape(seqs, slots, heads, HEAD_DIM)
    )
    scores = scores_of(query_heads, key_rows, allowed, factor)
    probs = jnp.exp(scores - log_total)
    probs_low = probs.astype(jnp.bfloat16)
    probs_grad = jnp.einsum(
        "sqhd,skhd->shqk", mixed_grad, value_rows, preferred_element_type=jnp.float32
    )
    delta = jnp.sum(probs * probs_grad, -1, keepdims=True)
    score_grad = (probs * (probs_grad - delta)).astype(jnp.bfloat16)
    query_grad = (
        jnp.einsum("shqk,skhd->sqhd", score_grad, key_rows, preferred_element_type=jnp.float32)
        * factor
    )
    query_grad = query_grad.reshape(seqs, slots, width).astype(jnp.bfloat16)
    key_grad_all = jnp.einsum(
        "shqk,sqhd->skhd", score_grad, query_heads, preferred_element_type=jnp.float32
    )
    key_grad_all = (key_grad_all * factor).reshape(seqs, 2 * slots, width)
    value_grad_all = jnp.einsum(
        "shqk,sqhd->skhd", probs_low, mixed_grad, preferred_element_type=jnp.float32
    )
    value_grad_all = value_grad_all.reshape(seqs, 2 * slots, width)
    keys_back, values_back = (
        swapped(key_grad_all[:, slots:].astype(jnp.bfloat16), PAIR, 0).astype(jnp.float32),
        swapped(value_grad_all[:, slots:].astype(jnp.bfloat16), PAIR, 0).astype(jnp.float32),
    )
    key_grad = (key_grad_all[:, :slots] + keys_back).astype(jnp.bfloat16)
    value_grad = (value_grad_all[:, :slots] + values_back).astype(jnp.bfloat16)
    query_weight_grad = outer_sum(token_rows, query_grad)
    query_bias_grad = row_total(query_grad)
    key_weight_grad = outer_sum(token_rows, key_grad)
    value_weight_grad = outer_sum(token_rows, value_grad)
    value_bias_grad = row_total(value_grad)
    tokens_grad = first_grad + product_back(query_grad, query_mat) + product_back(key_grad, key_mat)
    tokens_grad = tokens_grad + product_back(value_grad, value_mat)
    tokens_gradient = tokens_grad.astype(jnp.bfloat16).reshape(tokens.shape)
    attention_terms = (
        query_weight_grad,
        query_bias_grad,
        key_weight_grad,
        value_weight_grad,
        value_bias_grad,
        out_weight_grad,
        out_bias_grad,
        gain_first_grad,
        shift_first_grad,
    )
    attention_parts = (
        lax.psum_scatter(attention_terms[0], AXES, scatter_dimension=0, tiled=True),
        lax.psum_scatter(attention_terms[1], AXES, scatter_dimension=0, tiled=True),
        lax.psum_scatter(attention_terms[2], AXES, scatter_dimension=0, tiled=True),
        lax.psum_scatter(attention_terms[3], AXES, scatter_dimension=0, tiled=True),
        lax.psum_scatter(attention_terms[4], AXES, scatter_dimension=0, tiled=True),
        lax.psum_scatter(attention_terms[5], AXES, scatter_dimension=0, tiled=True),
        lax.psum_scatter(attention_terms[6], AXES, scatter_dimension=0, tiled=True),
        lax.psum_scatter(attention_terms[7], AXES, scatter_dimension=0, tiled=True),
        lax.psum_scatter(attention_terms[8], AXES, scatter_dimension=0, tiled=True),
    )
    return (
        layer_output,
        tokens_gradient,
        attention_parts[0],
        attention_parts[1],
        attention_parts[2],
        attention_parts[3],
        attention_parts[4],
        attention_parts[5],
        attention_parts[6],
        attention_parts[7],
        attention_parts[8],
        feedforward_parts[0],
        feedforward_parts[1],
        feedforward_parts[2],
        feedforward_parts[3],
        feedforward_parts[4],
        feedforward_parts[5],
    )


F32 = jnp.float32
BF16 = jnp.bfloat16
MESH = pl.DeviceIdType.MESH
CHIPS = 16
LINE = 4
VMEM_BYTES = 63 * 1024 * 1024


def dot(left, right, left_dim, right_dim, precision=None):
    return lax.dot_general(
        left,
        right,
        (((left_dim,), (right_dim,)), ((), ())),
        preferred_element_type=F32,
        precision=precision,
    )


def nn(left, right):
    return dot(left, right, 1, 0)


def nt(left, right):
    return dot(left, right, 1, 1)


def tn(left, right):
    return dot(left, right, 0, 0)


def iota(shape, dim):
    return lax.broadcasted_iota(jnp.int32, shape, dim)


class Refs(dict):
    __getattr__ = dict.__getitem__
    __setattr__ = dict.__setitem__


def column_sum(values):
    return jnp.sum(values, 0, keepdims=True)


def lane_mean(values):
    return jnp.mean(values, -1, keepdims=True)


def block(start, size):
    return pl.ds(pl.multiple_of(start * size, size), size)


def each(count, act):
    def step(s, carry):
        act(s)
        return carry

    lax.fori_loop(0, count, step, 0)


class Links:
    def __init__(self):
        self.b = lax.axis_index(BATCH)
        self.p = lax.axis_index(PAIR)
        self.z = lax.div(self.b, 4)
        x = lax.rem(self.b, 2)
        y = lax.rem(lax.div(self.b, 2), 2)
        self.f = x + self.p * (y - x)
        self.g = y + self.p * (x - y)
        self.near = self.chip(self.z, 1)
        self.far = self.index(self.z, self.f, 1 - self.g)
        third = lax.div(self.z, 3)
        second = lax.div(self.z, 2) - third
        zeroth = 1 - lax.div(self.z + 3, 4)
        self.is_z = (zeroth, 1 - zeroth - second - third, second, third)

    def index(self, z, f, g):
        return 4 * z + (1 + self.p) * f + (2 - self.p) * g

    def chip(self, z, side):
        return self.index(z, self.f + side * (1 - 2 * self.f), self.g)

    def by_z(self, values):
        return sum(flag * value for flag, value in zip(self.is_z, values))

    def column(self):
        return [lax.rem(self.z + step, LINE) for step in (1, 3, 2)]

    def other(self):
        return (self.b, 1 - self.p)

    def greet(self):
        semaphore = pltpu.get_barrier_semaphore()
        partners = [self.chip(z, 0) for z in self.column()] + [self.near, self.far]
        for device in [(chip, self.p) for chip in partners] + [self.other()]:
            pl.semaphore_signal(semaphore, inc=1, device_id=device, device_id_type=MESH)

    def meet(self):
        pl.semaphore_wait(pltpu.get_barrier_semaphore(), 6)


class Gather:
    ARRIVE = ((1, 2, 3), (2, 0, 3), (3, 1, 0), (2, 1, 0))
    FROM_FAR = CHIPS
    ARRIVALS = CHIPS + 1

    def __init__(self, links, ref, send, recv, near_first=False):
        self.links, self.ref, self.send, self.recv = links, ref, send, recv
        self.size = ref.shape[0] // CHIPS
        self.near_first = near_first

    def copy(self, rows, chip, arrival):
        part = self.ref.at[rows]
        return pltpu.make_async_remote_copy(
            src_ref=part,
            dst_ref=part,
            send_sem=self.send,
            recv_sem=self.recv.at[arrival],
            device_id=(chip, self.links.p),
            device_id_type=MESH,
        )

    def wait(self, shard):
        self.copy(block(shard, self.size), self.links.far, shard).wait_recv()

    def to_far(self, z, side):
        shard = self.links.chip(z, side)
        self.copy(block(shard, self.size), self.links.far, self.FROM_FAR).start()

    def to_near(self, z):
        shard = self.links.chip(z, 0)
        self.copy(block(shard, self.size), self.links.near, shard).start()

    def to_column(self, z, side):
        k = self.links
        shard = k.chip(k.z, side)
        self.copy(block(shard, self.size), k.chip(z, 0), shard).start()

    def own(self):
        k = self.links
        self.to_near(k.z)
        self.to_far(k.z, 0)
        for z in k.column():
            self.to_column(z, 0)

    def near(self, turn):
        k = self.links
        z = k.z if turn == 0 else k.by_z([order[turn - 1] for order in self.ARRIVE])
        self.wait(k.chip(z, 1))
        if self.near_first and turn == 0:
            for other in k.column():
                self.to_column(other, 1)
        self.to_far(z, 1)

    def along(self, turn):
        k = self.links
        z = k.by_z([order[turn] for order in self.ARRIVE])
        self.wait(k.chip(z, 0))
        if not self.near_first:
            self.to_near(z)
        self.to_far(z, 0)

    def steps(self):
        steps = [self.own, lambda: self.near(0)]
        for turn in range(LINE - 1):
            steps.append(lambda turn=turn: self.along(turn))
            steps.append(lambda turn=turn: self.near(turn + 1))
        return steps

    def finish(self):
        self.copy(slice(0, 8 * self.size), self.links.far, self.FROM_FAR).wait_recv()

    def drain(self):
        self.copy(slice(0, 15 * self.size), self.links.far, self.FROM_FAR).wait_send()


class Reduce:
    LEAVE = ((3, 2, 1), (3, 2, 0), (0, 1, 3), (0, 1, 2))
    SLOTS = 15
    ARRIVALS = 10

    def __init__(self, links, grad, land, send, recv, near_first=False):
        self.links, self.grad, self.land = links, grad, land
        self.send, self.recv = send, recv
        self.size = grad.shape[0] // CHIPS
        self.near_first = near_first

    def rows(self, z, f, count=1, far=0):
        k = self.links
        g = k.g + far * (1 - 2 * k.g)
        at = 4 * z + 2 * g + f
        return pl.ds(pl.multiple_of(at * self.size, self.size), count * self.size)

    def slots(self, slot, count=1):
        start = slot * self.size
        return pl.ds(start if isinstance(slot, int) else pl.multiple_of(start, self.size), count * self.size)

    def copy(self, rows, slots, chip, arrival):
        return pltpu.make_async_remote_copy(
            src_ref=self.grad.at[rows],
            dst_ref=self.land.at[slots],
            send_sem=self.send,
            recv_sem=self.recv.at[arrival],
            device_id=(chip, self.links.p),
            device_id_type=MESH,
        )

    def wait(self, arrival, count):
        rows = slice(0, count * self.size)
        self.copy(rows, rows, self.links.far, arrival).wait_recv()

    def wait_far(self, z):
        self.wait(z, 2)

    def wait_near(self, z):
        self.wait(4 if self.near_first else 4 + z, 1)

    def wait_column(self, side):
        self.wait(8 + side, 3)

    def far_slot(self, z, f):
        return 2 * z + f

    def near_slot(self, z):
        return 8 if self.near_first else 8 + z

    def column_slot(self, step, side):
        return (9 + 3 * side if self.near_first else 12) + step - 1

    def column_slots(self, side):
        return [self.column_slot(step, side) for step in range(1, LINE)]

    def total(self, rows, slots):
        total = self.grad[rows].astype(F32)
        for slot in slots:
            total = total + self.land[self.slots(slot)].astype(F32)
        return total

    def add_on(self, rows, slots):
        self.grad[rows] = self.total(rows, slots).astype(self.grad.dtype)

    def far(self, z):
        self.copy(self.rows(z, 0, 2, 1), self.slots(self.far_slot(z, 0), 2), self.links.far, z).start()

    def near(self, z):
        k = self.links
        more = []
        self.wait_far(z)
        if self.near_first:
            self.wait_column(1)
            more = self.column_slots(1)
        rows = self.rows(z, 1 - k.f)
        self.add_on(rows, [self.far_slot(z, 1 - k.f)] + more)
        arrival = 4 if self.near_first else 4 + z
        self.copy(rows, self.slots(self.near_slot(z)), k.near, arrival).start()

    def along(self, turn, side):
        k = self.links
        z = k.by_z([order[turn] for order in self.LEAVE])
        f = k.f + side * (1 - 2 * k.f)
        rows, more = self.rows(z, f), []
        if not self.near_first:
            self.wait_near(z)
            more = [self.near_slot(z)]
        elif side == 1:
            self.wait_far(z)
        self.add_on(rows, [self.far_slot(z, f)] + more)
        slot = self.column_slot(lax.rem(k.z - z + LINE, LINE), side)
        self.copy(rows, self.slots(slot), k.chip(z, 0), 8 + side).start()

    def steps(self):
        steps = [lambda z=z: self.far(z) for z in range(LINE)]
        near = [lambda z=z: self.near(z) for z in range(LINE)]
        sides = (1, 0) if self.near_first else (0,)
        along = [
            lambda turn=turn, side=side: self.along(turn, side)
            for turn in range(LINE - 1)
            for side in sides
        ]
        if self.near_first:
            return steps + along + [lambda: self.near(self.links.z)]
        return steps + near + along

    def result(self):
        k = self.links
        self.wait_near(k.z)
        self.wait_column(0)
        slots = [self.far_slot(k.z, k.f), self.near_slot(k.z)]
        return self.total(self.rows(k.z, k.f), slots + self.column_slots(0))

    def drain(self):
        rows = slice(0, 15 * self.size)
        self.copy(rows, rows, self.links.far, 0).wait_send()


class Steps:
    def __init__(self, seqs, course, transfers):
        lines = [iter(steps) for steps in transfers]
        self.seqs, self.count = seqs, 0
        self.waiting = {place: [next(lines[n]) for n in order] for place, order in course.items()}
        assert all(next(line, None) is None for line in lines)

    def run(self):
        for step in self.waiting.pop(self.count, ()):
            step()
        self.count += 1

    def once(self, act):
        self.run()
        act()

    def loop(self, act, first=None, count=None):
        count = self.seqs if count is None else count
        self.run()
        if first is not None:
            first()
        later = []
        for s in range(1, count):
            later.append((s, self.waiting.pop(self.count, ())))
            self.count += 1

        def turn(s):
            for at, steps in later:
                if steps:

                    @pl.when(s == at)
                    def _():
                        for step in steps:
                            step()

            act(s)

        each(count, turn)


def laying(blocks, cols):
    size = cols // blocks
    pick = iota((128, cols), 0) == lax.rem(iota((128, cols), 1), size)
    return pick, lax.div(iota((blocks, cols), 1), size) == iota((blocks, cols), 0)


def core_order(chip, p):
    low = lax.rem(chip, 4)
    step = (low == 1).astype(jnp.int32) - (low == 2).astype(jnp.int32)
    return chip + p * step


def vector_rows(shape, dim, vector, p):
    device, row = iota(shape, dim), iota(shape, 1 - dim)
    return row == 16 * core_order(lax.div(device, 2), p) + 2 * vector + lax.rem(device, 2)


def unit_rows(shape, dim, which, p):
    return iota(shape, 1 - dim) == 16 * core_order(iota(shape, dim), p) + which


def unpack_small(r, p):
    rows = CHIPS * 16
    flat = r.small_all[...].astype(BF16)
    pick, place = laying(2 * CHIPS, r.vec.shape[1])
    for vector in range(8):
        chosen = nn(vector_rows((2 * CHIPS, rows), 0, vector, 0).astype(BF16), flat[:, :128])
        laid = nn(chosen.astype(BF16), pick.astype(BF16))
        r.vec[vector : vector + 1] = column_sum(jnp.where(place, laid, 0.0))
    pick, place = laying(CHIPS, r.upb.shape[1])
    chosen = nn(unit_rows((CHIPS, rows), 0, p, 0).astype(BF16), flat[:, 128:])
    laid = nn(chosen.astype(BF16), pick.astype(BF16))
    r.upb[...] = column_sum(jnp.where(place, laid, 0.0))


def pack_small(r, p):
    rows, width = CHIPS * 16, r.gvec.shape[1]
    for vector in range(2, 8):
        r.gvec[vector : vector + 1] = column_sum(r.gacc[8 * vector : 8 * vector + 8])
    row = iota((rows, 1), 0)
    device = 2 * core_order(lax.div(row, 16), p) + lax.rem(row, 2)
    chosen = lax.div(lax.rem(iota((rows, 8), 0), 16), 2) == iota((rows, 8), 1)
    spread = nn(chosen.astype(BF16), r.gvec[...].astype(BF16))
    place = device == lax.div(iota((1, width), 1), width // (2 * CHIPS))
    pick, _ = laying(2 * CHIPS, width)
    narrow = nt(jnp.where(place, spread, 0.0).astype(BF16), pick.astype(BF16))
    pick, place = laying(CHIPS, r.upg.shape[1])
    blocks = nt(jnp.where(place, r.upg[...], 0.0).astype(BF16), pick.astype(BF16))
    wide = nn(unit_rows((rows, CHIPS), 1, p, p).astype(BF16), blocks.astype(BF16))
    low = jnp.concatenate([narrow, wide], 1).astype(BF16)
    space = r.gq2.shape[0] // CHIPS
    for chip in range(CHIPS):
        r.gq2[space * chip + space - 16 : space * chip + space] = low[16 * chip : 16 * chip + 16]


def half_lanes(values, half, factor=None):
    mask = lax.div(iota((1, values.shape[1]), 1), HEAD_DIM) == half
    kept = jnp.where(mask, values, jnp.zeros_like(values))
    return kept if factor is None else kept * jnp.asarray(factor, values.dtype)


def normalize(values):
    centred = values - lane_mean(values)
    scale = lax.rsqrt(lane_mean(centred * centred) + EPSILON)
    return centred * scale, scale


def norm_back(grad, hat, scale):
    return scale * (grad - lane_mean(grad) - hat * lane_mean(grad * hat))


def gelu_both(value):
    square = value * value
    root = 0.7978845608028654
    inner = value * (root + root * 0.044715 * square)
    bent = 0.5 * jnp.tanh(inner) + 0.5
    slope = root + 3.0 * root * 0.044715 * square
    return value * bent, bent + 2.0 * value * slope * (bent - bent * bent)


UP_LANES = (slice(0, 768), slice(768, 1536),)
UP_NEAR_FIRST = (False, True)
DOWN_LANES = (slice(0, 512), slice(512, 768),)
DOWN_NEAR_FIRST = (False, True)
UP_SUM_LANES = (slice(0, 768), slice(768, 1536),)
UP_SUM_NEAR_FIRST = (True, False)
DOWN_SUM_LANES = (slice(0, 512), slice(512, 768),)
DOWN_SUM_NEAR_FIRST = (False, True)
UNITS = (
    ("unpack",),
    ("att", 0),
    ("att", 1),
    ("att", 2),
    ("wo",),
    ("out",),
    ("up", 0),
    ("up", 1),
    ("do", 0),
    ("dw", 0),
    ("do", 1),
    ("dw", 1),
    ("ln2",),
    ("ddw",),
    ("gd", 0),
    ("gd", 1),
    ("gd", 2),
    ("gd", 3),
    ("hb",),
    ("gu", 0),
    ("gu", 1),
    ("gu", 2),
    ("gu", 3),
    ("no",),
    ("nw",),
    ("ln1",),
    ("mb",),
    ("go",),
    ("ab", 0),
    ("gq", 0),
    ("ab", 1),
    ("gq", 1),
    ("ab", 2),
    ("ps",),
    ("gq", 2),
    ("to",),
    ("tw",),
    ("te",),
    ("end",),
)
COURSE = {
    0: (0, 1, 2, 3, 0, 0, 2, 4, 0, 0, 3, 1, 1, 6, 2, 1, 0, 0, 1, 3, 0, 1, 1, 5, 1, 2, 2, 3, 3,),
    1: (2, 4, 2,),
    2: (4,),
    3: (2, 3, 3,),
    4: (4, 4, 5,),
    6: (6, 3,),
    7: (6,),
    8: (4, 4, 7,),
    10: (6,),
    12: (6, 5,),
    15: (4,),
    16: (5, 5,),
    17: (5, 5, 6,),
    18: (5, 6, 7, 7,),
    23: (6,),
    24: (7, 7,),
    25: (7, 7, 7,),
    40: (9,),
    41: (9,),
    42: (9,),
    43: (9,),
    44: (8,),
    45: (8, 8, 8, 9,),
    48: (9,),
    49: (9, 9, 9, 8,),
    50: (8, 8,),
    52: (8, 10, 10, 10,),
    55: (8, 9,),
    59: (10, 11,),
    60: (11, 8,),
    63: (8, 11, 11,),
    65: (10,),
    67: (10, 11, 10, 10, 10, 10, 11,),
    68: (11,),
    69: (12, 11,),
    70: (12,),
    72: (12, 12, 12,),
    74: (11,),
    75: (12, 12, 12, 13, 11,),
    77: (11, 13, 13, 13,),
    79: (12, 12, 12, 13,),
    80: (14, 13,),
    81: (13, 13, 14, 14, 8, 14,),
    83: (9, 13, 13, 13, 14, 14,),
    85: (14, 14, 14, 14, 14, 12, 10,),
    86: (9, 11, 10, 13, 14,),
}


class Layer:
    def __init__(self, r, p):
        self.r, self.p = r, p
        self.slots = r.tokens.shape[2]
        self.width = r.tokens.shape[3]
        self.half = self.width // 2
        self.units = r.wup.shape[1]

    def rows(self, s):
        return block(s, 2 * self.slots)

    def side(self, s, side):
        return block(2 * s + side, self.slots)

    def own_lanes(self, pair):
        return pl.ds(pl.multiple_of(self.p * self.half + 128 * pair, 128), 128)

    def project(self, s, pair):
        r = self.r
        result = nn(r.x_all[self.rows(s)], r.wq[pair][...])
        lanes = self.own_lanes(pair)
        query = result[:, :128] + r.vec[0:1, lanes]
        value = result[:, 256:] + r.vec[1:2, lanes]
        r.qkv[pair, self.rows(s)] = jnp.concatenate([query, result[:, 128:256], value], 1).astype(BF16)

    def mask(self, s):
        r = self.r
        rows, space = r.fill.shape[1:]
        rest = jnp.zeros((1, space - rows), F32)
        ids = [r.segment_ids[s, half : half + 1].astype(F32) for half in range(2)]
        across = jnp.broadcast_to(jnp.concatenate(ids + [rest], 1), (space, space))
        r.fill[s] = jnp.where(across.T[:rows] == across[:rows], 0.0, NEG_FILL).astype(BF16)

    def heads(self, s, pair):
        held = self.r.qkv[pair, self.rows(s)]
        return held[:, :128], held[:, 128:256], held[:, 256:]

    def widened(self, values):
        rest = self.r.fill.shape[2] - values.shape[0]
        return jnp.concatenate([values, jnp.zeros((rest, values.shape[1]), values.dtype)], 0)

    def both_halves(self, values, factor=None, widen=False):
        parts = [half_lanes(values, half, factor) for half in range(2)]
        return jnp.concatenate([self.widened(part) if widen else part for part in parts], 0)

    def attend(self, s, pair):
        r = self.r
        rows, space = r.fill.shape[1:]
        queries, keys, values = self.heads(s, pair)
        values_t = values.T
        r.probs_grad[...] = nt(self.both_halves(keys, HEAD_DIM**-0.5), self.widened(queries))
        parts = []
        for half in range(2):
            top, total = NEG_FILL, 0.0
            for at in range(0, rows, 64):
                here = slice(rows * half + at, rows * half + at + 64)
                scores = r.probs_grad[here] + r.fill[s, at : at + 64].astype(F32)
                r.probs_grad[here] = scores
                top = jnp.maximum(top, jnp.max(scores.reshape(8, 8, space), 0))
            top = jnp.max(top, 0, keepdims=True)
            for at in range(0, rows, 64):
                here = slice(rows * half + at, rows * half + at + 64)
                raised = jnp.exp(r.probs_grad[here] - top)
                r.probs_grad[here] = raised
                total = total + jnp.sum(raised.reshape(8, 8, space), 0)
            share = 1.0 / column_sum(total)
            lanes = slice(space * half, space * half + space)
            for at in range(0, rows, 64):
                here = slice(rows * half + at, rows * half + at + 64)
                r.pt[3 * s + pair, at : at + 64, lanes] = (r.probs_grad[here] * share).astype(BF16)
            head = values_t[HEAD_DIM * half : HEAD_DIM * half + HEAD_DIM]
            parts.append(nn(head, r.pt[3 * s + pair, :, lanes]))
        mixed = jnp.concatenate(parts, 0).T[:rows]
        r.mixed[self.rows(s), self.own_lanes(pair)] = mixed.astype(BF16)

    def out_project(self, s):
        r, p = self.r, self.p
        mixed = r.mixed[self.side(s, p)]
        sides = [nn(mixed, r.wo[side]) for side in range(2)]
        r.product[: self.slots] = jnp.concatenate(sides, 1)
        for at, rows in self.pieces(s):
            resid = r.x_all[rows].astype(F32) + r.product[at] + r.vec[2:3]
            hat, scale = normalize(resid)
            r.xhat[s, at] = hat
            r.rstd[s, at] = jnp.broadcast_to(scale, (scale.shape[0], 128))
            r.n_all[rows] = (hat * r.vec[3:4] + r.vec[4:5]).astype(BF16)

    def feed_up(self, s, lanes):
        r = self.r
        r.product[...] = nn(r.n_all[self.rows(s)], r.wup[:, lanes])
        for at, rows in self.strips(s):
            hidden, slope = gelu_both(r.product[at] + r.upb[:, lanes])
            r.hidden[rows, lanes] = hidden.astype(BF16)
            r.slope[rows, lanes] = slope.astype(BF16)

    def two(self, ref, n, side):
        return jnp.concatenate([ref[self.side(2 * n + s, side)] for s in range(2)], 0)

    def by_two(self, rows):
        return rows.reshape(2, self.slots, rows.shape[1])

    def feed_down(self, n, side, lanes):
        return self.by_two(nn(self.two(self.r.hidden, n, side), self.r.wdown[:, lanes]))

    def pieces(self, s):
        for at in range(0, self.slots, 32):
            start = (2 * s + self.p) * self.slots + at
            yield slice(at, at + 32), pl.ds(pl.multiple_of(start, 32), 32)

    def strips(self, s):
        for at in range(0, 2 * self.slots, 32):
            start = 2 * s * self.slots + at
            yield slice(at, at + 32), pl.ds(pl.multiple_of(start, 32), 32)

    def add_rows(self, vector, values):
        folded = values.reshape(values.shape[0] // 8, 8, values.shape[1])
        self.r.gacc[8 * vector : 8 * vector + 8] += jnp.sum(folded, 0)

    def finish_norm(self, s):
        r = self.r
        for at, rows in self.pieces(s):
            normed = r.xhat[s, at] * r.vec[3:4] + r.vec[4:5]
            resid = normed + r.part_own[s, at] + r.part_in[s, at].astype(F32) + r.vec[5:6]
            hat, scale = normalize(resid)
            r.final[s, at] = (hat * r.vec[6:7] + r.vec[7:8]).astype(BF16)
            grad = r.out_grad[s, at].astype(F32)
            self.add_rows(6, grad * hat)
            self.add_rows(7, grad)
            back = norm_back(grad * r.vec[6:7], hat, scale)
            r.resid_grad[s, at] = back
            low = back.astype(BF16)
            r.dd_all[rows] = low
            self.add_rows(5, low.astype(F32))

    def put_blocks(self, ref, first, result, size):
        space = ref.shape[0] // CHIPS
        low = result.astype(BF16)
        for n in range(result.shape[0] // size):
            chip = first + n
            step = (0, 1, -1, 0)[chip % 4]
            at = chip * space
            rows = pl.ds(pl.multiple_of(at + self.p * step * space, 16), size) if step else slice(at, at + size)
            ref[rows] = low[n * size : n * size + size]

    def down_weight_grad(self, m):
        r = self.r
        at = slice(self.half * m, self.half * m + self.half)
        self.put_blocks(r.gd, 4 * m, tn(r.hidden[:, at], r.dd_all[...]), self.half // 4)

    def hidden_back(self, s):
        r = self.r
        grads = r.dd_all[self.rows(s)]
        for start in range(0, self.units, self.width):
            lanes = slice(start, start + self.width)
            r.product[...] = nt(grads, r.wdown[lanes])
            total = 0.0
            for at, rows in self.strips(s):
                low = (r.product[at] * r.slope[rows, lanes].astype(F32)).astype(BF16)
                r.slope[rows, lanes] = low
                total = total + jnp.sum(low.astype(F32).reshape(4, 8, self.width), 0)
            r.upg[:, lanes] += column_sum(total)

    def up_weight_grad(self, m, n):
        r = self.r
        at = slice(self.half * m, self.half * m + self.half)
        lanes = slice(self.width * n, self.width * n + self.width)
        self.put_blocks(r.gu.at[:, lanes], 8 * m, tn(r.n_all[:, at], r.slope[:, lanes]), self.half // 8)

    def normed_back(self, n, side):
        return self.by_two(nt(self.two(self.r.slope, n, side), self.r.wup[...]))

    def first_norm_back(self, s):
        r = self.r
        for at, rows in self.pieces(s):
            grad = r.part_own[s, at] + r.part_in[s, at].astype(F32) + r.resid_grad[s, at]
            hat = r.xhat[s, at]
            self.add_rows(3, grad * hat)
            self.add_rows(4, grad)
            back = norm_back(grad * r.vec[3:4], hat, r.rstd[s, at, 0:1])
            r.resid_grad[s, at] = back
            low = back.astype(BF16)
            r.n_all[rows] = low
            self.add_rows(2, low.astype(F32))

    def out_weight_grad(self):
        r = self.r
        own = block(self.p, self.half)
        right = r.n_all[:, own]
        for m in range(2):
            at = slice(self.half * m, self.half * m + self.half)
            self.put_blocks(r.go, 8 * m, tn(r.mixed[:, at], right), self.half // 8)

    def mixed_back(self, s):
        r = self.r
        grads = r.n_all[self.rows(s)]
        own = block(self.p, self.half)
        total = nt(grads[:, : self.half], r.wo[0, own]) + nt(grads[:, self.half :], r.wo[1, own])
        r.dm[self.rows(s)] = total.astype(BF16)

    def attend_back(self, s, pair):
        r = self.r
        scale = HEAD_DIM**-0.5
        unit = 3 * s + pair
        rows, space = r.fill.shape[1:]
        queries, keys, values = self.heads(s, pair)
        grads = r.dm[self.rows(s), 128 * pair : 128 * pair + 128]
        r.probs_grad[...] = nt(self.both_halves(values), self.widened(grads))
        for half in range(2):
            lanes = slice(space * half, space * half + space)
            total = 0.0
            for at in range(0, rows, 64):
                grad = r.probs_grad[rows * half + at : rows * half + at + 64]
                product = r.pt[unit, at : at + 64, lanes].astype(F32) * grad
                total = total + jnp.sum(product.reshape(8, 8, space), 0)
            delta = column_sum(total)
            for at in range(0, rows, 64):
                grad = r.probs_grad[rows * half + at : rows * half + at + 64]
                probs = r.pt[unit, at : at + 64, lanes].astype(F32)
                r.score_grad[at : at + 64, lanes] = (probs * (grad - delta)).astype(BF16)
        key_grad = nn(r.score_grad[...], self.both_halves(queries, scale, True))
        keys_t = keys.T * jnp.asarray(scale, BF16)
        query_parts = []
        for half in range(2):
            at = HEAD_DIM * half
            query_parts.append(
                nn(keys_t[at : at + HEAD_DIM], r.score_grad[:, space * half : space * half + space])
            )
        query_grad = jnp.concatenate(query_parts, 0).T[:rows]
        r.dqkv[pair][self.rows(s), :256] = jnp.concatenate([query_grad, key_grad], 1).astype(BF16)
        for other in ((0,), (1, 2), ())[pair]:
            grads = r.dm[self.rows(s), 128 * other : 128 * other + 128]
            value_grad = nn(r.pt[3 * s + other], self.both_halves(grads, None, True))
            r.dqkv[other][self.rows(s), 256:] = value_grad.astype(BF16)

    def project_weight_grad(self, pair):
        r = self.r
        target, right = (r.gq0, r.gq1, r.gq2)[pair], r.dqkv[pair][...]
        if pair == 1:
            right = jnp.concatenate([right, r.dqkv[2][:, 256:]], 1)
        if pair == 2:
            right = right[:, :256]
        for m in range(2):
            at = slice(self.half * m, self.half * m + self.half)
            self.put_blocks(target, 8 * m, tn(r.x_all[:, at], right), self.half // 8)

    def project_bias_grad(self, pair):
        r = self.r
        right = r.dqkv[pair]
        lanes = self.own_lanes(pair)
        r.gvec[0:1, lanes] = column_sum(right[:, :128].astype(F32))
        r.gvec[1:2, lanes] = column_sum(right[:, 256:].astype(F32))

    def token_back(self, n, side):
        r = self.r
        total = 0.0
        for pair in range(3):
            total = total + nt(self.two(r.dqkv[pair], n, side), r.wq[pair][...])
        return self.by_two(total)


def ordered(size):
    column = iota((1, 8 * size), 1)
    within = lax.rem(column, 4 * size)
    source = 2 * size * lax.div(within, size) + size * lax.div(column, 4 * size) + lax.rem(within, size)
    return iota((8 * size, 8 * size), 0) == source


def place_small(r, p):
    r.small_in[...] = jnp.zeros_like(r.small_in)
    rows = [(row, 0, vector) for row, vector in enumerate(r.vectors)] + [(0, 128, r.up_bias)]
    for row, lane, vector in rows:
        count = vector.shape[0]
        values = vector[...].reshape(1, count).astype(F32)
        for core in range(2):

            @pl.when(p == core)
            def _():
                at = 2 * row + core
                r.small_in[at : at + 1, lane : lane + count] = values


def pack_square(r, half, piece):
    at = half * piece
    for core in range(2):
        if piece == 3:
            r.stack[core, :, at : at + half] = r.out_weight[:, half * core : half * core + half].astype(F32)
            continue
        for part, weight in enumerate((r.query_weight, r.key_weight, r.value_weight)):
            lane = half * core + 128 * piece
            r.stack[core, :, at + 128 * part : at + 128 * part + 128] = weight[:, lane : lane + 128].astype(F32)


def pack_up(r, half, size):
    rows = r.up_weight.shape[0]
    groups = [r.up_weight[:, 8 * size * group : 8 * size * group + 8 * size] for group in range(CHIPS // 4)]
    stacked = jnp.concatenate([group.astype(F32) for group in groups], 0).astype(BF16)
    ordered_units = nn(stacked, ordered(size).astype(BF16))
    for group in range(CHIPS // 4):
        to = 4 * half + 4 * size * group
        for core in range(2):
            r.stack[core, :, to : to + 4 * size] = ordered_units[
                rows * group : rows * group + rows, 4 * size * core : 4 * size * core + 4 * size
            ]


def layer_kernel(r):
    k = Links()
    p = k.p
    seqs = r.tokens.shape[0]
    layer = Layer(r, p)
    half = layer.half
    width = layer.width
    per = r.stack.shape[1]
    size = r.down_weight.shape[0]
    pack = r.stack.shape[2]
    def to_other(src, dst, group, arrival):
        return pltpu.make_async_remote_copy(
            src_ref=src,
            dst_ref=dst,
            send_sem=r.pair_send.at[group],
            recv_sem=r.pair_recv.at[arrival],
            device_id=k.other(),
            device_id_type=MESH,
        )

    def local(src, dst, which):
        return pltpu.make_async_copy(src, dst, r.local_done.at[which])

    def trade_own(ref, group, base):
        return lambda s: to_other(ref.at[layer.side(s, p)], ref.at[layer.side(s, p)], group, base + s)

    def trade_slot(src, dst, group, base):
        return lambda s: to_other(src.at[s], dst.at[s], group, base + s)

    def sent(group):
        to_other(r.part_out, r.part_in, group, 0).wait_send()

    small_swap = to_other(r.small_in, r.small_theirs, 0, 0)
    share = to_other(r.wo.at[p], r.wo.at[p], 1, 1)
    sums_swap = to_other(r.sum_small, r.sum_theirs, 2, 2)
    inputs = lambda s: to_other(r.tokens.at[s, 0], r.x_all.at[layer.side(s, p)], 3, 3)
    normed = trade_own(r.n_all, 4, 4)
    down_part = trade_slot(r.part_out, r.part_in, 5, 4 + seqs)
    down_grad = trade_own(r.dd_all, 6, 4 + 2 * seqs)
    normed_part = trade_slot(r.part_out, r.part_in, 7, 4 + 3 * seqs)
    branch = trade_own(r.n_all, 8, 4 + 4 * seqs)
    token_part = trade_slot(r.part_out, r.part_in, 9, 4 + 5 * seqs)

    def mixed(s, pair):
        part = r.mixed.at[layer.rows(s), layer.own_lanes(pair)]
        return to_other(part, part, 10, 4 + 6 * seqs + s)

    def mixed_in(s):
        part = r.mixed.at[layer.rows(s), block(p, half)]
        return to_other(part, part, 10, 4 + 6 * seqs + s)

    def pack_swap(lanes):
        return to_other(r.sum_pack.at[block(1 - p, per), lanes], r.out_pack.at[p, :, lanes], 11, 4 + 7 * seqs)

    pieces = [slice(0, half), slice(half, 2 * half), slice(2 * half, 4 * half)]
    pieces += [slice(4 * half + lanes.start, 4 * half + lanes.stop) for lanes in UP_LANES]

    def piece_swap(n):
        lanes = pieces[n]
        return to_other(
            r.stack.at[1 - p, :, lanes], r.sum_pack.at[block(p, per), lanes], 12, 5 + 7 * seqs + n
        )

    def place_piece(n, target):
        lanes = pieces[n]

        def act():
            piece_swap(n).wait_recv()
            r.sum_pack[block(p, per), lanes] = r.stack[p, :, lanes]
            target[block(k.b, 2 * per)] = r.sum_pack[:, lanes].astype(BF16)

        return act

    def gather(n, ref, near_first=False):
        return Gather(k, ref, r.gather_send.at[n], r.gather_recv.at[n], near_first)

    def reduce(n, grad, land, near_first=False):
        return Reduce(k, grad, land, r.reduce_send.at[n], r.reduce_recv.at[n], near_first)

    small = gather(0, r.small_all)
    heads = [gather(1 + pair, ref) for pair, ref in enumerate((r.wq0, r.wq1, r.wq2o))]
    ups = [gather(4 + n, r.wup.at[:, lanes], first) for n, (lanes, first) in enumerate(zip(UP_LANES, UP_NEAR_FIRST))]
    downs = [
        gather(6 + n, r.wdown.at[:, lanes], first)
        for n, (lanes, first) in enumerate(zip(DOWN_LANES, DOWN_NEAR_FIRST))
    ]
    gathers = [small] + heads + ups + downs
    down_sums = [
        reduce(n, r.gd.at[:, lanes], land, first)
        for n, (lanes, land, first) in enumerate(zip(DOWN_SUM_LANES, r.land_d, DOWN_SUM_NEAR_FIRST))
    ]
    up_sums = [
        reduce(2 + n, r.gu.at[:, lanes], land, first)
        for n, (lanes, land, first) in enumerate(zip(UP_SUM_LANES, r.land_u, UP_SUM_NEAR_FIRST))
    ]
    out_sum = reduce(4, r.goq, r.land_oq)
    head_sums = [reduce(5, r.gq1, r.land_q1), reduce(6, r.gq2, r.land_q2)]
    reduces = down_sums + up_sums + [out_sum] + head_sums

    def store(one, lanes):
        def act():
            r.sum_pack[:, lanes] = one.result()
            pack_swap(lanes).start()
            r.out_pack[p, :, lanes] = r.sum_pack[block(p, per), lanes]

        return act

    def store_down(one, lanes):
        def act():
            total = one.result()
            for group in range(size // per):
                to = slice(width * group + lanes.start, width * group + lanes.stop)
                r.out_pack[2, :, to] = total[per * group : per * group + per]

        return act

    def store_last():
        total = head_sums[1].result()
        r.sum_pack[:, packs[-1]] = total[: 2 * per]
        pack_swap(packs[-1]).start()
        r.sum_small[...] = total[2 * per :]
        sums_swap.start()
        r.out_pack[p, :, packs[-1]] = r.sum_pack[block(p, per), packs[-1]]

    packs = [slice(4 * half + lanes.start, 4 * half + lanes.stop) for lanes in UP_SUM_LANES]
    packs += [slice(0, 2 * half), slice(2 * half, 3 * half + 128), slice(3 * half + 128, 4 * half)]
    stores = [store_down(one, lanes) for one, lanes in zip(down_sums, DOWN_SUM_LANES)]
    stores += [store(one, lanes) for one, lanes in zip(up_sums + [out_sum] + head_sums[:1], packs)]
    stores.append(store_last)

    def place_small_rows():
        small_swap.wait_recv()
        r.small_all[block(k.b, 16)] = r.small_in[...] + r.small_theirs[...]

    def finish_out():
        heads[2].finish()
        r.wo[p] = r.wq2o[:, half:]
        share.start()

    starts = [place_small_rows]
    starts += [place_piece(n, target) for n, target in enumerate((r.wq0, r.wq1, r.wq2o))]
    starts += [place_piece(3 + n, r.wup.at[:, lanes]) for n, lanes in enumerate(UP_LANES)]
    spreads = [one.steps() for one in gathers]
    for steps_of, start in zip(spreads, starts):
        steps_of[0] = lambda start=start, own=steps_of[0]: (start(), own())
    sums = [one.steps() + [last] for one, last in zip(reduces, stores)]
    steps = Steps(seqs, COURSE, spreads + sums)

    k.greet()
    each(seqs, lambda s: local(r.tokens.at[s, 0], r.x_all.at[layer.side(s, p)], 0).start())
    local(r.cotangent.at[:, 0], r.out_grad, 1).start()
    pack_square(r, half, 0)
    place_small(r, p)
    k.meet()
    piece_swap(0).start()
    small_swap.start()
    pack_square(r, half, 1)
    piece_swap(1).start()
    pack_square(r, half, 2)
    pack_square(r, half, 3)
    piece_swap(2).start()
    pack_up(r, half, size)
    for n in range(3, len(pieces)):
        piece_swap(n).start()
    each(seqs, lambda s: inputs(s).start())
    r.wdown[block(k.b, size)] = r.down_weight[...]
    r.gvec[...] = jnp.zeros_like(r.gvec)
    r.gacc[...] = jnp.zeros_like(r.gacc)
    r.upg[...] = jnp.zeros_like(r.upg)

    def wait_once(*copies):
        fresh = [copy for copy in copies if copy not in waited]
        waited.extend(fresh)
        return lambda s: [copy(s).wait_recv() for copy in fresh]

    waited = []

    def unpack():
        def act():
            each(seqs, layer.mask)
            small.finish()
            unpack_small(r, p)
            to_other(r.part_out, r.part_in, 3, 3).wait_recv()
            local(r.part_out, r.part_in, 0).wait()

        steps.once(act)

    def attention(pair):
        def act(s):
            layer.project(s, pair)
            layer.attend(s, pair)
            mixed(s, pair).start()

        steps.loop(act, heads[pair].finish if pair < 2 else finish_out)

    def wait_share():
        steps.once(lambda: share.wait_recv())

    def first_half():
        def act(s):
            mixed_in(s).wait_recv()
            layer.out_project(s)
            normed(s).start()

        steps.loop(act)

    def feed(n):
        wait = wait_once(normed)

        def act(s):
            wait(s)
            layer.feed_up(s, UP_LANES[n])

        steps.loop(act, ups[n].finish)

    def feed_other(n):
        lanes = DOWN_LANES[n]

        def act(two):
            at = pl.ds(2 * two, 2)
            r.part_out[at, :, lanes] = layer.feed_down(two, 1 - p, lanes).astype(BF16)
            if n == len(DOWN_LANES) - 1:
                for s in range(2):
                    down_part(2 * two + s).start()

        steps.loop(act, downs[n].finish, seqs // 2)

    def feed_own(n):
        lanes = DOWN_LANES[n]

        def act(two):
            r.part_own[pl.ds(2 * two, 2), :, lanes] = layer.feed_down(two, p, lanes)

        steps.loop(act, count=seqs // 2)

    def second_norm():
        def act(s):
            down_part(s).wait_recv()
            layer.finish_norm(s)
            down_grad(s).start()
            local(r.final.at[s], r.layer_output.at[s, 0], 2).start()

        steps.loop(act, local(r.cotangent.at[:, 0], r.out_grad, 1).wait)

    def wait_grads():
        wait = wait_once(down_grad)
        steps.once(lambda: each(seqs, lambda s: wait(s) and None))

    def down_grads(m):
        steps.once(lambda: layer.down_weight_grad(m))

    def hidden_back():
        wait = wait_once(down_grad)

        def act(s):
            wait(s)
            layer.hidden_back(s)

        steps.loop(act)

    def up_grads(n):
        steps.once(lambda: layer.up_weight_grad(n // 2, n % 2))

    def back_other():
        def first():
            for group in (4, 5, 6):
                sent(group)

        def act(two):
            r.part_out[pl.ds(2 * two, 2)] = layer.normed_back(two, 1 - p).astype(BF16)
            for s in range(2):
                normed_part(2 * two + s).start()

        steps.loop(act, first, seqs // 2)

    def back_own():
        def act(two):
            r.part_own[pl.ds(2 * two, 2)] = layer.normed_back(two, p)

        steps.loop(act, count=seqs // 2)

    def first_norm():
        def act(s):
            normed_part(s).wait_recv()
            layer.first_norm_back(s)
            branch(s).start()

        steps.loop(act)

    def mixed_grad():
        def act(s):
            branch(s).wait_recv()
            layer.mixed_back(s)

        steps.loop(act)

    def out_grad():
        steps.once(layer.out_weight_grad)
        for one in downs:
            one.drain()

    def attention_back(pair):
        steps.loop(lambda s: layer.attend_back(s, pair))

    def head_grads(pair):
        steps.once(lambda: layer.project_weight_grad(pair))

    def pack_vectors():
        def act():
            for pair in range(3):
                layer.project_bias_grad(pair)
            pack_small(r, p)

        steps.once(act)

    def token_other():
        def act(two):
            r.part_out[pl.ds(2 * two, 2)] = layer.token_back(two, 1 - p).astype(BF16)
            for s in range(2):
                token_part(2 * two + s).start()

        steps.loop(act, lambda: sent(7), seqs // 2)

    def token_own():
        def act(two):
            r.part_own[pl.ds(2 * two, 2)] = layer.token_back(two, p)

        steps.loop(act, count=seqs // 2)

    def token_end():
        def first():
            for one in [small] + heads + ups:
                one.drain()
            for copy in (small_swap, share):
                copy.wait_send()
            to_other(r.stack.at[1 - p], r.stack.at[p], 12, 0).wait_send()
            for group in (3, 8, 10):
                sent(group)

        def act(s):
            token_part(s).wait_recv()
            total = r.part_own[s] + r.part_in[s].astype(F32) + r.resid_grad[s]
            r.token_grad[s] = total.astype(BF16)
            local(r.token_grad.at[s], r.tokens_gradient.at[s, 0], 3).start()

        steps.loop(act, first)

    def collect():
        def act():
            sums_swap.wait_recv()
            r.out_pack[2, 0:16, pack : pack + 256] = r.sum_small[...] + r.sum_theirs[...]
            whole = pack_swap(slice(0, pack))
            whole.wait()
            for one in reduces:
                one.drain()
            sums_swap.wait_send()
            sent(9)
            for outgoing in (2, 3):
                local(r.part_out, r.part_in, outgoing).wait()

        steps.once(act)

    units = dict(
        unpack=unpack,
        att=attention,
        wo=wait_share,
        out=first_half,
        up=feed,
        do=feed_other,
        dw=feed_own,
        ln2=second_norm,
        ddw=wait_grads,
        gd=down_grads,
        hb=hidden_back,
        gu=up_grads,
        no=back_other,
        nw=back_own,
        ln1=first_norm,
        mb=mixed_grad,
        go=out_grad,
        ab=attention_back,
        gq=head_grads,
        ps=pack_vectors,
        to=token_other,
        tw=token_own,
        te=token_end,
        end=collect,
    )
    for name, *which in UNITS:
        units[name](*which)
    assert not steps.waiting


def finish_kernel(r):
    p = lax.axis_index(PAIR)
    half = r.query_out.shape[1] // 2
    size = r.down_out.shape[0]
    for core in range(2):
        for pair in range(3):
            for part, target in enumerate((r.query_out, r.key_out, r.value_out)):
                place = (0, 1, 2, 6, 7, 8, 10, 11, 9)[3 * pair + part]
                at, lane = 128 * place, half * core + 128 * pair
                target[:, lane : lane + 128] = r.pack[core, :, at : at + 128]
        r.out_out[:, half * core : half * core + half] = r.pack[core, :, half : 2 * half]
    rows, width = r.query_out.shape
    groups = []
    for group in range(CHIPS // 4):
        at = 4 * half + 4 * size * group
        groups.append(jnp.concatenate([r.pack[core, :, at : at + 4 * size] for core in range(2)], 1))
    rest = jnp.concatenate(groups, 0)
    parts = []
    for _ in range(3):
        parts.append(rest.astype(BF16).astype(F32))
        rest = rest - parts[-1]
    laid = nt(jnp.concatenate(parts, 0).astype(BF16), ordered(size).astype(BF16))
    count = laid.shape[0] // 3
    laid = laid[:count] + laid[count : 2 * count] + laid[2 * count :]
    for group in range(CHIPS // 4):
        to = 8 * size * group
        r.up_out[:, to : to + 8 * size] = laid[rows * group : rows * group + rows]
    for group in range(size // rows):
        r.down_out[rows * group : rows * group + rows] = r.pack[2, :, width * group : width * group + width]
    small = r.pack[2, 0:16, 4 * half + r.up_out.shape[1] // 2 :]
    for vector, target in enumerate(r.vectors):
        row = jnp.where(p == 0, small[2 * vector : 2 * vector + 1], small[2 * vector + 1 : 2 * vector + 2])
        target[...] = row[:, : target.shape[1]]
    row = jnp.where(p == 0, small[0:1], small[1:2])
    r.up_vector[...] = row[:, 128 : 128 + size]


def call(kernel, ins, outs, scratch, semaphores, elsewhere=(), **params):
    names = list(ins) + list(outs) + list(scratch) + list(semaphores)

    def body(*refs):
        kernel(Refs(zip(names, refs)))

    def spec(name):
        return pl.BlockSpec(memory_space=pl.ANY if name in elsewhere else pltpu.VMEM)

    results = pl.pallas_call(
        body,
        out_shape=[jax.ShapeDtypeStruct(*held_as) for held_as in outs.values()],
        in_specs=[spec(name) for name in ins],
        out_specs=[spec(name) for name in outs],
        scratch_shapes=[pltpu.VMEM(*held_as) for held_as in scratch.values()] + list(semaphores.values()),
        compiler_params=pltpu.CompilerParams(**params),
        name=kernel.__name__,
    )(*ins.values())
    return Refs(zip(outs, results))


def fast(
    tokens,
    segment_ids,
    query_weight,
    query_bias,
    key_weight,
    value_weight,
    value_bias,
    out_weight,
    out_bias,
    first_gain,
    first_shift,
    up_weight,
    up_bias,
    down_weight,
    down_bias,
    second_gain,
    second_shift,
    cotangent,
):
    seqs, _, slots, width = tokens.shape
    units = up_weight.shape[1] // 2
    per = up_weight.shape[0]
    half = width // 2
    size = units // CHIPS
    rows = 2 * slots
    space = -(-rows // 128) * 128
    ins = dict(
        tokens=tokens,
        cotangent=cotangent,
        segment_ids=segment_ids,
        query_weight=query_weight,
        key_weight=key_weight,
        value_weight=value_weight,
        out_weight=out_weight,
        up_weight=up_weight,
        down_weight=down_weight,
        query_bias=query_bias,
        value_bias=value_bias,
        out_bias=out_bias,
        first_gain=first_gain,
        first_shift=first_shift,
        down_bias=down_bias,
        second_gain=second_gain,
        second_shift=second_shift,
        up_bias=up_bias,
    )
    pack = 4 * half + units
    outs = dict(
        layer_output=(tokens.shape, BF16),
        tokens_gradient=(tokens.shape, BF16),
        out_pack=((3, per, pack + 256), F32),
    )
    all_rows = seqs * rows
    held = dict(
        stack=((2, per, pack), F32),
        sum_pack=((2 * per, pack), F32),
        small_in=((16, 256), F32),
        small_theirs=((16, 256), F32),
        sum_theirs=((16, 256), F32),
        sum_small=((16, 256), F32),
        small_all=((CHIPS * 16, 256), F32),
        vec=((8, width), F32),
        upb=((1, units), F32),
        gvec=((8, width), F32),
        gacc=((64, width), F32),
        upg=((1, units), F32),
        fill=((seqs, rows, space), BF16),
        probs_grad=((2 * rows, space), F32),
        product=((rows, width), F32),
        score_grad=((rows, 2 * space), BF16),
        x_all=((all_rows, width), BF16),
        wq0=((width, half), BF16),
        wq1=((width, half), BF16),
        wq2o=((width, width), BF16),
        wo=((2, width, half), BF16),
        wup=((width, units), BF16),
        wdown=((units, width), BF16),
        qkv=((3, all_rows, half), BF16),
        pt=((3 * seqs, rows, 2 * space), BF16),
        mixed=((all_rows, width), BF16),
        xhat=((seqs, slots, width), F32),
        rstd=((seqs, slots, 128), F32),
        n_all=((all_rows, width), BF16),
        hidden=((all_rows, units), BF16),
        slope=((all_rows, units), BF16),
        part_own=((seqs, slots, width), F32),
        part_out=((seqs, slots, width), BF16),
        part_in=((seqs, slots, width), BF16),
        out_grad=((seqs, slots, width), BF16),
        final=((seqs, slots, width), BF16),
        token_grad=((seqs, slots, width), BF16),
        resid_grad=((seqs, slots, width), F32),
        dd_all=((all_rows, width), BF16),
        gd=((units, width), BF16),
        land_d0=((Reduce.SLOTS * size, DOWN_SUM_LANES[0].stop), BF16),
        land_d1=((Reduce.SLOTS * size, width - DOWN_SUM_LANES[0].stop), BF16),
        land_u0=((Reduce.SLOTS * 2 * per, UP_SUM_LANES[0].stop), BF16),
        land_u1=((Reduce.SLOTS * 2 * per, units - UP_SUM_LANES[0].stop), BF16),
        land_oq=((Reduce.SLOTS * 2 * per, width), BF16),
        land_q1=((Reduce.SLOTS * 2 * per, half + 128), BF16),
        land_q2=((Reduce.SLOTS * (2 * per + 16), half - 128), BF16),
    )
    dma = pltpu.SemaphoreType.DMA
    semaphores = dict(
        pair_send=dma((13,)),
        pair_recv=dma((9 + 7 * seqs + len(UP_LANES),)),
        gather_send=dma((8,)),
        gather_recv=dma((8, Gather.ARRIVALS)),
        local_done=dma((4,)),
        reduce_send=dma((7,)),
        reduce_recv=dma((7, Reduce.ARRIVALS)),
    )

    def layer(r):
        r.gu = r.hidden.at[0:width]
        last = width + 16 * CHIPS
        r.goq = r.slope.at[0:width, 0 : 2 * half]
        split = 3 * half + 128
        r.gq0 = r.slope.at[0:width, 0:half]
        r.gq1 = r.slope.at[0:width, 2 * half : split]
        r.gq2 = r.slope.at[0:last, split : 4 * half]
        r.go = r.slope.at[0:width, half : 2 * half]
        r.wq = [r.wq0, r.wq1, r.wq2o.at[:, 0:half]]
        r.dqkv = [r.wdown.at[0:all_rows, 0:half], r.wdown.at[0:all_rows, half:width], r.dd_all.at[:, 0:half]]
        r.dm = r.dd_all.at[:, half:width]
        r.land_d = [r.land_d0, r.land_d1]
        r.land_u = [r.land_u0, r.land_u1]
        r.vectors = [
            r.query_bias,
            r.value_bias,
            r.out_bias,
            r.first_gain,
            r.first_shift,
            r.down_bias,
            r.second_gain,
            r.second_shift,
        ]
        layer_kernel(r)

    elsewhere = dict(tokens=1, cotangent=1, layer_output=1, tokens_gradient=1)
    done = call(
        layer, ins, outs, held, semaphores, elsewhere, vmem_limit_bytes=VMEM_BYTES, collective_id=0, has_side_effects=True
    )

    square = ((per, width), F32)
    line = ((1, per), F32)
    finals = dict(
        query_out=square,
        query_vector=line,
        key_out=square,
        value_out=square,
        value_vector=line,
        out_out=square,
        out_vector=line,
        gain_vector=line,
        shift_vector=line,
        up_out=(up_weight.shape, F32),
        up_vector=((1, size), F32),
        down_out=(down_weight.shape, F32),
        down_vector=line,
        last_gain_vector=line,
        last_shift_vector=line,
    )

    def finish(r):
        r.vectors = [
            r.query_vector,
            r.value_vector,
            r.out_vector,
            r.gain_vector,
            r.shift_vector,
            r.down_vector,
            r.last_gain_vector,
            r.last_shift_vector,
        ]
        finish_kernel(r)

    final = call(finish, dict(pack=done.out_pack), finals, {}, {}, vmem_limit_bytes=16 * 1024 * 1024)
    flat = [value[0] if value.shape[0] == 1 else value for value in final.values()]
    return (done.layer_output, done.tokens_gradient, *flat)


def solution(mesh):
    in_specs = (
        P(BATCH, PAIR, None, None),
        P(BATCH, None, None),
        P(AXES, None),
        P(AXES),
        P(AXES, None),
        P(AXES, None),
        P(AXES),
        P(AXES, None),
        P(AXES),
        P(AXES),
        P(AXES),
        P(AXES, None),
        P(AXES),
        P(AXES, None),
        P(AXES),
        P(AXES),
        P(AXES),
        P(BATCH, PAIR, None, None),
    )
    out_specs = (
        P(BATCH, PAIR, None, None),
        P(BATCH, PAIR, None, None),
        P(AXES, None),
        P(AXES),
        P(AXES, None),
        P(AXES, None),
        P(AXES),
        P(AXES, None),
        P(AXES),
        P(AXES),
        P(AXES),
        P(AXES, None),
        P(AXES),
        P(AXES, None),
        P(AXES),
        P(AXES),
        P(AXES),
    )
    small_slice = dict(mesh.shape) == {BATCH: CHIPS, PAIR: 2}
    part = fast if small_slice else local
    return jax.shard_map(part, mesh=mesh, in_specs=in_specs, out_specs=out_specs, check_vma=False)
```

```python
import jax
import jax.numpy as jnp
from jax import lax
from jax.experimental import pallas as pl
from jax.experimental.pallas import tpu as pltpu
from jax.sharding import PartitionSpec as P

BATCH, PAIR = AXES = ("batch", "pair")
HEAD_DIM = 64


EPSILON = 1e-05
NEG_FILL = -1e30


def swapped(value, axis, stride):
    return lax.ppermute(value, axis, [(i, i ^ 1 << stride) for i in range(lax.axis_size(axis))])


def layer_norm(values, gain, shift):
    average = jnp.mean(values, -1, keepdims=True)
    centred = values - average
    variance = jnp.mean(centred * centred, -1, keepdims=True)
    return centred * lax.rsqrt(variance + EPSILON) * gain + shift


def matmul(left, right):
    return jnp.dot(left, right, preferred_element_type=jnp.float32)


def product_back(left, right):
    return lax.dot_general(
        left, right, (((left.ndim - 1,), (1,)), ((), ())), preferred_element_type=jnp.float32
    )


def outer_sum(left, right):
    flat_left = left.reshape(-1, left.shape[-1])
    flat_right = right.reshape(-1, right.shape[-1])
    return lax.dot_general(
        flat_left, flat_right, (((0,), (0,)), ((), ())), preferred_element_type=jnp.float32
    )


def row_total(values):
    return jnp.sum(values.astype(jnp.float32), (0, 1))


def scores_of(query_heads, key_rows, allowed, factor):
    raw = jnp.einsum("sqhd,skhd->shqk", query_heads, key_rows, preferred_element_type=jnp.float32)
    return jnp.where(allowed, raw * factor, NEG_FILL)


def local(
    tokens,
    segment_ids,
    query_weight,
    query_bias,
    key_weight,
    value_weight,
    value_bias,
    out_weight,
    out_bias,
    first_gain,
    first_shift,
    up_weight,
    up_bias,
    down_weight,
    down_bias,
    second_gain,
    second_shift,
    cotangent,
):
    seqs = tokens.shape[0]
    slots = tokens.shape[2]
    width = tokens.shape[3]
    heads = width // HEAD_DIM
    factor = HEAD_DIM ** (-0.5)
    token_rows = tokens.reshape(seqs, slots, width)
    attention_shards = (
        query_weight,
        query_bias,
        key_weight,
        value_weight,
        value_bias,
        out_weight,
        out_bias,
        first_gain,
        first_shift,
    )
    feedforward_shards = (up_weight, up_bias, down_weight, down_bias, second_gain, second_shift)
    attention_full = (
        lax.all_gather(attention_shards[0], AXES, axis=0, tiled=True),
        lax.all_gather(attention_shards[1], AXES, axis=0, tiled=True),
        lax.all_gather(attention_shards[2], AXES, axis=0, tiled=True),
        lax.all_gather(attention_shards[3], AXES, axis=0, tiled=True),
        lax.all_gather(attention_shards[4], AXES, axis=0, tiled=True),
        lax.all_gather(attention_shards[5], AXES, axis=0, tiled=True),
        lax.all_gather(attention_shards[6], AXES, axis=0, tiled=True),
        lax.all_gather(attention_shards[7], AXES, axis=0, tiled=True),
        lax.all_gather(attention_shards[8], AXES, axis=0, tiled=True),
    )
    feedforward_full = (
        lax.all_gather(feedforward_shards[0], AXES, axis=0, tiled=True),
        lax.all_gather(feedforward_shards[1], AXES, axis=0, tiled=True),
        lax.all_gather(feedforward_shards[2], AXES, axis=0, tiled=True),
        lax.all_gather(feedforward_shards[3], AXES, axis=0, tiled=True),
        lax.all_gather(feedforward_shards[4], AXES, axis=0, tiled=True),
        lax.all_gather(feedforward_shards[5], AXES, axis=0, tiled=True),
    )
    (
        query_mat,
        query_vec,
        key_mat,
        value_mat,
        value_vec,
        out_mat,
        out_vec,
        gain_first,
        shift_first,
    ) = attention_full
    up_mat, up_vec, down_mat, down_vec, gain_second, shift_second = feedforward_full
    pair_index = lax.axis_index(PAIR)
    own_ids = lax.dynamic_index_in_dim(segment_ids, pair_index, 1, keepdims=False)
    other_ids = lax.dynamic_index_in_dim(segment_ids, 1 - pair_index, 1, keepdims=False)
    key_ids = jnp.concatenate([own_ids, other_ids], 1)
    allowed = (own_ids[:, :, None] == key_ids[:, None, :])[:, None]
    queries = (matmul(token_rows, query_mat) + query_vec).astype(jnp.bfloat16)
    keys_own = matmul(token_rows, key_mat).astype(jnp.bfloat16)
    values_own = (matmul(token_rows, value_mat) + value_vec).astype(jnp.bfloat16)
    keys_other, values_other = swapped((keys_own, values_own), PAIR, 0)
    head_rows = (seqs, 2 * slots, heads, HEAD_DIM)
    key_rows = jnp.concatenate([keys_own, keys_other], 1).reshape(head_rows)
    value_rows = jnp.concatenate([values_own, values_other], 1).reshape(head_rows)
    query_heads = queries.reshape(seqs, slots, heads, HEAD_DIM)
    scores = scores_of(query_heads, key_rows, allowed, factor)
    row_max = jnp.max(scores, -1, keepdims=True)
    log_total = row_max + jnp.log(jnp.sum(jnp.exp(scores - row_max), -1, keepdims=True))
    probs_low = jnp.exp(scores - log_total).astype(jnp.bfloat16)
    mixed = jnp.einsum("shqk,skhd->sqhd", probs_low, value_rows, preferred_element_type=jnp.float32)
    mixed = mixed.reshape(seqs, slots, width).astype(jnp.bfloat16)
    first_resid = token_rows.astype(jnp.float32) + matmul(mixed, out_mat) + out_vec
    normed, first_pull = jax.vjp(
        layer_norm, first_resid, gain_first.astype(jnp.float32), shift_first.astype(jnp.float32)
    )
    normed_low = normed.astype(jnp.bfloat16)
    pre_hidden = matmul(normed_low, up_mat) + up_vec
    hidden, gelu_pull = jax.vjp(jax.nn.gelu, pre_hidden)
    hidden_low = hidden.astype(jnp.bfloat16)
    second_resid = normed + matmul(hidden_low, down_mat) + down_vec
    final, second_pull = jax.vjp(
        layer_norm, second_resid, gain_second.astype(jnp.float32), shift_second.astype(jnp.float32)
    )
    layer_output = final.astype(jnp.bfloat16).reshape(tokens.shape)
    out_grad = cotangent.reshape(seqs, slots, width).astype(jnp.float32)
    second_grad, gain_second_grad, shift_second_grad = second_pull(out_grad)
    down_in = second_grad.astype(jnp.bfloat16)
    down_weight_grad = outer_sum(hidden_low, down_in)
    down_bias_grad = row_total(down_in)
    hidden_grad = product_back(down_in, down_mat)
    (pre_grad,) = gelu_pull(hidden_grad)
    pre_low = pre_grad.astype(jnp.bfloat16)
    up_weight_grad = outer_sum(normed_low, pre_low)
    up_bias_grad = row_total(pre_low)
    normed_grad = product_back(pre_low, up_mat) + second_grad
    first_grad, gain_first_grad, shift_first_grad = first_pull(normed_grad)
    feedforward_terms = (
        up_weight_grad,
        up_bias_grad,
        down_weight_grad,
        down_bias_grad,
        gain_second_grad,
        shift_second_grad,
    )
    feedforward_parts = (
        lax.psum_scatter(feedforward_terms[0], AXES, scatter_dimension=0, tiled=True),
        lax.psum_scatter(feedforward_terms[1], AXES, scatter_dimension=0, tiled=True),
        lax.psum_scatter(feedforward_terms[2], AXES, scatter_dimension=0, tiled=True),
        lax.psum_scatter(feedforward_terms[3], AXES, scatter_dimension=0, tiled=True),
        lax.psum_scatter(feedforward_terms[4], AXES, scatter_dimension=0, tiled=True),
        lax.psum_scatter(feedforward_terms[5], AXES, scatter_dimension=0, tiled=True),
    )
    branch_low = first_grad.astype(jnp.bfloat16)
    out_weight_grad = outer_sum(mixed, branch_low)
    out_bias_grad = row_total(branch_low)
    mixed_grad = (
        product_back(branch_low, out_mat).astype(jnp.bfloat16).reshape(seqs, slots, heads, HEAD_DIM)
    )
    scores = scores_of(query_heads, key_rows, allowed, factor)
    probs = jnp.exp(scores - log_total)
    probs_low = probs.astype(jnp.bfloat16)
    probs_grad = jnp.einsum(
        "sqhd,skhd->shqk", mixed_grad, value_rows, preferred_element_type=jnp.float32
    )
    delta = jnp.sum(probs * probs_grad, -1, keepdims=True)
    score_grad = (probs * (probs_grad - delta)).astype(jnp.bfloat16)
    query_grad = (
        jnp.einsum("shqk,skhd->sqhd", score_grad, key_rows, preferred_element_type=jnp.float32)
        * factor
    )
    query_grad = query_grad.reshape(seqs, slots, width).astype(jnp.bfloat16)
    key_grad_all = jnp.einsum(
        "shqk,sqhd->skhd", score_grad, query_heads, preferred_element_type=jnp.float32
    )
    key_grad_all = (key_grad_all * factor).reshape(seqs, 2 * slots, width)
    value_grad_all = jnp.einsum(
        "shqk,sqhd->skhd", probs_low, mixed_grad, preferred_element_type=jnp.float32
    )
    value_grad_all = value_grad_all.reshape(seqs, 2 * slots, width)
    keys_back, values_back = (
        swapped(key_grad_all[:, slots:].astype(jnp.bfloat16), PAIR, 0).astype(jnp.float32),
        swapped(value_grad_all[:, slots:].astype(jnp.bfloat16), PAIR, 0).astype(jnp.float32),
    )
    key_grad = (key_grad_all[:, :slots] + keys_back).astype(jnp.bfloat16)
    value_grad = (value_grad_all[:, :slots] + values_back).astype(jnp.bfloat16)
    query_weight_grad = outer_sum(token_rows, query_grad)
    query_bias_grad = row_total(query_grad)
    key_weight_grad = outer_sum(token_rows, key_grad)
    value_weight_grad = outer_sum(token_rows, value_grad)
    value_bias_grad = row_total(value_grad)
    tokens_grad = first_grad + product_back(query_grad, query_mat) + product_back(key_grad, key_mat)
    tokens_grad = tokens_grad + product_back(value_grad, value_mat)
    tokens_gradient = tokens_grad.astype(jnp.bfloat16).reshape(tokens.shape)
    attention_terms = (
        query_weight_grad,
        query_bias_grad,
        key_weight_grad,
        value_weight_grad,
        value_bias_grad,
        out_weight_grad,
        out_bias_grad,
        gain_first_grad,
        shift_first_grad,
    )
    attention_parts = (
        lax.psum_scatter(attention_terms[0], AXES, scatter_dimension=0, tiled=True),
        lax.psum_scatter(attention_terms[1], AXES, scatter_dimension=0, tiled=True),
        lax.psum_scatter(attention_terms[2], AXES, scatter_dimension=0, tiled=True),
        lax.psum_scatter(attention_terms[3], AXES, scatter_dimension=0, tiled=True),
        lax.psum_scatter(attention_terms[4], AXES, scatter_dimension=0, tiled=True),
        lax.psum_scatter(attention_terms[5], AXES, scatter_dimension=0, tiled=True),
        lax.psum_scatter(attention_terms[6], AXES, scatter_dimension=0, tiled=True),
        lax.psum_scatter(attention_terms[7], AXES, scatter_dimension=0, tiled=True),
        lax.psum_scatter(attention_terms[8], AXES, scatter_dimension=0, tiled=True),
    )
    return (
        layer_output,
        tokens_gradient,
        attention_parts[0],
        attention_parts[1],
        attention_parts[2],
        attention_parts[3],
        attention_parts[4],
        attention_parts[5],
        attention_parts[6],
        attention_parts[7],
        attention_parts[8],
        feedforward_parts[0],
        feedforward_parts[1],
        feedforward_parts[2],
        feedforward_parts[3],
        feedforward_parts[4],
        feedforward_parts[5],
    )


F32 = jnp.float32
BF16 = jnp.bfloat16
MESH = pl.DeviceIdType.MESH
CHIPS = 16
LINE = 4
VMEM_BYTES = 63 * 1024 * 1024


def dot(left, right, left_dim, right_dim, precision=None):
    return lax.dot_general(
        left,
        right,
        (((left_dim,), (right_dim,)), ((), ())),
        preferred_element_type=F32,
        precision=precision,
    )


def nn(left, right):
    return dot(left, right, 1, 0)


def nt(left, right):
    return dot(left, right, 1, 1)


def tn(left, right):
    return dot(left, right, 0, 0)


def iota(shape, dim):
    return lax.broadcasted_iota(jnp.int32, shape, dim)


class Refs(dict):
    __getattr__ = dict.__getitem__
    __setattr__ = dict.__setitem__


def column_sum(values):
    return jnp.sum(values, 0, keepdims=True)


def lane_mean(values):
    return jnp.mean(values, -1, keepdims=True)


def block(start, size):
    return pl.ds(pl.multiple_of(start * size, size), size)


def each(count, act):
    def step(s, carry):
        act(s)
        return carry

    lax.fori_loop(0, count, step, 0)


class Links:
    def __init__(self):
        self.b = lax.axis_index(BATCH)
        self.p = lax.axis_index(PAIR)
        self.z = lax.div(self.b, 4)
        x = lax.rem(self.b, 2)
        y = lax.rem(lax.div(self.b, 2), 2)
        self.f = x + self.p * (y - x)
        self.g = y + self.p * (x - y)
        self.near = self.chip(self.z, 1)
        self.far = self.index(self.z, self.f, 1 - self.g)
        third = lax.div(self.z, 3)
        second = lax.div(self.z, 2) - third
        zeroth = 1 - lax.div(self.z + 3, 4)
        self.is_z = (zeroth, 1 - zeroth - second - third, second, third)

    def index(self, z, f, g):
        return 4 * z + (1 + self.p) * f + (2 - self.p) * g

    def chip(self, z, side):
        return self.index(z, self.f + side * (1 - 2 * self.f), self.g)

    def by_z(self, values):
        return sum(flag * value for flag, value in zip(self.is_z, values))

    def column(self):
        return [lax.rem(self.z + step, LINE) for step in (1, 3, 2)]

    def other(self):
        return (self.b, 1 - self.p)

    def greet(self):
        semaphore = pltpu.get_barrier_semaphore()
        partners = [self.chip(z, 0) for z in self.column()] + [self.near, self.far]
        for device in [(chip, self.p) for chip in partners] + [self.other()]:
            pl.semaphore_signal(semaphore, inc=1, device_id=device, device_id_type=MESH)

    def meet(self):
        pl.semaphore_wait(pltpu.get_barrier_semaphore(), 6)


class Gather:
    ARRIVE = ((1, 2, 3), (2, 0, 3), (3, 1, 0), (2, 1, 0))
    FROM_FAR = CHIPS
    ARRIVALS = CHIPS + 1

    def __init__(self, links, ref, send, recv, near_first=False):
        self.links, self.ref, self.send, self.recv = links, ref, send, recv
        self.size = ref.shape[0] // CHIPS
        self.near_first = near_first

    def copy(self, rows, chip, arrival):
        part = self.ref.at[rows]
        return pltpu.make_async_remote_copy(
            src_ref=part,
            dst_ref=part,
            send_sem=self.send,
            recv_sem=self.recv.at[arrival],
            device_id=(chip, self.links.p),
            device_id_type=MESH,
        )

    def wait(self, shard):
        self.copy(block(shard, self.size), self.links.far, shard).wait_recv()

    def to_far(self, z, side):
        shard = self.links.chip(z, side)
        self.copy(block(shard, self.size), self.links.far, self.FROM_FAR).start()

    def to_near(self, z):
        shard = self.links.chip(z, 0)
        self.copy(block(shard, self.size), self.links.near, shard).start()

    def to_column(self, z, side):
        k = self.links
        shard = k.chip(k.z, side)
        self.copy(block(shard, self.size), k.chip(z, 0), shard).start()

    def own(self):
        k = self.links
        self.to_near(k.z)
        self.to_far(k.z, 0)
        for z in k.column():
            self.to_column(z, 0)

    def near(self, turn):
        k = self.links
        z = k.z if turn == 0 else k.by_z([order[turn - 1] for order in self.ARRIVE])
        self.wait(k.chip(z, 1))
        if self.near_first and turn == 0:
            for other in k.column():
                self.to_column(other, 1)
        self.to_far(z, 1)

    def along(self, turn):
        k = self.links
        z = k.by_z([order[turn] for order in self.ARRIVE])
        self.wait(k.chip(z, 0))
        if not self.near_first:
            self.to_near(z)
        self.to_far(z, 0)

    def steps(self):
        steps = [self.own, lambda: self.near(0)]
        for turn in range(LINE - 1):
            steps.append(lambda turn=turn: self.along(turn))
            steps.append(lambda turn=turn: self.near(turn + 1))
        return steps

    def finish(self):
        self.copy(slice(0, 8 * self.size), self.links.far, self.FROM_FAR).wait_recv()

    def drain(self):
        self.copy(slice(0, 15 * self.size), self.links.far, self.FROM_FAR).wait_send()


class Reduce:
    LEAVE = ((3, 2, 1), (3, 2, 0), (0, 1, 3), (0, 1, 2))
    SLOTS = 15
    ARRIVALS = 10

    def __init__(self, links, grad, land, send, recv, near_first=False):
        self.links, self.grad, self.land = links, grad, land
        self.send, self.recv = send, recv
        self.size = grad.shape[0] // CHIPS
        self.near_first = near_first

    def rows(self, z, f, count=1, far=0):
        k = self.links
        g = k.g + far * (1 - 2 * k.g)
        at = 4 * z + 2 * g + f
        return pl.ds(pl.multiple_of(at * self.size, self.size), count * self.size)

    def slots(self, slot, count=1):
        start = slot * self.size
        return pl.ds(start if isinstance(slot, int) else pl.multiple_of(start, self.size), count * self.size)

    def copy(self, rows, slots, chip, arrival):
        return pltpu.make_async_remote_copy(
            src_ref=self.grad.at[rows],
            dst_ref=self.land.at[slots],
            send_sem=self.send,
            recv_sem=self.recv.at[arrival],
            device_id=(chip, self.links.p),
            device_id_type=MESH,
        )

    def wait(self, arrival, count):
        rows = slice(0, count * self.size)
        self.copy(rows, rows, self.links.far, arrival).wait_recv()

    def wait_far(self, z):
        self.wait(z, 2)

    def wait_near(self, z):
        self.wait(4 if self.near_first else 4 + z, 1)

    def wait_column(self, side):
        self.wait(8 + side, 3)

    def far_slot(self, z, f):
        return 2 * z + f

    def near_slot(self, z):
        return 8 if self.near_first else 8 + z

    def column_slot(self, step, side):
        return (9 + 3 * side if self.near_first else 12) + step - 1

    def column_slots(self, side):
        return [self.column_slot(step, side) for step in range(1, LINE)]

    def total(self, rows, slots):
        total = self.grad[rows].astype(F32)
        for slot in slots:
            total = total + self.land[self.slots(slot)].astype(F32)
        return total

    def add_on(self, rows, slots):
        self.grad[rows] = self.total(rows, slots).astype(self.grad.dtype)

    def far(self, z):
        self.copy(self.rows(z, 0, 2, 1), self.slots(self.far_slot(z, 0), 2), self.links.far, z).start()

    def near(self, z):
        k = self.links
        more = []
        self.wait_far(z)
        if self.near_first:
            self.wait_column(1)
            more = self.column_slots(1)
        rows = self.rows(z, 1 - k.f)
        self.add_on(rows, [self.far_slot(z, 1 - k.f)] + more)
        arrival = 4 if self.near_first else 4 + z
        self.copy(rows, self.slots(self.near_slot(z)), k.near, arrival).start()

    def along(self, turn, side):
        k = self.links
        z = k.by_z([order[turn] for order in self.LEAVE])
        f = k.f + side * (1 - 2 * k.f)
        rows, more = self.rows(z, f), []
        if not self.near_first:
            self.wait_near(z)
            more = [self.near_slot(z)]
        elif side == 1:
            self.wait_far(z)
        self.add_on(rows, [self.far_slot(z, f)] + more)
        slot = self.column_slot(lax.rem(k.z - z + LINE, LINE), side)
        self.copy(rows, self.slots(slot), k.chip(z, 0), 8 + side).start()

    def steps(self):
        steps = [lambda z=z: self.far(z) for z in range(LINE)]
        near = [lambda z=z: self.near(z) for z in range(LINE)]
        sides = (1, 0) if self.near_first else (0,)
        along = [
            lambda turn=turn, side=side: self.along(turn, side)
            for turn in range(LINE - 1)
            for side in sides
        ]
        if self.near_first:
            return steps + along + [lambda: self.near(self.links.z)]
        return steps + near + along

    def result(self):
        k = self.links
        self.wait_near(k.z)
        self.wait_column(0)
        slots = [self.far_slot(k.z, k.f), self.near_slot(k.z)]
        return self.total(self.rows(k.z, k.f), slots + self.column_slots(0))

    def drain(self):
        rows = slice(0, 15 * self.size)
        self.copy(rows, rows, self.links.far, 0).wait_send()


class Steps:
    def __init__(self, seqs, course, transfers):
        lines = [iter(steps) for steps in transfers]
        self.seqs, self.count = seqs, 0
        self.waiting = {place: [next(lines[n]) for n in order] for place, order in course.items()}
        assert all(next(line, None) is None for line in lines)

    def run(self):
        for step in self.waiting.pop(self.count, ()):
            step()
        self.count += 1

    def once(self, act):
        self.run()
        act()

    def loop(self, act, first=None, count=None):
        count = self.seqs if count is None else count
        self.run()
        if first is not None:
            first()
        later = []
        for s in range(1, count):
            later.append((s, self.waiting.pop(self.count, ())))
            self.count += 1

        def turn(s):
            for at, steps in later:
                if steps:

                    @pl.when(s == at)
                    def _():
                        for step in steps:
                            step()

            act(s)

        each(count, turn)


def laying(blocks, cols):
    size = cols // blocks
    pick = iota((128, cols), 0) == lax.rem(iota((128, cols), 1), size)
    return pick, lax.div(iota((blocks, cols), 1), size) == iota((blocks, cols), 0)


def core_order(chip, p):
    low = lax.rem(chip, 4)
    step = (low == 1).astype(jnp.int32) - (low == 2).astype(jnp.int32)
    return chip + p * step


def vector_rows(shape, dim, vector, p):
    device, row = iota(shape, dim), iota(shape, 1 - dim)
    return row == 16 * core_order(lax.div(device, 2), p) + 2 * vector + lax.rem(device, 2)


def unit_rows(shape, dim, which, p):
    return iota(shape, 1 - dim) == 16 * core_order(iota(shape, dim), p) + which


def unpack_small(r, p):
    rows = CHIPS * 16
    flat = r.small_all[...].astype(BF16)
    pick, place = laying(2 * CHIPS, r.vec.shape[1])
    for vector in range(8):
        chosen = nn(vector_rows((2 * CHIPS, rows), 0, vector, 0).astype(BF16), flat[:, :128])
        laid = nn(chosen.astype(BF16), pick.astype(BF16))
        r.vec[vector : vector + 1] = column_sum(jnp.where(place, laid, 0.0))
    pick, place = laying(CHIPS, r.upb.shape[1])
    chosen = nn(unit_rows((CHIPS, rows), 0, p, 0).astype(BF16), flat[:, 128:])
    laid = nn(chosen.astype(BF16), pick.astype(BF16))
    r.upb[...] = column_sum(jnp.where(place, laid, 0.0))


def pack_small(r, p):
    rows, width = CHIPS * 16, r.gvec.shape[1]
    for vector in range(2, 8):
        r.gvec[vector : vector + 1] = column_sum(r.gacc[8 * vector : 8 * vector + 8])
    row = iota((rows, 1), 0)
    device = 2 * core_order(lax.div(row, 16), p) + lax.rem(row, 2)
    chosen = lax.div(lax.rem(iota((rows, 8), 0), 16), 2) == iota((rows, 8), 1)
    spread = nn(chosen.astype(BF16), r.gvec[...].astype(BF16))
    place = device == lax.div(iota((1, width), 1), width // (2 * CHIPS))
    pick, _ = laying(2 * CHIPS, width)
    narrow = nt(jnp.where(place, spread, 0.0).astype(BF16), pick.astype(BF16))
    pick, place = laying(CHIPS, r.upg.shape[1])
    blocks = nt(jnp.where(place, r.upg[...], 0.0).astype(BF16), pick.astype(BF16))
    wide = nn(unit_rows((rows, CHIPS), 1, p, p).astype(BF16), blocks.astype(BF16))
    low = jnp.concatenate([narrow, wide], 1).astype(BF16)
    space = r.gq2.shape[0] // CHIPS
    for chip in range(CHIPS):
        r.gq2[space * chip + space - 16 : space * chip + space] = low[16 * chip : 16 * chip + 16]


def half_lanes(values, half, factor=None):
    mask = lax.div(iota((1, values.shape[1]), 1), HEAD_DIM) == half
    kept = jnp.where(mask, values, jnp.zeros_like(values))
    return kept if factor is None else kept * jnp.asarray(factor, values.dtype)


def normalize(values):
    centred = values - lane_mean(values)
    scale = lax.rsqrt(lane_mean(centred * centred) + EPSILON)
    return centred * scale, scale


def norm_back(grad, hat, scale):
    return scale * (grad - lane_mean(grad) - hat * lane_mean(grad * hat))


def gelu_both(value):
    square = value * value
    root = 0.7978845608028654
    inner = value * (root + root * 0.044715 * square)
    bent = 0.5 * jnp.tanh(inner) + 0.5
    slope = root + 3.0 * root * 0.044715 * square
    return value * bent, bent + 2.0 * value * slope * (bent - bent * bent)


UP_LANES = (slice(0, 768), slice(768, 1536),)
UP_NEAR_FIRST = (False, True)
DOWN_LANES = (slice(0, 512), slice(512, 768),)
DOWN_NEAR_FIRST = (False, True)
UP_SUM_LANES = (slice(0, 768), slice(768, 1536),)
UP_SUM_NEAR_FIRST = (True, False)
DOWN_SUM_LANES = (slice(0, 512), slice(512, 768),)
DOWN_SUM_NEAR_FIRST = (False, True)
UNITS = (
    ("sa",),
    ("sb",),
    ("unpack",),
    ("att", 0),
    ("att", 1),
    ("att", 2),
    ("wo",),
    ("out",),
    ("up", 0),
    ("up", 1),
    ("do", 0),
    ("do", 1),
    ("dw", 0),
    ("dw", 1),
    ("ln2",),
    ("ge",),
    ("ddw",),
    ("gd", 0),
    ("gd", 1),
    ("gd", 2),
    ("gd", 3),
    ("hb",),
    ("gu", 0),
    ("gu", 1),
    ("gu", 2),
    ("gu", 3),
    ("no",),
    ("nw",),
    ("ln1",),
    ("mb",),
    ("go",),
    ("ab", 0),
    ("gq", 0),
    ("ab", 1),
    ("gq", 1),
    ("ab", 2),
    ("ps",),
    ("gq", 2),
    ("to",),
    ("tw",),
    ("te",),
    ("end",),
)
COURSE = {
    0: (6,),
    1: (0, 1, 2, 3, 1, 6, 6, 2,),
    2: (3, 4, 0, 0, 7, 1, 5, 1, 1, 2, 0, 0, 1, 1, 2, 0, 0, 2, 3, 0, 1, 4, 2, 2, 3, 3, 6,),
    5: (2, 5,),
    6: (3, 3,),
    8: (4,),
    9: (3,),
    10: (6,),
    11: (4, 4,),
    13: (6,),
    14: (4, 4, 7, 6,),
    17: (4, 5,),
    19: (5,),
    20: (5, 5, 5, 5, 7,),
    24: (6, 7, 7, 7, 7, 7,),
    43: (9,),
    44: (9, 8,),
    46: (8, 9, 9, 8,),
    49: (8,),
    52: (9, 9,),
    53: (9, 9, 9, 8, 8, 8,),
    55: (8, 10, 10,),
    58: (10, 10, 8,),
    60: (9,),
    62: (8, 11, 11,),
    63: (8,),
    65: (11,),
    68: (10, 10, 10, 9,),
    69: (11, 11, 11,),
    72: (12, 10, 10, 10, 12, 11, 11,),
    75: (12, 12, 12, 12,),
    76: (11,),
    77: (13, 11,),
    78: (12,),
    79: (9, 11, 12, 13, 13, 13,),
    82: (13, 12, 12,),
    83: (14, 12, 14, 13,),
    84: (13, 13, 14, 14,),
    85: (11,),
    87: (14, 13, 14, 14, 8, 14, 13, 12, 10,),
    88: (13,),
    89: (14,),
    90: (14, 10,),
    91: (14, 13, 14,),
}


class Layer:
    def __init__(self, r, p):
        self.r, self.p = r, p
        self.slots = r.tokens.shape[2]
        self.width = r.tokens.shape[3]
        self.half = self.width // 2
        self.units = r.wup.shape[1]

    def rows(self, s):
        return block(s, 2 * self.slots)

    def side(self, s, side):
        return block(2 * s + side, self.slots)

    def own_lanes(self, pair):
        return pl.ds(pl.multiple_of(self.p * self.half + 128 * pair, 128), 128)

    def project(self, s, pair):
        r = self.r
        result = nn(r.x_all[self.rows(s)], r.wq[pair][...])
        lanes = self.own_lanes(pair)
        query = result[:, :128] + r.vec[0:1, lanes]
        value = result[:, 256:] + r.vec[1:2, lanes]
        r.qkv[pair, self.rows(s)] = jnp.concatenate([query, result[:, 128:256], value], 1).astype(BF16)

    def mask(self, s):
        r = self.r
        rows, space = r.fill.shape[1:]
        rest = jnp.zeros((1, space - rows), F32)
        ids = [r.segment_ids[s, half : half + 1].astype(F32) for half in range(2)]
        across = jnp.broadcast_to(jnp.concatenate(ids + [rest], 1), (space, space))
        r.fill[s] = jnp.where(across.T[:rows] == across[:rows], 0.0, NEG_FILL).astype(BF16)

    def heads(self, s, pair):
        held = self.r.qkv[pair, self.rows(s)]
        return held[:, :128], held[:, 128:256], held[:, 256:]

    def widened(self, values):
        rest = self.r.fill.shape[2] - values.shape[0]
        return jnp.concatenate([values, jnp.zeros((rest, values.shape[1]), values.dtype)], 0)

    def both_halves(self, values, factor=None, widen=False):
        parts = [half_lanes(values, half, factor) for half in range(2)]
        return jnp.concatenate([self.widened(part) if widen else part for part in parts], 0)

    def attend(self, s, pair):
        r = self.r
        rows, space = r.fill.shape[1:]
        queries, keys, values = self.heads(s, pair)
        values_t = values.T
        r.probs_grad[...] = nt(self.both_halves(keys, HEAD_DIM**-0.5), self.widened(queries))
        parts = []
        for half in range(2):
            top, total = NEG_FILL, 0.0
            for at in range(0, rows, 64):
                here = slice(rows * half + at, rows * half + at + 64)
                scores = r.probs_grad[here] + r.fill[s, at : at + 64].astype(F32)
                r.probs_grad[here] = scores
                top = jnp.maximum(top, jnp.max(scores.reshape(8, 8, space), 0))
            top = jnp.max(top, 0, keepdims=True)
            for at in range(0, rows, 64):
                here = slice(rows * half + at, rows * half + at + 64)
                raised = jnp.exp(r.probs_grad[here] - top)
                r.probs_grad[here] = raised
                total = total + jnp.sum(raised.reshape(8, 8, space), 0)
            share = 1.0 / column_sum(total)
            lanes = slice(space * half, space * half + space)
            for at in range(0, rows, 64):
                here = slice(rows * half + at, rows * half + at + 64)
                r.pt[3 * s + pair, at : at + 64, lanes] = (r.probs_grad[here] * share).astype(BF16)
            head = values_t[HEAD_DIM * half : HEAD_DIM * half + HEAD_DIM]
            parts.append(nn(head, r.pt[3 * s + pair, :, lanes]))
        mixed = jnp.concatenate(parts, 0).T[:rows]
        r.mixed[self.rows(s), self.own_lanes(pair)] = mixed.astype(BF16)

    def out_project(self, s):
        r, p = self.r, self.p
        mixed = r.mixed[self.side(s, p)]
        sides = [nn(mixed, r.wo[side]) for side in range(2)]
        r.product[: self.slots] = jnp.concatenate(sides, 1)
        for at, rows in self.pieces(s):
            resid = r.x_all[rows].astype(F32) + r.product[at] + r.vec[2:3]
            hat, scale = normalize(resid)
            r.xhat[s, at] = hat
            r.rstd[s, at] = jnp.broadcast_to(scale, (scale.shape[0], 128))
            r.n_all[rows] = (hat * r.vec[3:4] + r.vec[4:5]).astype(BF16)

    def feed_up(self, s, lanes):
        r = self.r
        r.product[...] = nn(r.n_all[self.rows(s)], r.wup[:, lanes])
        for at, rows in self.strips(s):
            hidden, slope = gelu_both(r.product[at] + r.upb[:, lanes])
            r.hidden[rows, lanes] = hidden.astype(BF16)
            r.slope[rows, lanes] = slope.astype(BF16)

    def two(self, ref, n, side):
        return jnp.concatenate([ref[self.side(2 * n + s, side)] for s in range(2)], 0)

    def by_two(self, rows):
        return rows.reshape(2, self.slots, rows.shape[1])

    def feed_down(self, n, side, lanes):
        return self.by_two(nn(self.two(self.r.hidden, n, side), self.r.wdown[:, lanes]))

    def pieces(self, s):
        for at in range(0, self.slots, 32):
            start = (2 * s + self.p) * self.slots + at
            yield slice(at, at + 32), pl.ds(pl.multiple_of(start, 32), 32)

    def strips(self, s):
        for at in range(0, 2 * self.slots, 32):
            start = 2 * s * self.slots + at
            yield slice(at, at + 32), pl.ds(pl.multiple_of(start, 32), 32)

    def add_rows(self, vector, values):
        folded = values.reshape(values.shape[0] // 8, 8, values.shape[1])
        self.r.gacc[8 * vector : 8 * vector + 8] += jnp.sum(folded, 0)

    def finish_norm(self, s):
        r = self.r
        for at, rows in self.pieces(s):
            normed = r.xhat[s, at] * r.vec[3:4] + r.vec[4:5]
            resid = normed + r.part_own[s, at] + r.part_in[s, at].astype(F32) + r.vec[5:6]
            hat, scale = normalize(resid)
            r.final[s, at] = (hat * r.vec[6:7] + r.vec[7:8]).astype(BF16)
            grad = r.out_grad[s, at].astype(F32)
            self.add_rows(6, grad * hat)
            self.add_rows(7, grad)
            back = norm_back(grad * r.vec[6:7], hat, scale)
            r.resid_grad[s, at] = back
            low = back.astype(BF16)
            r.dd_all[rows] = low
            self.add_rows(5, low.astype(F32))

    def put_blocks(self, ref, first, result, size):
        space = ref.shape[0] // CHIPS
        low = result.astype(BF16)
        for n in range(result.shape[0] // size):
            chip = first + n
            step = (0, 1, -1, 0)[chip % 4]
            at = chip * space
            rows = pl.ds(pl.multiple_of(at + self.p * step * space, 16), size) if step else slice(at, at + size)
            ref[rows] = low[n * size : n * size + size]

    def first_down_weight_grad(self):
        r = self.r
        most = slice(0, r.hidden.shape[0] - 2 * self.slots)
        r.first_sum[...] = tn(r.hidden[most, : self.half], r.dd_all[most])

    def down_weight_grad(self, m):
        r = self.r
        at = slice(self.half * m, self.half * m + self.half)
        if m == 0:
            last = slice(r.hidden.shape[0] - 2 * self.slots, r.hidden.shape[0])
            total = r.first_sum[...] + tn(r.hidden[last, at], r.dd_all[last])
        else:
            total = tn(r.hidden[:, at], r.dd_all[...])
        self.put_blocks(r.gd, 4 * m, total, self.half // 4)

    def hidden_back(self, s):
        r = self.r
        grads = r.dd_all[self.rows(s)]
        for start in range(0, self.units, self.width):
            lanes = slice(start, start + self.width)
            r.product[...] = nt(grads, r.wdown[lanes])
            total = 0.0
            for at, rows in self.strips(s):
                low = (r.product[at] * r.slope[rows, lanes].astype(F32)).astype(BF16)
                r.slope[rows, lanes] = low
                total = total + jnp.sum(low.astype(F32).reshape(4, 8, self.width), 0)
            r.upg[:, lanes] += column_sum(total)

    def up_weight_grad(self, m, n):
        r = self.r
        at = slice(self.half * m, self.half * m + self.half)
        lanes = slice(self.width * n, self.width * n + self.width)
        self.put_blocks(r.gu.at[:, lanes], 8 * m, tn(r.n_all[:, at], r.slope[:, lanes]), self.half // 8)

    def normed_back(self, n, side):
        return self.by_two(nt(self.two(self.r.slope, n, side), self.r.wup[...]))

    def first_norm_back(self, s):
        r = self.r
        for at, rows in self.pieces(s):
            grad = r.part_own[s, at] + r.part_in[s, at].astype(F32) + r.resid_grad[s, at]
            hat = r.xhat[s, at]
            self.add_rows(3, grad * hat)
            self.add_rows(4, grad)
            back = norm_back(grad * r.vec[3:4], hat, r.rstd[s, at, 0:1])
            r.resid_grad[s, at] = back
            low = back.astype(BF16)
            r.n_all[rows] = low
            self.add_rows(2, low.astype(F32))

    def out_weight_grad(self):
        r = self.r
        own = block(self.p, self.half)
        right = r.n_all[:, own]
        for m in range(2):
            at = slice(self.half * m, self.half * m + self.half)
            self.put_blocks(r.go, 8 * m, tn(r.mixed[:, at], right), self.half // 8)

    def mixed_back(self, s):
        r = self.r
        grads = r.n_all[self.rows(s)]
        own = block(self.p, self.half)
        total = nt(grads[:, : self.half], r.wo[0, own]) + nt(grads[:, self.half :], r.wo[1, own])
        r.dm[self.rows(s)] = total.astype(BF16)

    def attend_back(self, s, pair):
        r = self.r
        scale = HEAD_DIM**-0.5
        unit = 3 * s + pair
        rows, space = r.fill.shape[1:]
        queries, keys, values = self.heads(s, pair)
        grads = r.dm[self.rows(s), 128 * pair : 128 * pair + 128]
        r.probs_grad[...] = nt(self.both_halves(values), self.widened(grads))
        for half in range(2):
            lanes = slice(space * half, space * half + space)
            total = 0.0
            for at in range(0, rows, 64):
                grad = r.probs_grad[rows * half + at : rows * half + at + 64]
                product = r.pt[unit, at : at + 64, lanes].astype(F32) * grad
                total = total + jnp.sum(product.reshape(8, 8, space), 0)
            delta = column_sum(total)
            for at in range(0, rows, 64):
                grad = r.probs_grad[rows * half + at : rows * half + at + 64]
                probs = r.pt[unit, at : at + 64, lanes].astype(F32)
                r.score_grad[at : at + 64, lanes] = (probs * (grad - delta)).astype(BF16)
        key_grad = nn(r.score_grad[...], self.both_halves(queries, scale, True))
        keys_t = keys.T * jnp.asarray(scale, BF16)
        query_parts = []
        for half in range(2):
            at = HEAD_DIM * half
            query_parts.append(
                nn(keys_t[at : at + HEAD_DIM], r.score_grad[:, space * half : space * half + space])
            )
        query_grad = jnp.concatenate(query_parts, 0).T[:rows]
        r.dqkv[pair][self.rows(s), :256] = jnp.concatenate([query_grad, key_grad], 1).astype(BF16)
        for other in ((0,), (1, 2), ())[pair]:
            grads = r.dm[self.rows(s), 128 * other : 128 * other + 128]
            value_grad = nn(r.pt[3 * s + other], self.both_halves(grads, None, True))
            r.dqkv[other][self.rows(s), 256:] = value_grad.astype(BF16)

    def project_weight_grad(self, pair):
        r = self.r
        target, right = (r.gq0, r.gq1, r.gq2)[pair], r.dqkv[pair][...]
        if pair == 1:
            right = jnp.concatenate([right, r.dqkv[2][:, 256:]], 1)
        if pair == 2:
            right = right[:, :256]
        for m in range(2):
            at = slice(self.half * m, self.half * m + self.half)
            self.put_blocks(target, 8 * m, tn(r.x_all[:, at], right), self.half // 8)

    def project_bias_grad(self, pair):
        r = self.r
        right = r.dqkv[pair]
        lanes = self.own_lanes(pair)
        r.gvec[0:1, lanes] = column_sum(right[:, :128].astype(F32))
        r.gvec[1:2, lanes] = column_sum(right[:, 256:].astype(F32))

    def token_back(self, n, side):
        r = self.r
        total = 0.0
        for pair in range(3):
            total = total + nt(self.two(r.dqkv[pair], n, side), r.wq[pair][...])
        return self.by_two(total)


def ordered(size):
    column = iota((1, 8 * size), 1)
    within = lax.rem(column, 4 * size)
    source = 2 * size * lax.div(within, size) + size * lax.div(column, 4 * size) + lax.rem(within, size)
    return iota((8 * size, 8 * size), 0) == source


def place_small(r, p):
    r.small_in[...] = jnp.zeros_like(r.small_in)
    rows = [(row, 0, vector) for row, vector in enumerate(r.vectors)] + [(0, 128, r.up_bias)]
    for row, lane, vector in rows:
        count = vector.shape[0]
        values = vector[...].reshape(1, count).astype(F32)
        for core in range(2):

            @pl.when(p == core)
            def _():
                at = 2 * row + core
                r.small_in[at : at + 1, lane : lane + count] = values


def pack_square(r, half, piece):
    at = half * piece
    for core in range(2):
        if piece == 3:
            r.stack[core, :, at : at + half] = r.out_weight[:, half * core : half * core + half].astype(F32)
            continue
        for part, weight in enumerate((r.query_weight, r.key_weight, r.value_weight)):
            lane = half * core + 128 * piece
            r.stack[core, :, at + 128 * part : at + 128 * part + 128] = weight[:, lane : lane + 128].astype(F32)


def pack_up(r, half, size):
    rows = r.up_weight.shape[0]
    groups = [r.up_weight[:, 8 * size * group : 8 * size * group + 8 * size] for group in range(CHIPS // 4)]
    stacked = jnp.concatenate([group.astype(F32) for group in groups], 0).astype(BF16)
    ordered_units = nn(stacked, ordered(size).astype(BF16))
    for group in range(CHIPS // 4):
        to = 4 * half + 4 * size * group
        for core in range(2):
            r.stack[core, :, to : to + 4 * size] = ordered_units[
                rows * group : rows * group + rows, 4 * size * core : 4 * size * core + 4 * size
            ]


def layer_kernel(r):
    k = Links()
    p = k.p
    seqs = r.tokens.shape[0]
    layer = Layer(r, p)
    half = layer.half
    width = layer.width
    per = r.stack.shape[1]
    size = r.down_weight.shape[0]
    pack = r.stack.shape[2]
    def to_other(src, dst, group, arrival):
        return pltpu.make_async_remote_copy(
            src_ref=src,
            dst_ref=dst,
            send_sem=r.pair_send.at[group],
            recv_sem=r.pair_recv.at[arrival],
            device_id=k.other(),
            device_id_type=MESH,
        )

    def local(src, dst, which):
        return pltpu.make_async_copy(src, dst, r.local_done.at[which])

    def trade_own(ref, group, base):
        return lambda s: to_other(ref.at[layer.side(s, p)], ref.at[layer.side(s, p)], group, base + s)

    def trade_slot(src, dst, group, base):
        return lambda s: to_other(src.at[s], dst.at[s], group, base + s)

    def sent(group):
        to_other(r.part_out, r.part_in, group, 0).wait_send()

    small_swap = to_other(r.small_in, r.small_theirs, 0, 0)
    share = to_other(r.wo.at[p], r.wo.at[p], 1, 1)
    sums_swap = to_other(r.sum_small, r.sum_theirs, 2, 2)
    inputs = lambda s: to_other(r.tokens.at[s, 0], r.x_all.at[layer.side(s, p)], 3, 3)
    normed = trade_own(r.n_all, 4, 4)
    down_part = trade_slot(r.part_out, r.part_in, 5, 4 + seqs)
    down_grad = trade_own(r.dd_all, 6, 4 + 2 * seqs)
    normed_part = trade_slot(r.part_out, r.part_in, 7, 4 + 3 * seqs)
    branch = trade_own(r.n_all, 8, 4 + 4 * seqs)
    token_part = trade_slot(r.part_out, r.part_in, 9, 4 + 5 * seqs)

    def mixed(s, pair):
        part = r.mixed.at[layer.rows(s), layer.own_lanes(pair)]
        return to_other(part, part, 10, 4 + 6 * seqs + s)

    def mixed_in(s):
        part = r.mixed.at[layer.rows(s), block(p, half)]
        return to_other(part, part, 10, 4 + 6 * seqs + s)

    def pack_swap(lanes):
        return to_other(r.sum_pack.at[block(1 - p, per), lanes], r.out_pack.at[p, :, lanes], 11, 4 + 7 * seqs)

    pieces = [slice(0, half), slice(half, 2 * half), slice(2 * half, 4 * half)]
    pieces += [slice(4 * half + lanes.start, 4 * half + lanes.stop) for lanes in UP_LANES]

    def piece_swap(n):
        lanes = pieces[n]
        return to_other(
            r.stack.at[1 - p, :, lanes], r.sum_pack.at[block(p, per), lanes], 12, 5 + 7 * seqs + n
        )

    def place_piece(n, target):
        lanes = pieces[n]

        def act():
            piece_swap(n).wait_recv()
            r.sum_pack[block(p, per), lanes] = r.stack[p, :, lanes]
            target[block(k.b, 2 * per)] = r.sum_pack[:, lanes].astype(BF16)

        return act

    def gather(n, ref, near_first=False):
        return Gather(k, ref, r.gather_send.at[n], r.gather_recv.at[n], near_first)

    def reduce(n, grad, land, near_first=False):
        return Reduce(k, grad, land, r.reduce_send.at[n], r.reduce_recv.at[n], near_first)

    small = gather(0, r.small_all)
    heads = [gather(1 + pair, ref) for pair, ref in enumerate((r.wq0, r.wq1, r.wq2o))]
    ups = [gather(4 + n, r.wup.at[:, lanes], first) for n, (lanes, first) in enumerate(zip(UP_LANES, UP_NEAR_FIRST))]
    downs = [
        gather(6 + n, r.wdown.at[:, lanes], first)
        for n, (lanes, first) in enumerate(zip(DOWN_LANES, DOWN_NEAR_FIRST))
    ]
    gathers = [small] + heads + ups + downs
    down_sums = [
        reduce(n, r.gd.at[:, lanes], land, first)
        for n, (lanes, land, first) in enumerate(zip(DOWN_SUM_LANES, r.land_d, DOWN_SUM_NEAR_FIRST))
    ]
    up_sums = [
        reduce(2 + n, r.gu.at[:, lanes], land, first)
        for n, (lanes, land, first) in enumerate(zip(UP_SUM_LANES, r.land_u, UP_SUM_NEAR_FIRST))
    ]
    out_sum = reduce(4, r.goq, r.land_oq)
    head_sums = [reduce(5, r.gq1, r.land_q1), reduce(6, r.gq2, r.land_q2)]
    reduces = down_sums + up_sums + [out_sum] + head_sums

    def store(one, lanes):
        def act():
            r.sum_pack[:, lanes] = one.result()
            pack_swap(lanes).start()
            r.out_pack[p, :, lanes] = r.sum_pack[block(p, per), lanes]

        return act

    def store_down(one, lanes):
        def act():
            total = one.result()
            for group in range(size // per):
                to = slice(width * group + lanes.start, width * group + lanes.stop)
                r.out_pack[2, :, to] = total[per * group : per * group + per]

        return act

    def store_last():
        total = head_sums[1].result()
        r.sum_pack[:, packs[-1]] = total[: 2 * per]
        pack_swap(packs[-1]).start()
        r.sum_small[...] = total[2 * per :]
        sums_swap.start()
        r.out_pack[p, :, packs[-1]] = r.sum_pack[block(p, per), packs[-1]]

    packs = [slice(4 * half + lanes.start, 4 * half + lanes.stop) for lanes in UP_SUM_LANES]
    packs += [slice(0, 2 * half), slice(2 * half, 3 * half + 128), slice(3 * half + 128, 4 * half)]
    stores = [store_down(one, lanes) for one, lanes in zip(down_sums, DOWN_SUM_LANES)]
    stores += [store(one, lanes) for one, lanes in zip(up_sums + [out_sum] + head_sums[:1], packs)]
    stores.append(store_last)

    def place_small_rows():
        small_swap.wait_recv()
        r.small_all[block(k.b, 16)] = r.small_in[...] + r.small_theirs[...]

    def finish_out():
        heads[2].finish()
        r.wo[p] = r.wq2o[:, half:]
        share.start()

    starts = [place_small_rows]
    starts += [place_piece(n, target) for n, target in enumerate((r.wq0, r.wq1, r.wq2o))]
    starts += [place_piece(3 + n, r.wup.at[:, lanes]) for n, lanes in enumerate(UP_LANES)]
    spreads = [one.steps() for one in gathers]
    for steps_of, start in zip(spreads, starts):
        steps_of[0] = lambda start=start, own=steps_of[0]: (start(), own())
    sums = [one.steps() + [last] for one, last in zip(reduces, stores)]
    steps = Steps(seqs, COURSE, spreads + sums)

    k.greet()
    each(seqs, lambda s: local(r.tokens.at[s, 0], r.x_all.at[layer.side(s, p)], 0).start())
    local(r.cotangent.at[:, 0], r.out_grad, 1).start()
    r.wdown[block(k.b, size)] = r.down_weight[...]
    pack_square(r, half, 0)
    place_small(r, p)
    k.meet()
    piece_swap(0).start()
    small_swap.start()

    def wait_once(*copies):
        fresh = [copy for copy in copies if copy not in waited]
        waited.extend(fresh)
        return lambda s: [copy(s).wait_recv() for copy in fresh]

    waited = []

    def pack_heads():
        def act():
            pack_square(r, half, 1)
            piece_swap(1).start()
            pack_square(r, half, 2)
            pack_square(r, half, 3)
            piece_swap(2).start()

        steps.once(act)

    def pack_rest():
        def act():
            pack_up(r, half, size)
            for n in range(3, len(pieces)):
                piece_swap(n).start()
            each(seqs, lambda s: inputs(s).start())
            for sums in (r.gvec, r.gacc, r.upg):
                sums[...] = jnp.zeros_like(sums)

        steps.once(act)

    def unpack():
        def act():
            each(seqs, layer.mask)
            small.finish()
            unpack_small(r, p)
            to_other(r.part_out, r.part_in, 3, 3).wait_recv()
            local(r.part_out, r.part_in, 0).wait()

        steps.once(act)

    def attention(pair):
        def act(s):
            layer.project(s, pair)
            layer.attend(s, pair)
            mixed(s, pair).start()

        steps.loop(act, heads[pair].finish if pair < 2 else finish_out)

    def wait_share():
        steps.once(lambda: share.wait_recv())

    def first_half():
        def act(s):
            mixed_in(s).wait_recv()
            layer.out_project(s)
            normed(s).start()

        steps.loop(act)

    def feed(n):
        wait = wait_once(normed)

        def act(s):
            wait(s)
            layer.feed_up(s, UP_LANES[n])

        steps.loop(act, ups[n].finish)

    def feed_other(n):
        lanes = DOWN_LANES[n]

        def act(two):
            at = pl.ds(2 * two, 2)
            r.part_out[at, :, lanes] = layer.feed_down(two, 1 - p, lanes).astype(BF16)
            if n == len(DOWN_LANES) - 1:
                for s in range(2):
                    down_part(2 * two + s).start()

        steps.loop(act, downs[n].finish, seqs // 2)

    def feed_own(n):
        lanes = DOWN_LANES[n]

        def act(two):
            r.part_own[pl.ds(2 * two, 2), :, lanes] = layer.feed_down(two, p, lanes)

        steps.loop(act, count=seqs // 2)

    def second_norm():
        def act(s):
            down_part(s).wait_recv()
            layer.finish_norm(s)
            down_grad(s).start()
            local(r.final.at[s], r.layer_output.at[s, 0], 2).start()

        steps.loop(act, local(r.cotangent.at[:, 0], r.out_grad, 1).wait)

    def first_down_grads():
        def act():
            each(seqs - 1, lambda s: down_grad(s).wait_recv())
            layer.first_down_weight_grad()

        waited.append(down_grad)
        steps.once(act)

    def wait_grads():
        steps.once(lambda: down_grad(seqs - 1).wait_recv())

    def down_grads(m):
        steps.once(lambda: layer.down_weight_grad(m))

    def hidden_back():
        wait = wait_once(down_grad)

        def act(s):
            wait(s)
            layer.hidden_back(s)

        steps.loop(act)

    def up_grads(n):
        steps.once(lambda: layer.up_weight_grad(n // 2, n % 2))

    def back_other():
        def first():
            for group in (4, 5, 6):
                sent(group)

        def act(two):
            r.part_out[pl.ds(2 * two, 2)] = layer.normed_back(two, 1 - p).astype(BF16)
            for s in range(2):
                normed_part(2 * two + s).start()

        steps.loop(act, first, seqs // 2)

    def back_own():
        def act(two):
            r.part_own[pl.ds(2 * two, 2)] = layer.normed_back(two, p)

        steps.loop(act, count=seqs // 2)

    def first_norm():
        def act(s):
            normed_part(s).wait_recv()
            layer.first_norm_back(s)
            branch(s).start()

        steps.loop(act)

    def mixed_grad():
        def act(s):
            branch(s).wait_recv()
            layer.mixed_back(s)

        steps.loop(act)

    def out_grad():
        steps.once(layer.out_weight_grad)
        for one in downs:
            one.drain()

    def attention_back(pair):
        steps.loop(lambda s: layer.attend_back(s, pair))

    def head_grads(pair):
        steps.once(lambda: layer.project_weight_grad(pair))

    def pack_vectors():
        def act():
            for pair in range(3):
                layer.project_bias_grad(pair)
            pack_small(r, p)

        steps.once(act)

    def token_other():
        def act(two):
            r.part_out[pl.ds(2 * two, 2)] = layer.token_back(two, 1 - p).astype(BF16)
            for s in range(2):
                token_part(2 * two + s).start()

        steps.loop(act, lambda: sent(7), seqs // 2)

    def token_own():
        def act(two):
            r.part_own[pl.ds(2 * two, 2)] = layer.token_back(two, p)

        steps.loop(act, count=seqs // 2)

    def token_end():
        def first():
            for one in [small] + heads + ups:
                one.drain()
            for copy in (small_swap, share):
                copy.wait_send()
            to_other(r.stack.at[1 - p], r.stack.at[p], 12, 0).wait_send()
            for group in (3, 8, 10):
                sent(group)

        def act(s):
            token_part(s).wait_recv()
            total = r.part_own[s] + r.part_in[s].astype(F32) + r.resid_grad[s]
            r.token_grad[s] = total.astype(BF16)
            local(r.token_grad.at[s], r.tokens_gradient.at[s, 0], 3).start()

        steps.loop(act, first)

    def collect():
        def act():
            sums_swap.wait_recv()
            r.out_pack[2, 0:16, pack : pack + 256] = r.sum_small[...] + r.sum_theirs[...]
            whole = pack_swap(slice(0, pack))
            whole.wait()
            for one in reduces:
                one.drain()
            sums_swap.wait_send()
            sent(9)
            for outgoing in (2, 3):
                local(r.part_out, r.part_in, outgoing).wait()

        steps.once(act)

    units = dict(
        sa=pack_heads,
        sb=pack_rest,
        ge=first_down_grads,
        unpack=unpack,
        att=attention,
        wo=wait_share,
        out=first_half,
        up=feed,
        do=feed_other,
        dw=feed_own,
        ln2=second_norm,
        ddw=wait_grads,
        gd=down_grads,
        hb=hidden_back,
        gu=up_grads,
        no=back_other,
        nw=back_own,
        ln1=first_norm,
        mb=mixed_grad,
        go=out_grad,
        ab=attention_back,
        gq=head_grads,
        ps=pack_vectors,
        to=token_other,
        tw=token_own,
        te=token_end,
        end=collect,
    )
    for name, *which in UNITS:
        units[name](*which)
    assert not steps.waiting


def finish_kernel(r):
    p = lax.axis_index(PAIR)
    half = r.query_out.shape[1] // 2
    size = r.down_out.shape[0]
    for core in range(2):
        for pair in range(3):
            for part, target in enumerate((r.query_out, r.key_out, r.value_out)):
                place = (0, 1, 2, 6, 7, 8, 10, 11, 9)[3 * pair + part]
                at, lane = 128 * place, half * core + 128 * pair
                target[:, lane : lane + 128] = r.pack[core, :, at : at + 128]
        r.out_out[:, half * core : half * core + half] = r.pack[core, :, half : 2 * half]
    rows, width = r.query_out.shape
    groups = []
    for group in range(CHIPS // 4):
        at = 4 * half + 4 * size * group
        groups.append(jnp.concatenate([r.pack[core, :, at : at + 4 * size] for core in range(2)], 1))
    rest = jnp.concatenate(groups, 0)
    parts = []
    for _ in range(3):
        parts.append(rest.astype(BF16).astype(F32))
        rest = rest - parts[-1]
    laid = nt(jnp.concatenate(parts, 0).astype(BF16), ordered(size).astype(BF16))
    count = laid.shape[0] // 3
    laid = laid[:count] + laid[count : 2 * count] + laid[2 * count :]
    for group in range(CHIPS // 4):
        to = 8 * size * group
        r.up_out[:, to : to + 8 * size] = laid[rows * group : rows * group + rows]
    for group in range(size // rows):
        r.down_out[rows * group : rows * group + rows] = r.pack[2, :, width * group : width * group + width]
    small = r.pack[2, 0:16, 4 * half + r.up_out.shape[1] // 2 :]
    for vector, target in enumerate(r.vectors):
        row = jnp.where(p == 0, small[2 * vector : 2 * vector + 1], small[2 * vector + 1 : 2 * vector + 2])
        target[...] = row[:, : target.shape[1]]
    row = jnp.where(p == 0, small[0:1], small[1:2])
    r.up_vector[...] = row[:, 128 : 128 + size]


def call(kernel, ins, outs, scratch, semaphores, elsewhere=(), **params):
    names = list(ins) + list(outs) + list(scratch) + list(semaphores)

    def body(*refs):
        kernel(Refs(zip(names, refs)))

    def spec(name):
        return pl.BlockSpec(memory_space=pl.ANY if name in elsewhere else pltpu.VMEM)

    results = pl.pallas_call(
        body,
        out_shape=[jax.ShapeDtypeStruct(*held_as) for held_as in outs.values()],
        in_specs=[spec(name) for name in ins],
        out_specs=[spec(name) for name in outs],
        scratch_shapes=[pltpu.VMEM(*held_as) for held_as in scratch.values()] + list(semaphores.values()),
        compiler_params=pltpu.CompilerParams(**params),
        name=kernel.__name__,
    )(*ins.values())
    return Refs(zip(outs, results))


def fast(
    tokens,
    segment_ids,
    query_weight,
    query_bias,
    key_weight,
    value_weight,
    value_bias,
    out_weight,
    out_bias,
    first_gain,
    first_shift,
    up_weight,
    up_bias,
    down_weight,
    down_bias,
    second_gain,
    second_shift,
    cotangent,
):
    seqs, _, slots, width = tokens.shape
    units = up_weight.shape[1] // 2
    per = up_weight.shape[0]
    half = width // 2
    size = units // CHIPS
    rows = 2 * slots
    space = -(-rows // 128) * 128
    ins = dict(
        tokens=tokens,
        cotangent=cotangent,
        segment_ids=segment_ids,
        query_weight=query_weight,
        key_weight=key_weight,
        value_weight=value_weight,
        out_weight=out_weight,
        up_weight=up_weight,
        down_weight=down_weight,
        query_bias=query_bias,
        value_bias=value_bias,
        out_bias=out_bias,
        first_gain=first_gain,
        first_shift=first_shift,
        down_bias=down_bias,
        second_gain=second_gain,
        second_shift=second_shift,
        up_bias=up_bias,
    )
    pack = 4 * half + units
    outs = dict(
        layer_output=(tokens.shape, BF16),
        tokens_gradient=(tokens.shape, BF16),
        out_pack=((3, per, pack + 256), F32),
    )
    all_rows = seqs * rows
    held = dict(
        stack=((2, per, pack), F32),
        sum_pack=((2 * per, pack), F32),
        small_in=((16, 256), F32),
        small_theirs=((16, 256), F32),
        sum_theirs=((16, 256), F32),
        sum_small=((16, 256), F32),
        small_all=((CHIPS * 16, 256), F32),
        vec=((8, width), F32),
        upb=((1, units), F32),
        gvec=((8, width), F32),
        gacc=((64, width), F32),
        upg=((1, units), F32),
        fill=((seqs, rows, space), BF16),
        probs_grad=((2 * rows, space), F32),
        product=((rows, width), F32),
        score_grad=((rows, 2 * space), BF16),
        x_all=((all_rows, width), BF16),
        wq0=((width, half), BF16),
        wq1=((width, half), BF16),
        wq2o=((width, width), BF16),
        wo=((2, width, half), BF16),
        wup=((width, units), BF16),
        wdown=((units, width), BF16),
        qkv=((3, all_rows, half), BF16),
        pt=((3 * seqs, rows, 2 * space), BF16),
        mixed=((all_rows, width), BF16),
        xhat=((seqs, slots, width), F32),
        rstd=((seqs, slots, 128), F32),
        n_all=((all_rows, width), BF16),
        hidden=((all_rows, units), BF16),
        slope=((all_rows, units), BF16),
        part_own=((seqs, slots, width), F32),
        part_out=((seqs, slots, width), BF16),
        part_in=((seqs, slots, width), BF16),
        out_grad=((seqs, slots, width), BF16),
        final=((seqs, slots, width), BF16),
        token_grad=((seqs, slots, width), BF16),
        resid_grad=((seqs, slots, width), F32),
        dd_all=((all_rows, width), BF16),
        gd=((units, width), BF16),
        first_sum=((half, width), F32),
        land_d0=((Reduce.SLOTS * size, DOWN_SUM_LANES[0].stop), BF16),
        land_d1=((Reduce.SLOTS * size, width - DOWN_SUM_LANES[0].stop), BF16),
        land_u0=((Reduce.SLOTS * 2 * per, UP_SUM_LANES[0].stop), BF16),
        land_u1=((Reduce.SLOTS * 2 * per, units - UP_SUM_LANES[0].stop), BF16),
        land_oq=((Reduce.SLOTS * 2 * per, width), BF16),
        land_q1=((Reduce.SLOTS * 2 * per, half + 128), BF16),
        land_q2=((Reduce.SLOTS * (2 * per + 16), half - 128), BF16),
    )
    dma = pltpu.SemaphoreType.DMA
    semaphores = dict(
        pair_send=dma((13,)),
        pair_recv=dma((9 + 7 * seqs + len(UP_LANES),)),
        gather_send=dma((8,)),
        gather_recv=dma((8, Gather.ARRIVALS)),
        local_done=dma((4,)),
        reduce_send=dma((7,)),
        reduce_recv=dma((7, Reduce.ARRIVALS)),
    )

    def layer(r):
        r.gu = r.hidden.at[0:width]
        last = width + 16 * CHIPS
        r.goq = r.slope.at[0:width, 0 : 2 * half]
        split = 3 * half + 128
        r.gq0 = r.slope.at[0:width, 0:half]
        r.gq1 = r.slope.at[0:width, 2 * half : split]
        r.gq2 = r.slope.at[0:last, split : 4 * half]
        r.go = r.slope.at[0:width, half : 2 * half]
        r.wq = [r.wq0, r.wq1, r.wq2o.at[:, 0:half]]
        r.dqkv = [r.wdown.at[0:all_rows, 0:half], r.wdown.at[0:all_rows, half:width], r.dd_all.at[:, 0:half]]
        r.dm = r.dd_all.at[:, half:width]
        r.land_d = [r.land_d0, r.land_d1]
        r.land_u = [r.land_u0, r.land_u1]
        r.vectors = [
            r.query_bias,
            r.value_bias,
            r.out_bias,
            r.first_gain,
            r.first_shift,
            r.down_bias,
            r.second_gain,
            r.second_shift,
        ]
        layer_kernel(r)

    elsewhere = dict(tokens=1, cotangent=1, layer_output=1, tokens_gradient=1)
    done = call(
        layer, ins, outs, held, semaphores, elsewhere, vmem_limit_bytes=VMEM_BYTES, collective_id=0, has_side_effects=True
    )

    square = ((per, width), F32)
    line = ((1, per), F32)
    finals = dict(
        query_out=square,
        query_vector=line,
        key_out=square,
        value_out=square,
        value_vector=line,
        out_out=square,
        out_vector=line,
        gain_vector=line,
        shift_vector=line,
        up_out=(up_weight.shape, F32),
        up_vector=((1, size), F32),
        down_out=(down_weight.shape, F32),
        down_vector=line,
        last_gain_vector=line,
        last_shift_vector=line,
    )

    def finish(r):
        r.vectors = [
            r.query_vector,
            r.value_vector,
            r.out_vector,
            r.gain_vector,
            r.shift_vector,
            r.down_vector,
            r.last_gain_vector,
            r.last_shift_vector,
        ]
        finish_kernel(r)

    final = call(finish, dict(pack=done.out_pack), finals, {}, {}, vmem_limit_bytes=16 * 1024 * 1024)
    flat = [value[0] if value.shape[0] == 1 else value for value in final.values()]
    return (done.layer_output, done.tokens_gradient, *flat)


def solution(mesh):
    in_specs = (
        P(BATCH, PAIR, None, None),
        P(BATCH, None, None),
        P(AXES, None),
        P(AXES),
        P(AXES, None),
        P(AXES, None),
        P(AXES),
        P(AXES, None),
        P(AXES),
        P(AXES),
        P(AXES),
        P(AXES, None),
        P(AXES),
        P(AXES, None),
        P(AXES),
        P(AXES),
        P(AXES),
        P(BATCH, PAIR, None, None),
    )
    out_specs = (
        P(BATCH, PAIR, None, None),
        P(BATCH, PAIR, None, None),
        P(AXES, None),
        P(AXES),
        P(AXES, None),
        P(AXES, None),
        P(AXES),
        P(AXES, None),
        P(AXES),
        P(AXES),
        P(AXES),
        P(AXES, None),
        P(AXES),
        P(AXES, None),
        P(AXES),
        P(AXES),
        P(AXES),
    )
    small_slice = dict(mesh.shape) == {BATCH: CHIPS, PAIR: 2}
    part = fast if small_slice else local
    return jax.shard_map(part, mesh=mesh, in_specs=in_specs, out_specs=out_specs, check_vma=False)
```

```python
import jax
import jax.numpy as jnp
from jax import lax
from jax.experimental import pallas as pl
from jax.experimental.pallas import tpu as pltpu
from jax.sharding import PartitionSpec as P

BATCH, PAIR = AXES = ("batch", "pair")
HEAD_DIM = 64


EPSILON = 1e-05
NEG_FILL = -1e30


def swapped(value, axis, stride):
    return lax.ppermute(value, axis, [(i, i ^ 1 << stride) for i in range(lax.axis_size(axis))])


def layer_norm(values, gain, shift):
    average = jnp.mean(values, -1, keepdims=True)
    centred = values - average
    variance = jnp.mean(centred * centred, -1, keepdims=True)
    return centred * lax.rsqrt(variance + EPSILON) * gain + shift


def matmul(left, right):
    return jnp.dot(left, right, preferred_element_type=jnp.float32)


def product_back(left, right):
    return lax.dot_general(
        left, right, (((left.ndim - 1,), (1,)), ((), ())), preferred_element_type=jnp.float32
    )


def outer_sum(left, right):
    flat_left = left.reshape(-1, left.shape[-1])
    flat_right = right.reshape(-1, right.shape[-1])
    return lax.dot_general(
        flat_left, flat_right, (((0,), (0,)), ((), ())), preferred_element_type=jnp.float32
    )


def row_total(values):
    return jnp.sum(values.astype(jnp.float32), (0, 1))


def scores_of(query_heads, key_rows, allowed, factor):
    raw = jnp.einsum("sqhd,skhd->shqk", query_heads, key_rows, preferred_element_type=jnp.float32)
    return jnp.where(allowed, raw * factor, NEG_FILL)


def local(
    tokens,
    segment_ids,
    query_weight,
    query_bias,
    key_weight,
    value_weight,
    value_bias,
    out_weight,
    out_bias,
    first_gain,
    first_shift,
    up_weight,
    up_bias,
    down_weight,
    down_bias,
    second_gain,
    second_shift,
    cotangent,
):
    seqs = tokens.shape[0]
    slots = tokens.shape[2]
    width = tokens.shape[3]
    heads = width // HEAD_DIM
    factor = HEAD_DIM ** (-0.5)
    token_rows = tokens.reshape(seqs, slots, width)
    attention_shards = (
        query_weight,
        query_bias,
        key_weight,
        value_weight,
        value_bias,
        out_weight,
        out_bias,
        first_gain,
        first_shift,
    )
    feedforward_shards = (up_weight, up_bias, down_weight, down_bias, second_gain, second_shift)
    attention_full = (
        lax.all_gather(attention_shards[0], AXES, axis=0, tiled=True),
        lax.all_gather(attention_shards[1], AXES, axis=0, tiled=True),
        lax.all_gather(attention_shards[2], AXES, axis=0, tiled=True),
        lax.all_gather(attention_shards[3], AXES, axis=0, tiled=True),
        lax.all_gather(attention_shards[4], AXES, axis=0, tiled=True),
        lax.all_gather(attention_shards[5], AXES, axis=0, tiled=True),
        lax.all_gather(attention_shards[6], AXES, axis=0, tiled=True),
        lax.all_gather(attention_shards[7], AXES, axis=0, tiled=True),
        lax.all_gather(attention_shards[8], AXES, axis=0, tiled=True),
    )
    feedforward_full = (
        lax.all_gather(feedforward_shards[0], AXES, axis=0, tiled=True),
        lax.all_gather(feedforward_shards[1], AXES, axis=0, tiled=True),
        lax.all_gather(feedforward_shards[2], AXES, axis=0, tiled=True),
        lax.all_gather(feedforward_shards[3], AXES, axis=0, tiled=True),
        lax.all_gather(feedforward_shards[4], AXES, axis=0, tiled=True),
        lax.all_gather(feedforward_shards[5], AXES, axis=0, tiled=True),
    )
    (
        query_mat,
        query_vec,
        key_mat,
        value_mat,
        value_vec,
        out_mat,
        out_vec,
        gain_first,
        shift_first,
    ) = attention_full
    up_mat, up_vec, down_mat, down_vec, gain_second, shift_second = feedforward_full
    pair_index = lax.axis_index(PAIR)
    own_ids = lax.dynamic_index_in_dim(segment_ids, pair_index, 1, keepdims=False)
    other_ids = lax.dynamic_index_in_dim(segment_ids, 1 - pair_index, 1, keepdims=False)
    key_ids = jnp.concatenate([own_ids, other_ids], 1)
    allowed = (own_ids[:, :, None] == key_ids[:, None, :])[:, None]
    queries = (matmul(token_rows, query_mat) + query_vec).astype(jnp.bfloat16)
    keys_own = matmul(token_rows, key_mat).astype(jnp.bfloat16)
    values_own = (matmul(token_rows, value_mat) + value_vec).astype(jnp.bfloat16)
    keys_other, values_other = swapped((keys_own, values_own), PAIR, 0)
    head_rows = (seqs, 2 * slots, heads, HEAD_DIM)
    key_rows = jnp.concatenate([keys_own, keys_other], 1).reshape(head_rows)
    value_rows = jnp.concatenate([values_own, values_other], 1).reshape(head_rows)
    query_heads = queries.reshape(seqs, slots, heads, HEAD_DIM)
    scores = scores_of(query_heads, key_rows, allowed, factor)
    row_max = jnp.max(scores, -1, keepdims=True)
    log_total = row_max + jnp.log(jnp.sum(jnp.exp(scores - row_max), -1, keepdims=True))
    probs_low = jnp.exp(scores - log_total).astype(jnp.bfloat16)
    mixed = jnp.einsum("shqk,skhd->sqhd", probs_low, value_rows, preferred_element_type=jnp.float32)
    mixed = mixed.reshape(seqs, slots, width).astype(jnp.bfloat16)
    first_resid = token_rows.astype(jnp.float32) + matmul(mixed, out_mat) + out_vec
    normed, first_pull = jax.vjp(
        layer_norm, first_resid, gain_first.astype(jnp.float32), shift_first.astype(jnp.float32)
    )
    normed_low = normed.astype(jnp.bfloat16)
    pre_hidden = matmul(normed_low, up_mat) + up_vec
    hidden, gelu_pull = jax.vjp(jax.nn.gelu, pre_hidden)
    hidden_low = hidden.astype(jnp.bfloat16)
    second_resid = normed + matmul(hidden_low, down_mat) + down_vec
    final, second_pull = jax.vjp(
        layer_norm, second_resid, gain_second.astype(jnp.float32), shift_second.astype(jnp.float32)
    )
    layer_output = final.astype(jnp.bfloat16).reshape(tokens.shape)
    out_grad = cotangent.reshape(seqs, slots, width).astype(jnp.float32)
    second_grad, gain_second_grad, shift_second_grad = second_pull(out_grad)
    down_in = second_grad.astype(jnp.bfloat16)
    down_weight_grad = outer_sum(hidden_low, down_in)
    down_bias_grad = row_total(down_in)
    hidden_grad = product_back(down_in, down_mat)
    (pre_grad,) = gelu_pull(hidden_grad)
    pre_low = pre_grad.astype(jnp.bfloat16)
    up_weight_grad = outer_sum(normed_low, pre_low)
    up_bias_grad = row_total(pre_low)
    normed_grad = product_back(pre_low, up_mat) + second_grad
    first_grad, gain_first_grad, shift_first_grad = first_pull(normed_grad)
    feedforward_terms = (
        up_weight_grad,
        up_bias_grad,
        down_weight_grad,
        down_bias_grad,
        gain_second_grad,
        shift_second_grad,
    )
    feedforward_parts = (
        lax.psum_scatter(feedforward_terms[0], AXES, scatter_dimension=0, tiled=True),
        lax.psum_scatter(feedforward_terms[1], AXES, scatter_dimension=0, tiled=True),
        lax.psum_scatter(feedforward_terms[2], AXES, scatter_dimension=0, tiled=True),
        lax.psum_scatter(feedforward_terms[3], AXES, scatter_dimension=0, tiled=True),
        lax.psum_scatter(feedforward_terms[4], AXES, scatter_dimension=0, tiled=True),
        lax.psum_scatter(feedforward_terms[5], AXES, scatter_dimension=0, tiled=True),
    )
    branch_low = first_grad.astype(jnp.bfloat16)
    out_weight_grad = outer_sum(mixed, branch_low)
    out_bias_grad = row_total(branch_low)
    mixed_grad = (
        product_back(branch_low, out_mat).astype(jnp.bfloat16).reshape(seqs, slots, heads, HEAD_DIM)
    )
    scores = scores_of(query_heads, key_rows, allowed, factor)
    probs = jnp.exp(scores - log_total)
    probs_low = probs.astype(jnp.bfloat16)
    probs_grad = jnp.einsum(
        "sqhd,skhd->shqk", mixed_grad, value_rows, preferred_element_type=jnp.float32
    )
    delta = jnp.sum(probs * probs_grad, -1, keepdims=True)
    score_grad = (probs * (probs_grad - delta)).astype(jnp.bfloat16)
    query_grad = (
        jnp.einsum("shqk,skhd->sqhd", score_grad, key_rows, preferred_element_type=jnp.float32)
        * factor
    )
    query_grad = query_grad.reshape(seqs, slots, width).astype(jnp.bfloat16)
    key_grad_all = jnp.einsum(
        "shqk,sqhd->skhd", score_grad, query_heads, preferred_element_type=jnp.float32
    )
    key_grad_all = (key_grad_all * factor).reshape(seqs, 2 * slots, width)
    value_grad_all = jnp.einsum(
        "shqk,sqhd->skhd", probs_low, mixed_grad, preferred_element_type=jnp.float32
    )
    value_grad_all = value_grad_all.reshape(seqs, 2 * slots, width)
    keys_back, values_back = (
        swapped(key_grad_all[:, slots:].astype(jnp.bfloat16), PAIR, 0).astype(jnp.float32),
        swapped(value_grad_all[:, slots:].astype(jnp.bfloat16), PAIR, 0).astype(jnp.float32),
    )
    key_grad = (key_grad_all[:, :slots] + keys_back).astype(jnp.bfloat16)
    value_grad = (value_grad_all[:, :slots] + values_back).astype(jnp.bfloat16)
    query_weight_grad = outer_sum(token_rows, query_grad)
    query_bias_grad = row_total(query_grad)
    key_weight_grad = outer_sum(token_rows, key_grad)
    value_weight_grad = outer_sum(token_rows, value_grad)
    value_bias_grad = row_total(value_grad)
    tokens_grad = first_grad + product_back(query_grad, query_mat) + product_back(key_grad, key_mat)
    tokens_grad = tokens_grad + product_back(value_grad, value_mat)
    tokens_gradient = tokens_grad.astype(jnp.bfloat16).reshape(tokens.shape)
    attention_terms = (
        query_weight_grad,
        query_bias_grad,
        key_weight_grad,
        value_weight_grad,
        value_bias_grad,
        out_weight_grad,
        out_bias_grad,
        gain_first_grad,
        shift_first_grad,
    )
    attention_parts = (
        lax.psum_scatter(attention_terms[0], AXES, scatter_dimension=0, tiled=True),
        lax.psum_scatter(attention_terms[1], AXES, scatter_dimension=0, tiled=True),
        lax.psum_scatter(attention_terms[2], AXES, scatter_dimension=0, tiled=True),
        lax.psum_scatter(attention_terms[3], AXES, scatter_dimension=0, tiled=True),
        lax.psum_scatter(attention_terms[4], AXES, scatter_dimension=0, tiled=True),
        lax.psum_scatter(attention_terms[5], AXES, scatter_dimension=0, tiled=True),
        lax.psum_scatter(attention_terms[6], AXES, scatter_dimension=0, tiled=True),
        lax.psum_scatter(attention_terms[7], AXES, scatter_dimension=0, tiled=True),
        lax.psum_scatter(attention_terms[8], AXES, scatter_dimension=0, tiled=True),
    )
    return (
        layer_output,
        tokens_gradient,
        attention_parts[0],
        attention_parts[1],
        attention_parts[2],
        attention_parts[3],
        attention_parts[4],
        attention_parts[5],
        attention_parts[6],
        attention_parts[7],
        attention_parts[8],
        feedforward_parts[0],
        feedforward_parts[1],
        feedforward_parts[2],
        feedforward_parts[3],
        feedforward_parts[4],
        feedforward_parts[5],
    )


F32 = jnp.float32
BF16 = jnp.bfloat16
MESH = pl.DeviceIdType.MESH
CHIPS = 16
LINE = 4
VMEM_BYTES = 63 * 1024 * 1024


def dot(left, right, left_dim, right_dim, precision=None):
    return lax.dot_general(
        left,
        right,
        (((left_dim,), (right_dim,)), ((), ())),
        preferred_element_type=F32,
        precision=precision,
    )


def nn(left, right):
    return dot(left, right, 1, 0)


def nt(left, right):
    return dot(left, right, 1, 1)


def tn(left, right):
    return dot(left, right, 0, 0)


def iota(shape, dim):
    return lax.broadcasted_iota(jnp.int32, shape, dim)


class Refs(dict):
    __getattr__ = dict.__getitem__
    __setattr__ = dict.__setitem__


def column_sum(values):
    return jnp.sum(values, 0, keepdims=True)


def lane_mean(values):
    return jnp.mean(values, -1, keepdims=True)


def block(start, size):
    return pl.ds(pl.multiple_of(start * size, size), size)


def each(count, act):
    def step(s, carry):
        act(s)
        return carry

    lax.fori_loop(0, count, step, 0)


class Links:
    def __init__(self):
        self.b = lax.axis_index(BATCH)
        self.p = lax.axis_index(PAIR)
        self.z = lax.div(self.b, 4)
        x = lax.rem(self.b, 2)
        y = lax.rem(lax.div(self.b, 2), 2)
        self.f = x + self.p * (y - x)
        self.g = y + self.p * (x - y)
        self.near = self.chip(self.z, 1)
        self.far = self.index(self.z, self.f, 1 - self.g)
        third = lax.div(self.z, 3)
        second = lax.div(self.z, 2) - third
        zeroth = 1 - lax.div(self.z + 3, 4)
        self.is_z = (zeroth, 1 - zeroth - second - third, second, third)

    def index(self, z, f, g):
        return 4 * z + (1 + self.p) * f + (2 - self.p) * g

    def chip(self, z, side):
        return self.index(z, self.f + side * (1 - 2 * self.f), self.g)

    def by_z(self, values):
        return sum(flag * value for flag, value in zip(self.is_z, values))

    def column(self):
        return [lax.rem(self.z + step, LINE) for step in (1, 3, 2)]

    def other(self):
        return (self.b, 1 - self.p)

    def greet(self):
        semaphore = pltpu.get_barrier_semaphore()
        partners = [self.chip(z, 0) for z in self.column()] + [self.near, self.far]
        for device in [(chip, self.p) for chip in partners] + [self.other()]:
            pl.semaphore_signal(semaphore, inc=1, device_id=device, device_id_type=MESH)

    def meet(self):
        pl.semaphore_wait(pltpu.get_barrier_semaphore(), 6)


class Gather:
    ARRIVE = ((1, 2, 3), (2, 0, 3), (3, 1, 0), (2, 1, 0))
    FROM_FAR = CHIPS
    ARRIVALS = CHIPS + 1

    def __init__(self, links, ref, send, recv, near_first=False):
        self.links, self.ref, self.send, self.recv = links, ref, send, recv
        self.size = ref.shape[0] // CHIPS
        self.near_first = near_first

    def copy(self, rows, chip, arrival):
        part = self.ref.at[rows]
        return pltpu.make_async_remote_copy(
            src_ref=part,
            dst_ref=part,
            send_sem=self.send,
            recv_sem=self.recv.at[arrival],
            device_id=(chip, self.links.p),
            device_id_type=MESH,
        )

    def wait(self, shard):
        self.copy(block(shard, self.size), self.links.far, shard).wait_recv()

    def to_far(self, z, side):
        shard = self.links.chip(z, side)
        self.copy(block(shard, self.size), self.links.far, self.FROM_FAR).start()

    def to_near(self, z):
        shard = self.links.chip(z, 0)
        self.copy(block(shard, self.size), self.links.near, shard).start()

    def to_column(self, z, side):
        k = self.links
        shard = k.chip(k.z, side)
        self.copy(block(shard, self.size), k.chip(z, 0), shard).start()

    def own(self):
        k = self.links
        self.to_near(k.z)
        self.to_far(k.z, 0)
        for z in k.column():
            self.to_column(z, 0)

    def near(self, turn):
        k = self.links
        z = k.z if turn == 0 else k.by_z([order[turn - 1] for order in self.ARRIVE])
        self.wait(k.chip(z, 1))
        if self.near_first and turn == 0:
            for other in k.column():
                self.to_column(other, 1)
        self.to_far(z, 1)

    def along(self, turn):
        k = self.links
        z = k.by_z([order[turn] for order in self.ARRIVE])
        self.wait(k.chip(z, 0))
        if not self.near_first:
            self.to_near(z)
        self.to_far(z, 0)

    def steps(self):
        steps = [self.own, lambda: self.near(0)]
        for turn in range(LINE - 1):
            steps.append(lambda turn=turn: self.along(turn))
            steps.append(lambda turn=turn: self.near(turn + 1))
        return steps

    def finish(self):
        self.copy(slice(0, 8 * self.size), self.links.far, self.FROM_FAR).wait_recv()

    def drain(self):
        self.copy(slice(0, 15 * self.size), self.links.far, self.FROM_FAR).wait_send()


class Reduce:
    LEAVE = ((3, 2, 1), (3, 2, 0), (0, 1, 3), (0, 1, 2))
    SLOTS = 15
    ARRIVALS = 10

    def __init__(self, links, grad, land, send, recv, near_first=False):
        self.links, self.grad, self.land = links, grad, land
        self.send, self.recv = send, recv
        self.size = grad.shape[0] // CHIPS
        self.near_first = near_first

    def rows(self, z, f, count=1, far=0):
        k = self.links
        g = k.g + far * (1 - 2 * k.g)
        at = 4 * z + 2 * g + f
        return pl.ds(pl.multiple_of(at * self.size, self.size), count * self.size)

    def slots(self, slot, count=1):
        start = slot * self.size
        return pl.ds(start if isinstance(slot, int) else pl.multiple_of(start, self.size), count * self.size)

    def copy(self, rows, slots, chip, arrival):
        return pltpu.make_async_remote_copy(
            src_ref=self.grad.at[rows],
            dst_ref=self.land.at[slots],
            send_sem=self.send,
            recv_sem=self.recv.at[arrival],
            device_id=(chip, self.links.p),
            device_id_type=MESH,
        )

    def wait(self, arrival, count):
        rows = slice(0, count * self.size)
        self.copy(rows, rows, self.links.far, arrival).wait_recv()

    def wait_far(self, z):
        self.wait(z, 2)

    def wait_near(self, z):
        self.wait(4 if self.near_first else 4 + z, 1)

    def wait_column(self, side):
        self.wait(8 + side, 3)

    def far_slot(self, z, f):
        return 2 * z + f

    def near_slot(self, z):
        return 8 if self.near_first else 8 + z

    def column_slot(self, step, side):
        return (9 + 3 * side if self.near_first else 12) + step - 1

    def column_slots(self, side):
        return [self.column_slot(step, side) for step in range(1, LINE)]

    def total(self, rows, slots):
        total = self.grad[rows].astype(F32)
        for slot in slots:
            total = total + self.land[self.slots(slot)].astype(F32)
        return total

    def add_on(self, rows, slots):
        self.grad[rows] = self.total(rows, slots).astype(self.grad.dtype)

    def far(self, z):
        self.copy(self.rows(z, 0, 2, 1), self.slots(self.far_slot(z, 0), 2), self.links.far, z).start()

    def near(self, z):
        k = self.links
        more = []
        self.wait_far(z)
        if self.near_first:
            self.wait_column(1)
            more = self.column_slots(1)
        rows = self.rows(z, 1 - k.f)
        self.add_on(rows, [self.far_slot(z, 1 - k.f)] + more)
        arrival = 4 if self.near_first else 4 + z
        self.copy(rows, self.slots(self.near_slot(z)), k.near, arrival).start()

    def along(self, turn, side):
        k = self.links
        z = k.by_z([order[turn] for order in self.LEAVE])
        f = k.f + side * (1 - 2 * k.f)
        rows, more = self.rows(z, f), []
        if not self.near_first:
            self.wait_near(z)
            more = [self.near_slot(z)]
        elif side == 1:
            self.wait_far(z)
        self.add_on(rows, [self.far_slot(z, f)] + more)
        slot = self.column_slot(lax.rem(k.z - z + LINE, LINE), side)
        self.copy(rows, self.slots(slot), k.chip(z, 0), 8 + side).start()

    def steps(self):
        steps = [lambda z=z: self.far(z) for z in range(LINE)]
        near = [lambda z=z: self.near(z) for z in range(LINE)]
        sides = (1, 0) if self.near_first else (0,)
        along = [
            lambda turn=turn, side=side: self.along(turn, side)
            for turn in range(LINE - 1)
            for side in sides
        ]
        if self.near_first:
            return steps + along + [lambda: self.near(self.links.z)]
        return steps + near + along

    def result(self):
        k = self.links
        self.wait_near(k.z)
        self.wait_column(0)
        slots = [self.far_slot(k.z, k.f), self.near_slot(k.z)]
        return self.total(self.rows(k.z, k.f), slots + self.column_slots(0))

    def drain(self):
        rows = slice(0, 15 * self.size)
        self.copy(rows, rows, self.links.far, 0).wait_send()


class Steps:
    def __init__(self, seqs, course, transfers):
        lines = [iter(steps) for steps in transfers]
        self.seqs, self.count = seqs, 0
        self.waiting = {place: [next(lines[n]) for n in order] for place, order in course.items()}
        assert all(next(line, None) is None for line in lines)

    def run(self):
        for step in self.waiting.pop(self.count, ()):
            step()
        self.count += 1

    def once(self, act):
        self.run()
        act()

    def loop(self, act, first=None, count=None):
        count = self.seqs if count is None else count
        self.run()
        if first is not None:
            first()
        later = []
        for s in range(1, count):
            later.append((s, self.waiting.pop(self.count, ())))
            self.count += 1

        def turn(s):
            for at, steps in later:
                if steps:

                    @pl.when(s == at)
                    def _():
                        for step in steps:
                            step()

            act(s)

        each(count, turn)


def laying(blocks, cols):
    size = cols // blocks
    pick = iota((128, cols), 0) == lax.rem(iota((128, cols), 1), size)
    return pick, lax.div(iota((blocks, cols), 1), size) == iota((blocks, cols), 0)


def core_order(chip, p):
    low = lax.rem(chip, 4)
    step = (low == 1).astype(jnp.int32) - (low == 2).astype(jnp.int32)
    return chip + p * step


def vector_rows(shape, dim, vector, p):
    device, row = iota(shape, dim), iota(shape, 1 - dim)
    return row == 16 * core_order(lax.div(device, 2), p) + 2 * vector + lax.rem(device, 2)


def unit_rows(shape, dim, which, p):
    return iota(shape, 1 - dim) == 16 * core_order(iota(shape, dim), p) + which


def unpack_small(r, p):
    rows = CHIPS * 16
    flat = r.small_all[...].astype(BF16)
    pick, place = laying(2 * CHIPS, r.vec.shape[1])
    for vector in range(8):
        chosen = nn(vector_rows((2 * CHIPS, rows), 0, vector, 0).astype(BF16), flat[:, :128])
        laid = nn(chosen.astype(BF16), pick.astype(BF16))
        r.vec[vector : vector + 1] = column_sum(jnp.where(place, laid, 0.0))
    pick, place = laying(CHIPS, r.upb.shape[1])
    chosen = nn(unit_rows((CHIPS, rows), 0, p, 0).astype(BF16), flat[:, 128:])
    laid = nn(chosen.astype(BF16), pick.astype(BF16))
    r.upb[...] = column_sum(jnp.where(place, laid, 0.0))


def pack_small(r, p):
    rows, width = CHIPS * 16, r.gvec.shape[1]
    for vector in range(2, 8):
        r.gvec[vector : vector + 1] = column_sum(r.gacc[8 * vector : 8 * vector + 8])
    row = iota((rows, 1), 0)
    device = 2 * core_order(lax.div(row, 16), p) + lax.rem(row, 2)
    chosen = lax.div(lax.rem(iota((rows, 8), 0), 16), 2) == iota((rows, 8), 1)
    spread = nn(chosen.astype(BF16), r.gvec[...].astype(BF16))
    place = device == lax.div(iota((1, width), 1), width // (2 * CHIPS))
    pick, _ = laying(2 * CHIPS, width)
    narrow = nt(jnp.where(place, spread, 0.0).astype(BF16), pick.astype(BF16))
    pick, place = laying(CHIPS, r.upg.shape[1])
    blocks = nt(jnp.where(place, r.upg[...], 0.0).astype(BF16), pick.astype(BF16))
    wide = nn(unit_rows((rows, CHIPS), 1, p, p).astype(BF16), blocks.astype(BF16))
    low = jnp.concatenate([narrow, wide], 1).astype(BF16)
    space = r.gq2.shape[0] // CHIPS
    for chip in range(CHIPS):
        r.gq2[space * chip + space - 16 : space * chip + space] = low[16 * chip : 16 * chip + 16]


def half_lanes(values, half, factor=None):
    mask = lax.div(iota((1, values.shape[1]), 1), HEAD_DIM) == half
    kept = jnp.where(mask, values, jnp.zeros_like(values))
    return kept if factor is None else kept * jnp.asarray(factor, values.dtype)


def normalize(values):
    centred = values - lane_mean(values)
    scale = lax.rsqrt(lane_mean(centred * centred) + EPSILON)
    return centred * scale, scale


def norm_back(grad, hat, scale):
    return scale * (grad - lane_mean(grad) - hat * lane_mean(grad * hat))


def gelu_both(value):
    square = value * value
    root = 0.7978845608028654
    inner = value * (root + root * 0.044715 * square)
    bent = 0.5 * jnp.tanh(inner) + 0.5
    slope = root + 3.0 * root * 0.044715 * square
    return value * bent, bent + 2.0 * value * slope * (bent - bent * bent)


UP_LANES = (slice(0, 768), slice(768, 1536),)
UP_NEAR_FIRST = (False, True)
DOWN_LANES = (slice(0, 512), slice(512, 768),)
DOWN_NEAR_FIRST = (False, True)
UP_SUM_LANES = (slice(0, 768), slice(768, 1536),)
UP_SUM_NEAR_FIRST = (True, False)
DOWN_SUM_LANES = (slice(0, 512), slice(512, 768),)
DOWN_SUM_NEAR_FIRST = (False, True)
UNITS = (
    ("sa",),
    ("sb",),
    ("unpack",),
    ("att", 0),
    ("att", 1),
    ("att", 2),
    ("wo",),
    ("out",),
    ("up", 0),
    ("up", 1),
    ("do", 0),
    ("do", 1),
    ("dw", 0),
    ("dw", 1),
    ("ln2",),
    ("ge",),
    ("ddw",),
    ("gd", 0),
    ("gd", 1),
    ("gd", 2),
    ("gd", 3),
    ("hb",),
    ("gu", 0),
    ("gu", 1),
    ("gu", 2),
    ("gu", 3),
    ("no",),
    ("nw",),
    ("ln1",),
    ("mb",),
    ("go",),
    ("ab", 0),
    ("gq", 0),
    ("ab", 1),
    ("gq", 1),
    ("ab", 2),
    ("ps",),
    ("gq", 2),
    ("to",),
    ("tw",),
    ("te",),
    ("end",),
)
COURSE = {
    0: (6,),
    1: (0, 3, 1,),
    2: (2, 6, 4, 6, 4, 5, 6, 6, 0, 0, 3, 3, 1, 0, 0, 2, 7, 1, 3, 3, 2, 1, 1, 0, 3, 0, 2, 2, 1, 1, 0, 3, 2, 1, 2, 4,),
    3: (6,),
    4: (2, 3,),
    5: (4, 4,),
    6: (5,),
    8: (7, 7,),
    9: (5,),
    10: (4, 4,),
    11: (6,),
    13: (5,),
    15: (4,),
    17: (5, 5, 5,),
    18: (5,),
    20: (7, 7, 6,),
    22: (7, 7, 7,),
    43: (8,),
    45: (9, 9, 9,),
    46: (9,),
    49: (8,),
    52: (10,),
    54: (10, 10, 10, 9,),
    55: (9, 9, 9, 9, 9,),
    56: (11, 11, 11,),
    63: (11,),
    64: (10, 10, 10, 10, 10, 10,),
    66: (11,),
    67: (8,),
    69: (11, 11, 11, 8,),
    72: (12, 11, 11, 8, 8, 8, 8,),
    74: (12, 11,),
    76: (12, 12, 12, 8, 8, 8,),
    78: (13,),
    80: (12,),
    81: (12, 11, 12,),
    83: (13, 13, 13, 13, 14, 14,),
    84: (12, 12, 12,),
    85: (13, 13, 13, 14, 14, 14, 10, 13, 13, 14, 14, 13, 14, 8,),
    88: (12,),
    89: (9, 14,),
    90: (14, 14, 10,),
    91: (13, 9, 14,),
}


class Layer:
    def __init__(self, r, p):
        self.r, self.p = r, p
        self.slots = r.tokens.shape[2]
        self.width = r.tokens.shape[3]
        self.half = self.width // 2
        self.units = r.wup.shape[1]

    def rows(self, s):
        return block(s, 2 * self.slots)

    def side(self, s, side):
        return block(2 * s + side, self.slots)

    def own_lanes(self, pair):
        return pl.ds(pl.multiple_of(self.p * self.half + 128 * pair, 128), 128)

    def project(self, s, pair):
        r = self.r
        result = nn(r.x_all[self.rows(s)], r.wq[pair][...])
        lanes = self.own_lanes(pair)
        query = result[:, :128] + r.vec[0:1, lanes]
        value = result[:, 256:] + r.vec[1:2, lanes]
        r.qkv[pair, self.rows(s)] = jnp.concatenate([query, result[:, 128:256], value], 1).astype(BF16)

    def mask(self, s):
        r = self.r
        rows, space = r.fill.shape[1:]
        rest = jnp.zeros((1, space - rows), F32)
        ids = [r.segment_ids[s, half : half + 1].astype(F32) for half in range(2)]
        across = jnp.broadcast_to(jnp.concatenate(ids + [rest], 1), (space, space))
        r.fill[s] = jnp.where(across.T[:rows] == across[:rows], 0.0, NEG_FILL).astype(BF16)

    def heads(self, s, pair):
        held = self.r.qkv[pair, self.rows(s)]
        return held[:, :128], held[:, 128:256], held[:, 256:]

    def widened(self, values):
        rest = self.r.fill.shape[2] - values.shape[0]
        return jnp.concatenate([values, jnp.zeros((rest, values.shape[1]), values.dtype)], 0)

    def both_halves(self, values, factor=None, widen=False):
        parts = [half_lanes(values, half, factor) for half in range(2)]
        return jnp.concatenate([self.widened(part) if widen else part for part in parts], 0)

    def attend(self, s, pair):
        r = self.r
        rows, space = r.fill.shape[1:]
        queries, keys, values = self.heads(s, pair)
        values_t = values.T
        r.probs_grad[...] = nt(self.both_halves(keys, HEAD_DIM**-0.5), self.widened(queries))
        parts = []
        for half in range(2):
            top, total = NEG_FILL, 0.0
            for at in range(0, rows, 64):
                here = slice(rows * half + at, rows * half + at + 64)
                scores = r.probs_grad[here] + r.fill[s, at : at + 64].astype(F32)
                r.probs_grad[here] = scores
                top = jnp.maximum(top, jnp.max(scores.reshape(8, 8, space), 0))
            top = jnp.max(top, 0, keepdims=True)
            for at in range(0, rows, 64):
                here = slice(rows * half + at, rows * half + at + 64)
                raised = jnp.exp(r.probs_grad[here] - top)
                r.probs_grad[here] = raised
                total = total + jnp.sum(raised.reshape(8, 8, space), 0)
            share = 1.0 / column_sum(total)
            lanes = slice(space * half, space * half + space)
            for at in range(0, rows, 64):
                here = slice(rows * half + at, rows * half + at + 64)
                r.pt[3 * s + pair, at : at + 64, lanes] = (r.probs_grad[here] * share).astype(BF16)
            head = values_t[HEAD_DIM * half : HEAD_DIM * half + HEAD_DIM]
            parts.append(nn(head, r.pt[3 * s + pair, :, lanes]))
        mixed = jnp.concatenate(parts, 0).T[:rows]
        r.mixed[self.rows(s), self.own_lanes(pair)] = mixed.astype(BF16)

    def out_project(self, s):
        r, p = self.r, self.p
        mixed = r.mixed[self.side(s, p)]
        sides = [nn(mixed, r.wo[side]) for side in range(2)]
        r.product[: self.slots] = jnp.concatenate(sides, 1)
        for at, rows in self.pieces(s):
            resid = r.x_all[rows].astype(F32) + r.product[at] + r.vec[2:3]
            hat, scale = normalize(resid)
            r.xhat[s, at] = hat
            r.rstd[s, at] = jnp.broadcast_to(scale, (scale.shape[0], 128))
            r.n_all[rows] = (hat * r.vec[3:4] + r.vec[4:5]).astype(BF16)

    def feed_up(self, s, lanes):
        r = self.r
        r.product[...] = nn(r.n_all[self.rows(s)], r.wup[:, lanes])
        for at, rows in self.strips(s):
            hidden, slope = gelu_both(r.product[at] + r.upb[:, lanes])
            r.hidden[rows, lanes] = hidden.astype(BF16)
            r.slope[rows, lanes] = slope.astype(BF16)

    def two(self, ref, n, side):
        return jnp.concatenate([ref[self.side(2 * n + s, side)] for s in range(2)], 0)

    def by_two(self, rows):
        return rows.reshape(2, self.slots, rows.shape[1])

    def feed_down(self, n, side, lanes):
        return self.by_two(nn(self.two(self.r.hidden, n, side), self.r.wdown[:, lanes]))

    def pieces(self, s):
        for at in range(0, self.slots, 32):
            start = (2 * s + self.p) * self.slots + at
            yield slice(at, at + 32), pl.ds(pl.multiple_of(start, 32), 32)

    def strips(self, s):
        for at in range(0, 2 * self.slots, 32):
            start = 2 * s * self.slots + at
            yield slice(at, at + 32), pl.ds(pl.multiple_of(start, 32), 32)

    def add_rows(self, vector, values):
        folded = values.reshape(values.shape[0] // 8, 8, values.shape[1])
        self.r.gacc[8 * vector : 8 * vector + 8] += jnp.sum(folded, 0)

    def finish_norm(self, s):
        r = self.r
        for at, rows in self.pieces(s):
            normed = r.xhat[s, at] * r.vec[3:4] + r.vec[4:5]
            resid = normed + r.part_own[s, at] + r.part_in[s, at].astype(F32) + r.vec[5:6]
            hat, scale = normalize(resid)
            r.final[s, at] = (hat * r.vec[6:7] + r.vec[7:8]).astype(BF16)
            grad = r.out_grad[s, at].astype(F32)
            self.add_rows(6, grad * hat)
            self.add_rows(7, grad)
            back = norm_back(grad * r.vec[6:7], hat, scale)
            r.resid_grad[s, at] = back
            low = back.astype(BF16)
            r.dd_all[rows] = low
            self.add_rows(5, low.astype(F32))

    def put_blocks(self, ref, first, result, size):
        space = ref.shape[0] // CHIPS
        low = result.astype(BF16)
        for n in range(result.shape[0] // size):
            chip = first + n
            step = (0, 1, -1, 0)[chip % 4]
            at = chip * space
            rows = pl.ds(pl.multiple_of(at + self.p * step * space, 16), size) if step else slice(at, at + size)
            ref[rows] = low[n * size : n * size + size]

    def first_down_weight_grad(self):
        r = self.r
        most = slice(0, r.hidden.shape[0] - 2 * self.slots)
        r.first_sum[...] = tn(r.hidden[most, : self.half], r.dd_all[most])

    def down_weight_grad(self, m):
        r = self.r
        at = slice(self.half * m, self.half * m + self.half)
        if m == 0:
            last = slice(r.hidden.shape[0] - 2 * self.slots, r.hidden.shape[0])
            total = r.first_sum[...] + tn(r.hidden[last, at], r.dd_all[last])
        else:
            total = tn(r.hidden[:, at], r.dd_all[...])
        self.put_blocks(r.gd, 4 * m, total, self.half // 4)

    def hidden_back(self, s):
        r = self.r
        grads = r.dd_all[self.rows(s)]
        for start in range(0, self.units, self.width):
            lanes = slice(start, start + self.width)
            r.product[...] = nt(grads, r.wdown[lanes])
            total = 0.0
            for at, rows in self.strips(s):
                low = (r.product[at] * r.slope[rows, lanes].astype(F32)).astype(BF16)
                r.slope[rows, lanes] = low
                total = total + jnp.sum(low.astype(F32).reshape(4, 8, self.width), 0)
            r.upg[:, lanes] += column_sum(total)

    def up_weight_grad(self, m, n):
        r = self.r
        at = slice(self.half * m, self.half * m + self.half)
        lanes = slice(self.width * n, self.width * n + self.width)
        self.put_blocks(r.gu.at[:, lanes], 8 * m, tn(r.n_all[:, at], r.slope[:, lanes]), self.half // 8)

    def normed_back(self, n, side):
        return self.by_two(nt(self.two(self.r.slope, n, side), self.r.wup[...]))

    def first_norm_back(self, s):
        r = self.r
        for at, rows in self.pieces(s):
            grad = r.part_own[s, at] + r.part_in[s, at].astype(F32) + r.resid_grad[s, at]
            hat = r.xhat[s, at]
            self.add_rows(3, grad * hat)
            self.add_rows(4, grad)
            back = norm_back(grad * r.vec[3:4], hat, r.rstd[s, at, 0:1])
            r.resid_grad[s, at] = back
            low = back.astype(BF16)
            r.n_all[rows] = low
            self.add_rows(2, low.astype(F32))

    def out_weight_grad(self):
        r = self.r
        own = block(self.p, self.half)
        right = r.n_all[:, own]
        for m in range(2):
            at = slice(self.half * m, self.half * m + self.half)
            self.put_blocks(r.go, 8 * m, tn(r.mixed[:, at], right), self.half // 8)

    def mixed_back(self, s):
        r = self.r
        grads = r.n_all[self.rows(s)]
        own = block(self.p, self.half)
        total = nt(grads[:, : self.half], r.wo[0, own]) + nt(grads[:, self.half :], r.wo[1, own])
        r.dm[self.rows(s)] = total.astype(BF16)

    def attend_back(self, s, pair):
        r = self.r
        scale = HEAD_DIM**-0.5
        unit = 3 * s + pair
        rows, space = r.fill.shape[1:]
        queries, keys, values = self.heads(s, pair)
        grads = r.dm[self.rows(s), 128 * pair : 128 * pair + 128]
        r.probs_grad[...] = nt(self.both_halves(values), self.widened(grads))
        for half in range(2):
            lanes = slice(space * half, space * half + space)
            total = 0.0
            for at in range(0, rows, 64):
                grad = r.probs_grad[rows * half + at : rows * half + at + 64]
                product = r.pt[unit, at : at + 64, lanes].astype(F32) * grad
                total = total + jnp.sum(product.reshape(8, 8, space), 0)
            delta = column_sum(total)
            for at in range(0, rows, 64):
                grad = r.probs_grad[rows * half + at : rows * half + at + 64]
                probs = r.pt[unit, at : at + 64, lanes].astype(F32)
                r.score_grad[at : at + 64, lanes] = (probs * (grad - delta)).astype(BF16)
        key_grad = nn(r.score_grad[...], self.both_halves(queries, scale, True))
        keys_t = keys.T * jnp.asarray(scale, BF16)
        query_parts = []
        for half in range(2):
            at = HEAD_DIM * half
            query_parts.append(
                nn(keys_t[at : at + HEAD_DIM], r.score_grad[:, space * half : space * half + space])
            )
        query_grad = jnp.concatenate(query_parts, 0).T[:rows]
        r.dqkv[pair][self.rows(s), :256] = jnp.concatenate([query_grad, key_grad], 1).astype(BF16)
        for other in ((0,), (1, 2), ())[pair]:
            grads = r.dm[self.rows(s), 128 * other : 128 * other + 128]
            value_grad = nn(r.pt[3 * s + other], self.both_halves(grads, None, True))
            r.dqkv[other][self.rows(s), 256:] = value_grad.astype(BF16)

    def project_weight_grad(self, pair):
        r = self.r
        target, right = (r.gq0, r.gq1, r.gq2)[pair], r.dqkv[pair][...]
        if pair == 1:
            right = jnp.concatenate([right, r.dqkv[2][:, 256:]], 1)
        if pair == 2:
            right = right[:, :256]
        for m in range(2):
            at = slice(self.half * m, self.half * m + self.half)
            self.put_blocks(target, 8 * m, tn(r.x_all[:, at], right), self.half // 8)

    def project_bias_grad(self, pair):
        r = self.r
        right = r.dqkv[pair]
        lanes = self.own_lanes(pair)
        r.gvec[0:1, lanes] = column_sum(right[:, :128].astype(F32))
        r.gvec[1:2, lanes] = column_sum(right[:, 256:].astype(F32))

    def token_back(self, n, side):
        r = self.r
        total = 0.0
        for pair in range(3):
            total = total + nt(self.two(r.dqkv[pair], n, side), r.wq[pair][...])
        return self.by_two(total)


def ordered(size):
    column = iota((1, 8 * size), 1)
    within = lax.rem(column, 4 * size)
    source = 2 * size * lax.div(within, size) + size * lax.div(column, 4 * size) + lax.rem(within, size)
    return iota((8 * size, 8 * size), 0) == source


def place_small(r, p):
    r.small_in[...] = jnp.zeros_like(r.small_in)
    rows = [(row, 0, vector) for row, vector in enumerate(r.vectors)] + [(0, 128, r.up_bias)]
    for row, lane, vector in rows:
        count = vector.shape[0]
        values = vector[...].reshape(1, count).astype(F32)
        for core in range(2):

            @pl.when(p == core)
            def _():
                at = 2 * row + core
                r.small_in[at : at + 1, lane : lane + count] = values


def pack_square(r, half, piece):
    at = half * piece
    for core in range(2):
        if piece == 3:
            r.stack[core, :, at : at + half] = r.out_weight[:, half * core : half * core + half].astype(F32)
            continue
        for part, weight in enumerate((r.query_weight, r.key_weight, r.value_weight)):
            lane = half * core + 128 * piece
            r.stack[core, :, at + 128 * part : at + 128 * part + 128] = weight[:, lane : lane + 128].astype(F32)


def pack_up(r, half, size):
    rows = r.up_weight.shape[0]
    groups = [r.up_weight[:, 8 * size * group : 8 * size * group + 8 * size] for group in range(CHIPS // 4)]
    stacked = jnp.concatenate([group.astype(F32) for group in groups], 0).astype(BF16)
    ordered_units = nn(stacked, ordered(size).astype(BF16))
    for group in range(CHIPS // 4):
        to = 4 * half + 4 * size * group
        for core in range(2):
            r.stack[core, :, to : to + 4 * size] = ordered_units[
                rows * group : rows * group + rows, 4 * size * core : 4 * size * core + 4 * size
            ]


def layer_kernel(r):
    k = Links()
    p = k.p
    seqs = r.tokens.shape[0]
    layer = Layer(r, p)
    half = layer.half
    width = layer.width
    per = r.stack.shape[1]
    size = r.down_weight.shape[0]
    pack = r.stack.shape[2]
    def to_other(src, dst, group, arrival):
        return pltpu.make_async_remote_copy(
            src_ref=src,
            dst_ref=dst,
            send_sem=r.pair_send.at[group],
            recv_sem=r.pair_recv.at[arrival],
            device_id=k.other(),
            device_id_type=MESH,
        )

    def local(src, dst, which):
        return pltpu.make_async_copy(src, dst, r.local_done.at[which])

    def trade_own(ref, group, base):
        return lambda s: to_other(ref.at[layer.side(s, p)], ref.at[layer.side(s, p)], group, base + s)

    def trade_slot(src, dst, group, base):
        return lambda s: to_other(src.at[s], dst.at[s], group, base + s)

    def sent(group):
        to_other(r.part_out, r.part_in, group, 0).wait_send()

    small_swap = to_other(r.small_in, r.small_theirs, 0, 0)
    share = to_other(r.wo.at[p], r.wo.at[p], 1, 1)
    sums_swap = to_other(r.sum_small, r.sum_theirs, 2, 2)
    inputs = lambda s: to_other(r.tokens.at[s, 0], r.x_all.at[layer.side(s, p)], 3, 3)
    normed = trade_own(r.n_all, 4, 4)
    down_part = trade_slot(r.part_out, r.part_in, 5, 4 + seqs)
    down_grad = trade_own(r.dd_all, 6, 4 + 2 * seqs)
    normed_part = trade_slot(r.part_out, r.part_in, 7, 4 + 3 * seqs)
    branch = trade_own(r.n_all, 8, 4 + 4 * seqs)
    token_part = trade_slot(r.part_out, r.part_in, 9, 4 + 5 * seqs)

    def mixed(s, pair):
        part = r.mixed.at[layer.rows(s), layer.own_lanes(pair)]
        return to_other(part, part, 10, 4 + 6 * seqs + s)

    def mixed_in(s):
        part = r.mixed.at[layer.rows(s), block(p, half)]
        return to_other(part, part, 10, 4 + 6 * seqs + s)

    def pack_swap(lanes):
        return to_other(r.sum_pack.at[block(1 - p, per), lanes], r.out_pack.at[p, :, lanes], 11, 4 + 7 * seqs)

    pieces = [slice(0, half), slice(half, 2 * half), slice(2 * half, 4 * half)]
    pieces += [slice(4 * half + lanes.start, 4 * half + lanes.stop) for lanes in UP_LANES]

    def piece_swap(n):
        lanes = pieces[n]
        return to_other(
            r.stack.at[1 - p, :, lanes], r.sum_pack.at[block(p, per), lanes], 12, 5 + 7 * seqs + n
        )

    def place_piece(n, target):
        lanes = pieces[n]

        def act():
            piece_swap(n).wait_recv()
            r.sum_pack[block(p, per), lanes] = r.stack[p, :, lanes]
            target[block(k.b, 2 * per)] = r.sum_pack[:, lanes].astype(BF16)

        return act

    def gather(n, ref, near_first=False):
        return Gather(k, ref, r.gather_send.at[n], r.gather_recv.at[n], near_first)

    def reduce(n, grad, land, near_first=False):
        return Reduce(k, grad, land, r.reduce_send.at[n], r.reduce_recv.at[n], near_first)

    small = gather(0, r.small_all)
    heads = [gather(1 + pair, ref) for pair, ref in enumerate((r.wq0, r.wq1, r.wq2o))]
    ups = [gather(4 + n, r.wup.at[:, lanes], first) for n, (lanes, first) in enumerate(zip(UP_LANES, UP_NEAR_FIRST))]
    downs = [
        gather(6 + n, r.wdown.at[:, lanes], first)
        for n, (lanes, first) in enumerate(zip(DOWN_LANES, DOWN_NEAR_FIRST))
    ]
    gathers = [small] + heads + ups + downs
    down_sums = [
        reduce(n, r.gd.at[:, lanes], land, first)
        for n, (lanes, land, first) in enumerate(zip(DOWN_SUM_LANES, r.land_d, DOWN_SUM_NEAR_FIRST))
    ]
    up_sums = [
        reduce(2 + n, r.gu.at[:, lanes], land, first)
        for n, (lanes, land, first) in enumerate(zip(UP_SUM_LANES, r.land_u, UP_SUM_NEAR_FIRST))
    ]
    out_sum = reduce(4, r.goq, r.land_oq)
    head_sums = [reduce(5, r.gq1, r.land_q1), reduce(6, r.gq2, r.land_q2)]
    reduces = down_sums + up_sums + [out_sum] + head_sums

    def store(one, lanes):
        def act():
            r.sum_pack[:, lanes] = one.result()
            pack_swap(lanes).start()
            r.out_pack[p, :, lanes] = r.sum_pack[block(p, per), lanes]

        return act

    def store_down(one, lanes):
        def act():
            total = one.result()
            for group in range(size // per):
                to = slice(width * group + lanes.start, width * group + lanes.stop)
                r.out_pack[2, :, to] = total[per * group : per * group + per]

        return act

    def store_last():
        total = head_sums[1].result()
        r.sum_pack[:, packs[-1]] = total[: 2 * per]
        pack_swap(packs[-1]).start()
        r.sum_small[...] = total[2 * per :]
        sums_swap.start()
        r.out_pack[p, :, packs[-1]] = r.sum_pack[block(p, per), packs[-1]]

    packs = [slice(4 * half + lanes.start, 4 * half + lanes.stop) for lanes in UP_SUM_LANES]
    packs += [slice(0, 2 * half), slice(2 * half, 3 * half + 128), slice(3 * half + 128, 4 * half)]
    stores = [store_down(one, lanes) for one, lanes in zip(down_sums, DOWN_SUM_LANES)]
    stores += [store(one, lanes) for one, lanes in zip(up_sums + [out_sum] + head_sums[:1], packs)]
    stores.append(store_last)

    def place_small_rows():
        small_swap.wait_recv()
        r.small_all[block(k.b, 16)] = r.small_in[...] + r.small_theirs[...]

    def finish_out():
        heads[2].finish()
        r.wo[p] = r.wq2o[:, half:]
        share.start()

    starts = [place_small_rows]
    starts += [place_piece(n, target) for n, target in enumerate((r.wq0, r.wq1, r.wq2o))]
    starts += [place_piece(3 + n, r.wup.at[:, lanes]) for n, lanes in enumerate(UP_LANES)]
    spreads = [one.steps() for one in gathers]
    for steps_of, start in zip(spreads, starts):
        steps_of[0] = lambda start=start, own=steps_of[0]: (start(), own())
    sums = [one.steps() + [last] for one, last in zip(reduces, stores)]
    steps = Steps(seqs, COURSE, spreads + sums)

    k.greet()
    each(seqs, lambda s: local(r.tokens.at[s, 0], r.x_all.at[layer.side(s, p)], 0).start())
    local(r.cotangent.at[:, 0], r.out_grad, 1).start()
    r.wdown[block(k.b, size)] = r.down_weight[...]
    pack_square(r, half, 0)
    place_small(r, p)
    k.meet()
    piece_swap(0).start()
    small_swap.start()

    def wait_once(*copies):
        fresh = [copy for copy in copies if copy not in waited]
        waited.extend(fresh)
        return lambda s: [copy(s).wait_recv() for copy in fresh]

    waited = []

    def pack_heads():
        def act():
            pack_square(r, half, 1)
            piece_swap(1).start()
            pack_square(r, half, 2)
            pack_square(r, half, 3)
            piece_swap(2).start()

        steps.once(act)

    def pack_rest():
        def act():
            pack_up(r, half, size)
            for n in range(3, len(pieces)):
                piece_swap(n).start()
            each(seqs, lambda s: inputs(s).start())
            for sums in (r.gvec, r.gacc, r.upg):
                sums[...] = jnp.zeros_like(sums)

        steps.once(act)

    def unpack():
        def act():
            each(seqs, layer.mask)
            small.finish()
            unpack_small(r, p)
            to_other(r.part_out, r.part_in, 3, 3).wait_recv()
            local(r.part_out, r.part_in, 0).wait()

        steps.once(act)

    def attention(pair):
        def act(s):
            layer.project(s, pair)
            layer.attend(s, pair)
            mixed(s, pair).start()

        steps.loop(act, heads[pair].finish if pair < 2 else finish_out)

    def wait_share():
        steps.once(lambda: share.wait_recv())

    def first_half():
        def act(s):
            mixed_in(s).wait_recv()
            layer.out_project(s)
            normed(s).start()

        steps.loop(act)

    def feed(n):
        wait = wait_once(normed)

        def act(s):
            wait(s)
            layer.feed_up(s, UP_LANES[n])

        steps.loop(act, ups[n].finish)

    def feed_other(n):
        lanes = DOWN_LANES[n]

        def act(two):
            at = pl.ds(2 * two, 2)
            r.part_out[at, :, lanes] = layer.feed_down(two, 1 - p, lanes).astype(BF16)
            if n == len(DOWN_LANES) - 1:
                for s in range(2):
                    down_part(2 * two + s).start()

        steps.loop(act, downs[n].finish, seqs // 2)

    def feed_own(n):
        lanes = DOWN_LANES[n]

        def act(two):
            r.part_own[pl.ds(2 * two, 2), :, lanes] = layer.feed_down(two, p, lanes)

        steps.loop(act, count=seqs // 2)

    def second_norm():
        def act(s):
            down_part(s).wait_recv()
            layer.finish_norm(s)
            down_grad(s).start()
            local(r.final.at[s], r.layer_output.at[s, 0], 2).start()

        steps.loop(act, local(r.cotangent.at[:, 0], r.out_grad, 1).wait)

    def first_down_grads():
        def act():
            each(seqs - 1, lambda s: down_grad(s).wait_recv())
            layer.first_down_weight_grad()

        waited.append(down_grad)
        steps.once(act)

    def wait_grads():
        steps.once(lambda: down_grad(seqs - 1).wait_recv())

    def down_grads(m):
        steps.once(lambda: layer.down_weight_grad(m))

    def hidden_back():
        wait = wait_once(down_grad)

        def act(s):
            wait(s)
            layer.hidden_back(s)

        steps.loop(act)

    def up_grads(n):
        steps.once(lambda: layer.up_weight_grad(n // 2, n % 2))

    def back_other():
        def first():
            for group in (4, 5, 6):
                sent(group)

        def act(two):
            r.part_out[pl.ds(2 * two, 2)] = layer.normed_back(two, 1 - p).astype(BF16)
            for s in range(2):
                normed_part(2 * two + s).start()

        steps.loop(act, first, seqs // 2)

    def back_own():
        def act(two):
            r.part_own[pl.ds(2 * two, 2)] = layer.normed_back(two, p)

        steps.loop(act, count=seqs // 2)

    def first_norm():
        def act(s):
            normed_part(s).wait_recv()
            layer.first_norm_back(s)
            branch(s).start()

        steps.loop(act)

    def mixed_grad():
        def act(s):
            branch(s).wait_recv()
            layer.mixed_back(s)

        steps.loop(act)

    def out_grad():
        steps.once(layer.out_weight_grad)
        for one in downs:
            one.drain()

    def attention_back(pair):
        steps.loop(lambda s: layer.attend_back(s, pair))

    def head_grads(pair):
        steps.once(lambda: layer.project_weight_grad(pair))

    def pack_vectors():
        def act():
            for pair in range(3):
                layer.project_bias_grad(pair)
            pack_small(r, p)

        steps.once(act)

    def token_other():
        def act(two):
            r.part_out[pl.ds(2 * two, 2)] = layer.token_back(two, 1 - p).astype(BF16)
            for s in range(2):
                token_part(2 * two + s).start()

        steps.loop(act, lambda: sent(7), seqs // 2)

    def token_own():
        def act(two):
            r.part_own[pl.ds(2 * two, 2)] = layer.token_back(two, p)

        steps.loop(act, count=seqs // 2)

    def token_end():
        def first():
            for one in [small] + heads + ups:
                one.drain()
            for copy in (small_swap, share):
                copy.wait_send()
            to_other(r.stack.at[1 - p], r.stack.at[p], 12, 0).wait_send()
            for group in (3, 8, 10):
                sent(group)

        def act(s):
            token_part(s).wait_recv()
            total = r.part_own[s] + r.part_in[s].astype(F32) + r.resid_grad[s]
            r.token_grad[s] = total.astype(BF16)
            local(r.token_grad.at[s], r.tokens_gradient.at[s, 0], 3).start()

        steps.loop(act, first)

    def collect():
        def act():
            sums_swap.wait_recv()
            r.out_pack[2, 0:16, pack : pack + 256] = r.sum_small[...] + r.sum_theirs[...]
            whole = pack_swap(slice(0, pack))
            whole.wait()
            for one in reduces:
                one.drain()
            sums_swap.wait_send()
            sent(9)
            for outgoing in (2, 3):
                local(r.part_out, r.part_in, outgoing).wait()

        steps.once(act)

    units = dict(
        sa=pack_heads,
        sb=pack_rest,
        ge=first_down_grads,
        unpack=unpack,
        att=attention,
        wo=wait_share,
        out=first_half,
        up=feed,
        do=feed_other,
        dw=feed_own,
        ln2=second_norm,
        ddw=wait_grads,
        gd=down_grads,
        hb=hidden_back,
        gu=up_grads,
        no=back_other,
        nw=back_own,
        ln1=first_norm,
        mb=mixed_grad,
        go=out_grad,
        ab=attention_back,
        gq=head_grads,
        ps=pack_vectors,
        to=token_other,
        tw=token_own,
        te=token_end,
        end=collect,
    )
    for name, *which in UNITS:
        units[name](*which)
    assert not steps.waiting


def finish_kernel(r):
    p = lax.axis_index(PAIR)
    half = r.query_out.shape[1] // 2
    size = r.down_out.shape[0]
    for core in range(2):
        for pair in range(3):
            for part, target in enumerate((r.query_out, r.key_out, r.value_out)):
                place = (0, 1, 2, 6, 7, 8, 10, 11, 9)[3 * pair + part]
                at, lane = 128 * place, half * core + 128 * pair
                target[:, lane : lane + 128] = r.pack[core, :, at : at + 128]
        r.out_out[:, half * core : half * core + half] = r.pack[core, :, half : 2 * half]
    rows, width = r.query_out.shape
    groups = []
    for group in range(CHIPS // 4):
        at = 4 * half + 4 * size * group
        groups.append(jnp.concatenate([r.pack[core, :, at : at + 4 * size] for core in range(2)], 1))
    rest = jnp.concatenate(groups, 0)
    parts = []
    for _ in range(3):
        parts.append(rest.astype(BF16).astype(F32))
        rest = rest - parts[-1]
    laid = nt(jnp.concatenate(parts, 0).astype(BF16), ordered(size).astype(BF16))
    count = laid.shape[0] // 3
    laid = laid[:count] + laid[count : 2 * count] + laid[2 * count :]
    for group in range(CHIPS // 4):
        to = 8 * size * group
        r.up_out[:, to : to + 8 * size] = laid[rows * group : rows * group + rows]
    for group in range(size // rows):
        r.down_out[rows * group : rows * group + rows] = r.pack[2, :, width * group : width * group + width]
    small = r.pack[2, 0:16, 4 * half + r.up_out.shape[1] // 2 :]
    for vector, target in enumerate(r.vectors):
        row = jnp.where(p == 0, small[2 * vector : 2 * vector + 1], small[2 * vector + 1 : 2 * vector + 2])
        target[...] = row[:, : target.shape[1]]
    row = jnp.where(p == 0, small[0:1], small[1:2])
    r.up_vector[...] = row[:, 128 : 128 + size]


def call(kernel, ins, outs, scratch, semaphores, elsewhere=(), **params):
    names = list(ins) + list(outs) + list(scratch) + list(semaphores)

    def body(*refs):
        kernel(Refs(zip(names, refs)))

    def spec(name):
        return pl.BlockSpec(memory_space=pl.ANY if name in elsewhere else pltpu.VMEM)

    results = pl.pallas_call(
        body,
        out_shape=[jax.ShapeDtypeStruct(*held_as) for held_as in outs.values()],
        in_specs=[spec(name) for name in ins],
        out_specs=[spec(name) for name in outs],
        scratch_shapes=[pltpu.VMEM(*held_as) for held_as in scratch.values()] + list(semaphores.values()),
        compiler_params=pltpu.CompilerParams(**params),
        name=kernel.__name__,
    )(*ins.values())
    return Refs(zip(outs, results))


def fast(
    tokens,
    segment_ids,
    query_weight,
    query_bias,
    key_weight,
    value_weight,
    value_bias,
    out_weight,
    out_bias,
    first_gain,
    first_shift,
    up_weight,
    up_bias,
    down_weight,
    down_bias,
    second_gain,
    second_shift,
    cotangent,
):
    seqs, _, slots, width = tokens.shape
    units = up_weight.shape[1] // 2
    per = up_weight.shape[0]
    half = width // 2
    size = units // CHIPS
    rows = 2 * slots
    space = -(-rows // 128) * 128
    ins = dict(
        tokens=tokens,
        cotangent=cotangent,
        segment_ids=segment_ids,
        query_weight=query_weight,
        key_weight=key_weight,
        value_weight=value_weight,
        out_weight=out_weight,
        up_weight=up_weight,
        down_weight=down_weight,
        query_bias=query_bias,
        value_bias=value_bias,
        out_bias=out_bias,
        first_gain=first_gain,
        first_shift=first_shift,
        down_bias=down_bias,
        second_gain=second_gain,
        second_shift=second_shift,
        up_bias=up_bias,
    )
    pack = 4 * half + units
    outs = dict(
        layer_output=(tokens.shape, BF16),
        tokens_gradient=(tokens.shape, BF16),
        out_pack=((3, per, pack + 256), F32),
    )
    all_rows = seqs * rows
    held = dict(
        stack=((2, per, pack), F32),
        sum_pack=((2 * per, pack), F32),
        small_in=((16, 256), F32),
        small_theirs=((16, 256), F32),
        sum_theirs=((16, 256), F32),
        sum_small=((16, 256), F32),
        small_all=((CHIPS * 16, 256), F32),
        vec=((8, width), F32),
        upb=((1, units), F32),
        gvec=((8, width), F32),
        gacc=((64, width), F32),
        upg=((1, units), F32),
        fill=((seqs, rows, space), BF16),
        probs_grad=((2 * rows, space), F32),
        product=((rows, width), F32),
        score_grad=((rows, 2 * space), BF16),
        x_all=((all_rows, width), BF16),
        wq0=((width, half), BF16),
        wq1=((width, half), BF16),
        wq2o=((width, width), BF16),
        wo=((2, width, half), BF16),
        wup=((width, units), BF16),
        wdown=((units, width), BF16),
        qkv=((3, all_rows, half), BF16),
        pt=((3 * seqs, rows, 2 * space), BF16),
        mixed=((all_rows, width), BF16),
        xhat=((seqs, slots, width), F32),
        rstd=((seqs, slots, 128), F32),
        n_all=((all_rows, width), BF16),
        hidden=((all_rows, units), BF16),
        slope=((all_rows, units), BF16),
        part_own=((seqs, slots, width), F32),
        part_out=((seqs, slots, width), BF16),
        part_in=((seqs, slots, width), BF16),
        out_grad=((seqs, slots, width), BF16),
        final=((seqs, slots, width), BF16),
        token_grad=((seqs, slots, width), BF16),
        resid_grad=((seqs, slots, width), F32),
        dd_all=((all_rows, width), BF16),
        gd=((units, width), BF16),
        first_sum=((half, width), F32),
        land_d0=((Reduce.SLOTS * size, DOWN_SUM_LANES[0].stop), BF16),
        land_d1=((Reduce.SLOTS * size, width - DOWN_SUM_LANES[0].stop), BF16),
        land_u0=((Reduce.SLOTS * 2 * per, UP_SUM_LANES[0].stop), BF16),
        land_u1=((Reduce.SLOTS * 2 * per, units - UP_SUM_LANES[0].stop), BF16),
        land_oq=((Reduce.SLOTS * 2 * per, width), BF16),
        land_q1=((Reduce.SLOTS * 2 * per, half + 128), BF16),
        land_q2=((Reduce.SLOTS * (2 * per + 16), half - 128), BF16),
    )
    dma = pltpu.SemaphoreType.DMA
    semaphores = dict(
        pair_send=dma((13,)),
        pair_recv=dma((9 + 7 * seqs + len(UP_LANES),)),
        gather_send=dma((8,)),
        gather_recv=dma((8, Gather.ARRIVALS)),
        local_done=dma((4,)),
        reduce_send=dma((7,)),
        reduce_recv=dma((7, Reduce.ARRIVALS)),
    )

    def layer(r):
        r.gu = r.hidden.at[0:width]
        last = width + 16 * CHIPS
        r.goq = r.slope.at[0:width, 0 : 2 * half]
        split = 3 * half + 128
        r.gq0 = r.slope.at[0:width, 0:half]
        r.gq1 = r.slope.at[0:width, 2 * half : split]
        r.gq2 = r.slope.at[0:last, split : 4 * half]
        r.go = r.slope.at[0:width, half : 2 * half]
        r.wq = [r.wq0, r.wq1, r.wq2o.at[:, 0:half]]
        r.dqkv = [r.wdown.at[0:all_rows, 0:half], r.wdown.at[0:all_rows, half:width], r.dd_all.at[:, 0:half]]
        r.dm = r.dd_all.at[:, half:width]
        r.land_d = [r.land_d0, r.land_d1]
        r.land_u = [r.land_u0, r.land_u1]
        r.vectors = [
            r.query_bias,
            r.value_bias,
            r.out_bias,
            r.first_gain,
            r.first_shift,
            r.down_bias,
            r.second_gain,
            r.second_shift,
        ]
        layer_kernel(r)

    elsewhere = dict(tokens=1, cotangent=1, layer_output=1, tokens_gradient=1)
    done = call(
        layer, ins, outs, held, semaphores, elsewhere, vmem_limit_bytes=VMEM_BYTES, collective_id=0, has_side_effects=True
    )

    square = ((per, width), F32)
    line = ((1, per), F32)
    finals = dict(
        query_out=square,
        query_vector=line,
        key_out=square,
        value_out=square,
        value_vector=line,
        out_out=square,
        out_vector=line,
        gain_vector=line,
        shift_vector=line,
        up_out=(up_weight.shape, F32),
        up_vector=((1, size), F32),
        down_out=(down_weight.shape, F32),
        down_vector=line,
        last_gain_vector=line,
        last_shift_vector=line,
    )

    def finish(r):
        r.vectors = [
            r.query_vector,
            r.value_vector,
            r.out_vector,
            r.gain_vector,
            r.shift_vector,
            r.down_vector,
            r.last_gain_vector,
            r.last_shift_vector,
        ]
        finish_kernel(r)

    final = call(finish, dict(pack=done.out_pack), finals, {}, {}, vmem_limit_bytes=16 * 1024 * 1024)
    flat = [value[0] if value.shape[0] == 1 else value for value in final.values()]
    return (done.layer_output, done.tokens_gradient, *flat)


def solution(mesh):
    in_specs = (
        P(BATCH, PAIR, None, None),
        P(BATCH, None, None),
        P(AXES, None),
        P(AXES),
        P(AXES, None),
        P(AXES, None),
        P(AXES),
        P(AXES, None),
        P(AXES),
        P(AXES),
        P(AXES),
        P(AXES, None),
        P(AXES),
        P(AXES, None),
        P(AXES),
        P(AXES),
        P(AXES),
        P(BATCH, PAIR, None, None),
    )
    out_specs = (
        P(BATCH, PAIR, None, None),
        P(BATCH, PAIR, None, None),
        P(AXES, None),
        P(AXES),
        P(AXES, None),
        P(AXES, None),
        P(AXES),
        P(AXES, None),
        P(AXES),
        P(AXES),
        P(AXES),
        P(AXES, None),
        P(AXES),
        P(AXES, None),
        P(AXES),
        P(AXES),
        P(AXES),
    )
    small_slice = dict(mesh.shape) == {BATCH: CHIPS, PAIR: 2}
    part = fast if small_slice else local
    return jax.shard_map(part, mesh=mesh, in_specs=in_specs, out_specs=out_specs, check_vma=False)
```

```python
import jax
import jax.numpy as jnp
from jax import lax
from jax.experimental import pallas as pl
from jax.experimental.pallas import tpu as pltpu
from jax.sharding import PartitionSpec as P

BATCH, PAIR = AXES = ("batch", "pair")
HEAD_DIM = 64


EPSILON = 1e-05
NEG_FILL = -1e30


def swapped(value, axis, stride):
    return lax.ppermute(value, axis, [(i, i ^ 1 << stride) for i in range(lax.axis_size(axis))])


def layer_norm(values, gain, shift):
    average = jnp.mean(values, -1, keepdims=True)
    centred = values - average
    variance = jnp.mean(centred * centred, -1, keepdims=True)
    return centred * lax.rsqrt(variance + EPSILON) * gain + shift


def matmul(left, right):
    return jnp.dot(left, right, preferred_element_type=jnp.float32)


def product_back(left, right):
    return lax.dot_general(
        left, right, (((left.ndim - 1,), (1,)), ((), ())), preferred_element_type=jnp.float32
    )


def outer_sum(left, right):
    flat_left = left.reshape(-1, left.shape[-1])
    flat_right = right.reshape(-1, right.shape[-1])
    return lax.dot_general(
        flat_left, flat_right, (((0,), (0,)), ((), ())), preferred_element_type=jnp.float32
    )


def row_total(values):
    return jnp.sum(values.astype(jnp.float32), (0, 1))


def scores_of(query_heads, key_rows, allowed, factor):
    raw = jnp.einsum("sqhd,skhd->shqk", query_heads, key_rows, preferred_element_type=jnp.float32)
    return jnp.where(allowed, raw * factor, NEG_FILL)


def local(
    tokens,
    segment_ids,
    query_weight,
    query_bias,
    key_weight,
    value_weight,
    value_bias,
    out_weight,
    out_bias,
    first_gain,
    first_shift,
    up_weight,
    up_bias,
    down_weight,
    down_bias,
    second_gain,
    second_shift,
    cotangent,
):
    seqs = tokens.shape[0]
    slots = tokens.shape[2]
    width = tokens.shape[3]
    heads = width // HEAD_DIM
    factor = HEAD_DIM ** (-0.5)
    token_rows = tokens.reshape(seqs, slots, width)
    attention_shards = (
        query_weight,
        query_bias,
        key_weight,
        value_weight,
        value_bias,
        out_weight,
        out_bias,
        first_gain,
        first_shift,
    )
    feedforward_shards = (up_weight, up_bias, down_weight, down_bias, second_gain, second_shift)
    attention_full = (
        lax.all_gather(attention_shards[0], AXES, axis=0, tiled=True),
        lax.all_gather(attention_shards[1], AXES, axis=0, tiled=True),
        lax.all_gather(attention_shards[2], AXES, axis=0, tiled=True),
        lax.all_gather(attention_shards[3], AXES, axis=0, tiled=True),
        lax.all_gather(attention_shards[4], AXES, axis=0, tiled=True),
        lax.all_gather(attention_shards[5], AXES, axis=0, tiled=True),
        lax.all_gather(attention_shards[6], AXES, axis=0, tiled=True),
        lax.all_gather(attention_shards[7], AXES, axis=0, tiled=True),
        lax.all_gather(attention_shards[8], AXES, axis=0, tiled=True),
    )
    feedforward_full = (
        lax.all_gather(feedforward_shards[0], AXES, axis=0, tiled=True),
        lax.all_gather(feedforward_shards[1], AXES, axis=0, tiled=True),
        lax.all_gather(feedforward_shards[2], AXES, axis=0, tiled=True),
        lax.all_gather(feedforward_shards[3], AXES, axis=0, tiled=True),
        lax.all_gather(feedforward_shards[4], AXES, axis=0, tiled=True),
        lax.all_gather(feedforward_shards[5], AXES, axis=0, tiled=True),
    )
    (
        query_mat,
        query_vec,
        key_mat,
        value_mat,
        value_vec,
        out_mat,
        out_vec,
        gain_first,
        shift_first,
    ) = attention_full
    up_mat, up_vec, down_mat, down_vec, gain_second, shift_second = feedforward_full
    pair_index = lax.axis_index(PAIR)
    own_ids = lax.dynamic_index_in_dim(segment_ids, pair_index, 1, keepdims=False)
    other_ids = lax.dynamic_index_in_dim(segment_ids, 1 - pair_index, 1, keepdims=False)
    key_ids = jnp.concatenate([own_ids, other_ids], 1)
    allowed = (own_ids[:, :, None] == key_ids[:, None, :])[:, None]
    queries = (matmul(token_rows, query_mat) + query_vec).astype(jnp.bfloat16)
    keys_own = matmul(token_rows, key_mat).astype(jnp.bfloat16)
    values_own = (matmul(token_rows, value_mat) + value_vec).astype(jnp.bfloat16)
    keys_other, values_other = swapped((keys_own, values_own), PAIR, 0)
    head_rows = (seqs, 2 * slots, heads, HEAD_DIM)
    key_rows = jnp.concatenate([keys_own, keys_other], 1).reshape(head_rows)
    value_rows = jnp.concatenate([values_own, values_other], 1).reshape(head_rows)
    query_heads = queries.reshape(seqs, slots, heads, HEAD_DIM)
    scores = scores_of(query_heads, key_rows, allowed, factor)
    row_max = jnp.max(scores, -1, keepdims=True)
    log_total = row_max + jnp.log(jnp.sum(jnp.exp(scores - row_max), -1, keepdims=True))
    probs_low = jnp.exp(scores - log_total).astype(jnp.bfloat16)
    mixed = jnp.einsum("shqk,skhd->sqhd", probs_low, value_rows, preferred_element_type=jnp.float32)
    mixed = mixed.reshape(seqs, slots, width).astype(jnp.bfloat16)
    first_resid = token_rows.astype(jnp.float32) + matmul(mixed, out_mat) + out_vec
    normed, first_pull = jax.vjp(
        layer_norm, first_resid, gain_first.astype(jnp.float32), shift_first.astype(jnp.float32)
    )
    normed_low = normed.astype(jnp.bfloat16)
    pre_hidden = matmul(normed_low, up_mat) + up_vec
    hidden, gelu_pull = jax.vjp(jax.nn.gelu, pre_hidden)
    hidden_low = hidden.astype(jnp.bfloat16)
    second_resid = normed + matmul(hidden_low, down_mat) + down_vec
    final, second_pull = jax.vjp(
        layer_norm, second_resid, gain_second.astype(jnp.float32), shift_second.astype(jnp.float32)
    )
    layer_output = final.astype(jnp.bfloat16).reshape(tokens.shape)
    out_grad = cotangent.reshape(seqs, slots, width).astype(jnp.float32)
    second_grad, gain_second_grad, shift_second_grad = second_pull(out_grad)
    down_in = second_grad.astype(jnp.bfloat16)
    down_weight_grad = outer_sum(hidden_low, down_in)
    down_bias_grad = row_total(down_in)
    hidden_grad = product_back(down_in, down_mat)
    (pre_grad,) = gelu_pull(hidden_grad)
    pre_low = pre_grad.astype(jnp.bfloat16)
    up_weight_grad = outer_sum(normed_low, pre_low)
    up_bias_grad = row_total(pre_low)
    normed_grad = product_back(pre_low, up_mat) + second_grad
    first_grad, gain_first_grad, shift_first_grad = first_pull(normed_grad)
    feedforward_terms = (
        up_weight_grad,
        up_bias_grad,
        down_weight_grad,
        down_bias_grad,
        gain_second_grad,
        shift_second_grad,
    )
    feedforward_parts = (
        lax.psum_scatter(feedforward_terms[0], AXES, scatter_dimension=0, tiled=True),
        lax.psum_scatter(feedforward_terms[1], AXES, scatter_dimension=0, tiled=True),
        lax.psum_scatter(feedforward_terms[2], AXES, scatter_dimension=0, tiled=True),
        lax.psum_scatter(feedforward_terms[3], AXES, scatter_dimension=0, tiled=True),
        lax.psum_scatter(feedforward_terms[4], AXES, scatter_dimension=0, tiled=True),
        lax.psum_scatter(feedforward_terms[5], AXES, scatter_dimension=0, tiled=True),
    )
    branch_low = first_grad.astype(jnp.bfloat16)
    out_weight_grad = outer_sum(mixed, branch_low)
    out_bias_grad = row_total(branch_low)
    mixed_grad = (
        product_back(branch_low, out_mat).astype(jnp.bfloat16).reshape(seqs, slots, heads, HEAD_DIM)
    )
    scores = scores_of(query_heads, key_rows, allowed, factor)
    probs = jnp.exp(scores - log_total)
    probs_low = probs.astype(jnp.bfloat16)
    probs_grad = jnp.einsum(
        "sqhd,skhd->shqk", mixed_grad, value_rows, preferred_element_type=jnp.float32
    )
    delta = jnp.sum(probs * probs_grad, -1, keepdims=True)
    score_grad = (probs * (probs_grad - delta)).astype(jnp.bfloat16)
    query_grad = (
        jnp.einsum("shqk,skhd->sqhd", score_grad, key_rows, preferred_element_type=jnp.float32)
        * factor
    )
    query_grad = query_grad.reshape(seqs, slots, width).astype(jnp.bfloat16)
    key_grad_all = jnp.einsum(
        "shqk,sqhd->skhd", score_grad, query_heads, preferred_element_type=jnp.float32
    )
    key_grad_all = (key_grad_all * factor).reshape(seqs, 2 * slots, width)
    value_grad_all = jnp.einsum(
        "shqk,sqhd->skhd", probs_low, mixed_grad, preferred_element_type=jnp.float32
    )
    value_grad_all = value_grad_all.reshape(seqs, 2 * slots, width)
    keys_back, values_back = (
        swapped(key_grad_all[:, slots:].astype(jnp.bfloat16), PAIR, 0).astype(jnp.float32),
        swapped(value_grad_all[:, slots:].astype(jnp.bfloat16), PAIR, 0).astype(jnp.float32),
    )
    key_grad = (key_grad_all[:, :slots] + keys_back).astype(jnp.bfloat16)
    value_grad = (value_grad_all[:, :slots] + values_back).astype(jnp.bfloat16)
    query_weight_grad = outer_sum(token_rows, query_grad)
    query_bias_grad = row_total(query_grad)
    key_weight_grad = outer_sum(token_rows, key_grad)
    value_weight_grad = outer_sum(token_rows, value_grad)
    value_bias_grad = row_total(value_grad)
    tokens_grad = first_grad + product_back(query_grad, query_mat) + product_back(key_grad, key_mat)
    tokens_grad = tokens_grad + product_back(value_grad, value_mat)
    tokens_gradient = tokens_grad.astype(jnp.bfloat16).reshape(tokens.shape)
    attention_terms = (
        query_weight_grad,
        query_bias_grad,
        key_weight_grad,
        value_weight_grad,
        value_bias_grad,
        out_weight_grad,
        out_bias_grad,
        gain_first_grad,
        shift_first_grad,
    )
    attention_parts = (
        lax.psum_scatter(attention_terms[0], AXES, scatter_dimension=0, tiled=True),
        lax.psum_scatter(attention_terms[1], AXES, scatter_dimension=0, tiled=True),
        lax.psum_scatter(attention_terms[2], AXES, scatter_dimension=0, tiled=True),
        lax.psum_scatter(attention_terms[3], AXES, scatter_dimension=0, tiled=True),
        lax.psum_scatter(attention_terms[4], AXES, scatter_dimension=0, tiled=True),
        lax.psum_scatter(attention_terms[5], AXES, scatter_dimension=0, tiled=True),
        lax.psum_scatter(attention_terms[6], AXES, scatter_dimension=0, tiled=True),
        lax.psum_scatter(attention_terms[7], AXES, scatter_dimension=0, tiled=True),
        lax.psum_scatter(attention_terms[8], AXES, scatter_dimension=0, tiled=True),
    )
    return (
        layer_output,
        tokens_gradient,
        attention_parts[0],
        attention_parts[1],
        attention_parts[2],
        attention_parts[3],
        attention_parts[4],
        attention_parts[5],
        attention_parts[6],
        attention_parts[7],
        attention_parts[8],
        feedforward_parts[0],
        feedforward_parts[1],
        feedforward_parts[2],
        feedforward_parts[3],
        feedforward_parts[4],
        feedforward_parts[5],
    )


F32 = jnp.float32
BF16 = jnp.bfloat16
MESH = pl.DeviceIdType.MESH
CHIPS = 16
LINE = 4
VMEM_BYTES = 63 * 1024 * 1024


def dot(left, right, left_dim, right_dim, precision=None):
    return lax.dot_general(
        left,
        right,
        (((left_dim,), (right_dim,)), ((), ())),
        preferred_element_type=F32,
        precision=precision,
    )


def nn(left, right):
    return dot(left, right, 1, 0)


def nt(left, right):
    return dot(left, right, 1, 1)


def tn(left, right):
    return dot(left, right, 0, 0)


def iota(shape, dim):
    return lax.broadcasted_iota(jnp.int32, shape, dim)


class Refs(dict):
    __getattr__ = dict.__getitem__
    __setattr__ = dict.__setitem__


def column_sum(values):
    return jnp.sum(values, 0, keepdims=True)


def lane_mean(values):
    return jnp.mean(values, -1, keepdims=True)


def block(start, size):
    return pl.ds(pl.multiple_of(start * size, size), size)


def each(count, act):
    def step(s, carry):
        act(s)
        return carry

    lax.fori_loop(0, count, step, 0)


class Links:
    def __init__(self):
        self.b = lax.axis_index(BATCH)
        self.p = lax.axis_index(PAIR)
        self.z = lax.div(self.b, 4)
        x = lax.rem(self.b, 2)
        y = lax.rem(lax.div(self.b, 2), 2)
        self.f = x + self.p * (y - x)
        self.g = y + self.p * (x - y)
        self.near = self.chip(self.z, 1)
        self.far = self.index(self.z, self.f, 1 - self.g)
        third = lax.div(self.z, 3)
        second = lax.div(self.z, 2) - third
        zeroth = 1 - lax.div(self.z + 3, 4)
        self.is_z = (zeroth, 1 - zeroth - second - third, second, third)

    def index(self, z, f, g):
        return 4 * z + (1 + self.p) * f + (2 - self.p) * g

    def chip(self, z, side):
        return self.index(z, self.f + side * (1 - 2 * self.f), self.g)

    def by_z(self, values):
        return sum(flag * value for flag, value in zip(self.is_z, values))

    def column(self):
        return [lax.rem(self.z + step, LINE) for step in (1, 3, 2)]

    def other(self):
        return (self.b, 1 - self.p)

    def greet(self):
        semaphore = pltpu.get_barrier_semaphore()
        partners = [self.chip(z, 0) for z in self.column()] + [self.near, self.far]
        for device in [(chip, self.p) for chip in partners] + [self.other()]:
            pl.semaphore_signal(semaphore, inc=1, device_id=device, device_id_type=MESH)

    def meet(self):
        pl.semaphore_wait(pltpu.get_barrier_semaphore(), 6)


class Gather:
    ARRIVE = ((1, 2, 3), (2, 0, 3), (3, 1, 0), (2, 1, 0))
    FROM_FAR = CHIPS
    ARRIVALS = CHIPS + 1

    def __init__(self, links, ref, send, recv, near_first=False):
        self.links, self.ref, self.send, self.recv = links, ref, send, recv
        self.size = ref.shape[0] // CHIPS
        self.near_first = near_first

    def copy(self, rows, chip, arrival):
        part = self.ref.at[rows]
        return pltpu.make_async_remote_copy(
            src_ref=part,
            dst_ref=part,
            send_sem=self.send,
            recv_sem=self.recv.at[arrival],
            device_id=(chip, self.links.p),
            device_id_type=MESH,
        )

    def wait(self, shard):
        self.copy(block(shard, self.size), self.links.far, shard).wait_recv()

    def to_far(self, z, side):
        shard = self.links.chip(z, side)
        self.copy(block(shard, self.size), self.links.far, self.FROM_FAR).start()

    def to_near(self, z):
        shard = self.links.chip(z, 0)
        self.copy(block(shard, self.size), self.links.near, shard).start()

    def to_column(self, z, side):
        k = self.links
        shard = k.chip(k.z, side)
        self.copy(block(shard, self.size), k.chip(z, 0), shard).start()

    def own(self):
        k = self.links
        self.to_near(k.z)
        self.to_far(k.z, 0)
        for z in k.column():
            self.to_column(z, 0)

    def near(self, turn):
        k = self.links
        z = k.z if turn == 0 else k.by_z([order[turn - 1] for order in self.ARRIVE])
        self.wait(k.chip(z, 1))
        if self.near_first and turn == 0:
            for other in k.column():
                self.to_column(other, 1)
        self.to_far(z, 1)

    def along(self, turn):
        k = self.links
        z = k.by_z([order[turn] for order in self.ARRIVE])
        self.wait(k.chip(z, 0))
        if not self.near_first:
            self.to_near(z)
        self.to_far(z, 0)

    def steps(self):
        steps = [self.own, lambda: self.near(0)]
        for turn in range(LINE - 1):
            steps.append(lambda turn=turn: self.along(turn))
            steps.append(lambda turn=turn: self.near(turn + 1))
        return steps

    def finish(self):
        self.copy(slice(0, 8 * self.size), self.links.far, self.FROM_FAR).wait_recv()

    def drain(self):
        self.copy(slice(0, 15 * self.size), self.links.far, self.FROM_FAR).wait_send()


class Reduce:
    LEAVE = ((3, 2, 1), (3, 2, 0), (0, 1, 3), (0, 1, 2))
    SLOTS = 15
    ARRIVALS = 10

    def __init__(self, links, grad, land, send, recv, near_first=False):
        self.links, self.grad, self.land = links, grad, land
        self.send, self.recv = send, recv
        self.size = grad.shape[0] // CHIPS
        self.near_first = near_first

    def rows(self, z, f, count=1, far=0):
        k = self.links
        g = k.g + far * (1 - 2 * k.g)
        at = 4 * z + 2 * g + f
        return pl.ds(pl.multiple_of(at * self.size, self.size), count * self.size)

    def slots(self, slot, count=1):
        start = slot * self.size
        return pl.ds(start if isinstance(slot, int) else pl.multiple_of(start, self.size), count * self.size)

    def copy(self, rows, slots, chip, arrival):
        return pltpu.make_async_remote_copy(
            src_ref=self.grad.at[rows],
            dst_ref=self.land.at[slots],
            send_sem=self.send,
            recv_sem=self.recv.at[arrival],
            device_id=(chip, self.links.p),
            device_id_type=MESH,
        )

    def wait(self, arrival, count):
        rows = slice(0, count * self.size)
        self.copy(rows, rows, self.links.far, arrival).wait_recv()

    def wait_far(self, z):
        self.wait(z, 2)

    def wait_near(self, z):
        self.wait(4 if self.near_first else 4 + z, 1)

    def wait_column(self, side):
        self.wait(8 + side, 3)

    def far_slot(self, z, f):
        return 2 * z + f

    def near_slot(self, z):
        return 8 if self.near_first else 8 + z

    def column_slot(self, step, side):
        return (9 + 3 * side if self.near_first else 12) + step - 1

    def column_slots(self, side):
        return [self.column_slot(step, side) for step in range(1, LINE)]

    def total(self, rows, slots):
        total = self.grad[rows].astype(F32)
        for slot in slots:
            total = total + self.land[self.slots(slot)].astype(F32)
        return total

    def add_on(self, rows, slots):
        self.grad[rows] = self.total(rows, slots).astype(self.grad.dtype)

    def far(self, z):
        self.copy(self.rows(z, 0, 2, 1), self.slots(self.far_slot(z, 0), 2), self.links.far, z).start()

    def near(self, z):
        k = self.links
        more = []
        self.wait_far(z)
        if self.near_first:
            self.wait_column(1)
            more = self.column_slots(1)
        rows = self.rows(z, 1 - k.f)
        self.add_on(rows, [self.far_slot(z, 1 - k.f)] + more)
        arrival = 4 if self.near_first else 4 + z
        self.copy(rows, self.slots(self.near_slot(z)), k.near, arrival).start()

    def along(self, turn, side):
        k = self.links
        z = k.by_z([order[turn] for order in self.LEAVE])
        f = k.f + side * (1 - 2 * k.f)
        rows, more = self.rows(z, f), []
        if not self.near_first:
            self.wait_near(z)
            more = [self.near_slot(z)]
        elif side == 1:
            self.wait_far(z)
        self.add_on(rows, [self.far_slot(z, f)] + more)
        slot = self.column_slot(lax.rem(k.z - z + LINE, LINE), side)
        self.copy(rows, self.slots(slot), k.chip(z, 0), 8 + side).start()

    def steps(self):
        steps = [lambda z=z: self.far(z) for z in range(LINE)]
        near = [lambda z=z: self.near(z) for z in range(LINE)]
        sides = (1, 0) if self.near_first else (0,)
        along = [
            lambda turn=turn, side=side: self.along(turn, side)
            for turn in range(LINE - 1)
            for side in sides
        ]
        if self.near_first:
            return steps + along + [lambda: self.near(self.links.z)]
        return steps + near + along

    def result(self):
        k = self.links
        self.wait_near(k.z)
        self.wait_column(0)
        slots = [self.far_slot(k.z, k.f), self.near_slot(k.z)]
        return self.total(self.rows(k.z, k.f), slots + self.column_slots(0))

    def drain(self):
        rows = slice(0, 15 * self.size)
        self.copy(rows, rows, self.links.far, 0).wait_send()


class Steps:
    def __init__(self, seqs, course, transfers):
        lines = [iter(steps) for steps in transfers]
        self.seqs, self.count = seqs, 0
        self.waiting = {place: [next(lines[n]) for n in order] for place, order in course.items()}
        assert all(next(line, None) is None for line in lines)

    def run(self):
        for step in self.waiting.pop(self.count, ()):
            step()
        self.count += 1

    def once(self, act):
        self.run()
        act()

    def loop(self, act, first=None, count=None):
        count = self.seqs if count is None else count
        self.run()
        if first is not None:
            first()
        later = []
        for s in range(1, count):
            later.append((s, self.waiting.pop(self.count, ())))
            self.count += 1

        def turn(s):
            for at, steps in later:
                if steps:

                    @pl.when(s == at)
                    def _():
                        for step in steps:
                            step()

            act(s)

        each(count, turn)


def laying(blocks, cols):
    size = cols // blocks
    pick = iota((128, cols), 0) == lax.rem(iota((128, cols), 1), size)
    return pick, lax.div(iota((blocks, cols), 1), size) == iota((blocks, cols), 0)


def core_order(chip, p):
    low = lax.rem(chip, 4)
    step = (low == 1).astype(jnp.int32) - (low == 2).astype(jnp.int32)
    return chip + p * step


def vector_rows(shape, dim, vector, p):
    device, row = iota(shape, dim), iota(shape, 1 - dim)
    return row == 16 * core_order(lax.div(device, 2), p) + 2 * vector + lax.rem(device, 2)


def unit_rows(shape, dim, which, p):
    return iota(shape, 1 - dim) == 16 * core_order(iota(shape, dim), p) + which


def unpack_small(r, p):
    rows = CHIPS * 16
    flat = r.small_all[...].astype(BF16)
    pick, place = laying(2 * CHIPS, r.vec.shape[1])
    for vector in range(8):
        chosen = nn(vector_rows((2 * CHIPS, rows), 0, vector, 0).astype(BF16), flat[:, :128])
        laid = nn(chosen.astype(BF16), pick.astype(BF16))
        r.vec[vector : vector + 1] = column_sum(jnp.where(place, laid, 0.0))
    pick, place = laying(CHIPS, r.upb.shape[1])
    chosen = nn(unit_rows((CHIPS, rows), 0, p, 0).astype(BF16), flat[:, 128:])
    laid = nn(chosen.astype(BF16), pick.astype(BF16))
    r.upb[...] = column_sum(jnp.where(place, laid, 0.0))


def pack_small(r, p):
    rows, width = CHIPS * 16, r.gvec.shape[1]
    for vector in range(2, 8):
        r.gvec[vector : vector + 1] = column_sum(r.gacc[8 * vector : 8 * vector + 8])
    row = iota((rows, 1), 0)
    device = 2 * core_order(lax.div(row, 16), p) + lax.rem(row, 2)
    chosen = lax.div(lax.rem(iota((rows, 8), 0), 16), 2) == iota((rows, 8), 1)
    spread = nn(chosen.astype(BF16), r.gvec[...].astype(BF16))
    place = device == lax.div(iota((1, width), 1), width // (2 * CHIPS))
    pick, _ = laying(2 * CHIPS, width)
    narrow = nt(jnp.where(place, spread, 0.0).astype(BF16), pick.astype(BF16))
    pick, place = laying(CHIPS, r.upg.shape[1])
    blocks = nt(jnp.where(place, r.upg[...], 0.0).astype(BF16), pick.astype(BF16))
    wide = nn(unit_rows((rows, CHIPS), 1, p, p).astype(BF16), blocks.astype(BF16))
    low = jnp.concatenate([narrow, wide], 1).astype(BF16)
    space = r.gq2.shape[0] // CHIPS
    for chip in range(CHIPS):
        r.gq2[space * chip + space - 16 : space * chip + space] = low[16 * chip : 16 * chip + 16]


def half_lanes(values, half, factor=None):
    mask = lax.div(iota((1, values.shape[1]), 1), HEAD_DIM) == half
    kept = jnp.where(mask, values, jnp.zeros_like(values))
    return kept if factor is None else kept * jnp.asarray(factor, values.dtype)


def normalize(values):
    centred = values - lane_mean(values)
    scale = lax.rsqrt(lane_mean(centred * centred) + EPSILON)
    return centred * scale, scale


def norm_back(grad, hat, scale):
    return scale * (grad - lane_mean(grad) - hat * lane_mean(grad * hat))


def gelu_both(value):
    square = value * value
    root = 0.7978845608028654
    inner = value * (root + root * 0.044715 * square)
    bent = 0.5 * jnp.tanh(inner) + 0.5
    slope = root + 3.0 * root * 0.044715 * square
    return value * bent, bent + 2.0 * value * slope * (bent - bent * bent)


UP_LANES = (slice(0, 768), slice(768, 1536),)
UP_NEAR_FIRST = (False, True)
DOWN_LANES = (slice(0, 512), slice(512, 768),)
DOWN_NEAR_FIRST = (False, True)
UP_SUM_LANES = (slice(0, 768), slice(768, 1536),)
UP_SUM_NEAR_FIRST = (True, False)
DOWN_SUM_LANES = (slice(0, 512), slice(512, 768),)
DOWN_SUM_NEAR_FIRST = (False, True)
UNITS = (
    ("unpack",),
    ("att", 0),
    ("att", 1),
    ("att", 2),
    ("wo",),
    ("out",),
    ("up", 0),
    ("up", 1),
    ("do", 0),
    ("dw", 0),
    ("do", 1),
    ("dw", 1),
    ("ln2",),
    ("ddw",),
    ("gd", 0),
    ("gd", 1),
    ("gd", 2),
    ("gd", 3),
    ("hb",),
    ("gu", 0),
    ("gu", 1),
    ("gu", 2),
    ("gu", 3),
    ("no",),
    ("nw",),
    ("ln1",),
    ("mb",),
    ("go",),
    ("ab", 0),
    ("gq", 0),
    ("ab", 1),
    ("gq", 1),
    ("ab", 2),
    ("ps",),
    ("gq", 2),
    ("to",),
    ("tw",),
    ("te",),
    ("end",),
)
COURSE = {
    0: (0, 1, 2, 3, 0, 0, 2, 4, 0, 0, 3, 1, 1, 6, 2, 1, 0, 0, 1, 3, 0, 1, 1, 5, 1, 2, 2, 3, 3,),
    1: (2, 4, 2,),
    2: (4,),
    3: (2, 3, 3,),
    4: (4, 4, 5,),
    6: (6, 3,),
    7: (6,),
    8: (4, 4, 7,),
    10: (6,),
    12: (6, 5,),
    15: (4,),
    16: (5, 5,),
    17: (5, 5, 6,),
    18: (5, 6, 7, 7,),
    23: (6,),
    24: (7, 7,),
    25: (7, 7, 7,),
    40: (9,),
    41: (9,),
    42: (9,),
    43: (9,),
    44: (8,),
    45: (8, 8, 8, 9,),
    48: (9,),
    49: (9, 9, 9, 8,),
    50: (8, 8,),
    52: (8, 10, 10, 10,),
    55: (8, 9,),
    59: (10, 11,),
    60: (11, 8,),
    63: (8, 11, 11,),
    65: (10,),
    67: (10, 11, 10, 10, 10, 10, 11,),
    68: (11,),
    69: (12, 11,),
    70: (12,),
    72: (12, 12, 12,),
    74: (11,),
    75: (12, 12, 12, 13, 11,),
    77: (11, 13, 13, 13,),
    79: (12, 12, 12, 13,),
    80: (14, 13,),
    81: (13, 13, 14, 14, 8, 14,),
    83: (9, 13, 13, 13, 14, 14,),
    85: (14, 14, 14, 14, 14, 12, 10,),
    86: (9, 11, 10, 13, 14,),
}


class Layer:
    def __init__(self, r, p):
        self.r, self.p = r, p
        self.slots = r.tokens.shape[2]
        self.width = r.tokens.shape[3]
        self.half = self.width // 2
        self.units = r.wup.shape[1]

    def rows(self, s):
        return block(s, 2 * self.slots)

    def side(self, s, side):
        return block(2 * s + side, self.slots)

    def own_lanes(self, pair):
        return pl.ds(pl.multiple_of(self.p * self.half + 128 * pair, 128), 128)

    def project(self, s, pair):
        r = self.r
        result = nn(r.x_all[self.rows(s)], r.wq[pair][...])
        lanes = self.own_lanes(pair)
        query = result[:, :128] + r.vec[0:1, lanes]
        value = result[:, 256:] + r.vec[1:2, lanes]
        r.qkv[pair, self.rows(s)] = jnp.concatenate([query, result[:, 128:256], value], 1).astype(BF16)

    def mask(self, s):
        r = self.r
        rows, space = r.fill.shape[1:]
        rest = jnp.zeros((1, space - rows), F32)
        ids = [r.segment_ids[s, half : half + 1].astype(F32) for half in range(2)]
        across = jnp.broadcast_to(jnp.concatenate(ids + [rest], 1), (space, space))
        r.fill[s] = jnp.where(across.T[:rows] == across[:rows], 0.0, NEG_FILL).astype(BF16)

    def heads(self, s, pair):
        held = self.r.qkv[pair, self.rows(s)]
        return held[:, :128], held[:, 128:256], held[:, 256:]

    def widened(self, values):
        rest = self.r.fill.shape[2] - values.shape[0]
        return jnp.concatenate([values, jnp.zeros((rest, values.shape[1]), values.dtype)], 0)

    def both_halves(self, values, factor=None, widen=False):
        parts = [half_lanes(values, half, factor) for half in range(2)]
        return jnp.concatenate([self.widened(part) if widen else part for part in parts], 0)

    def attend(self, s, pair):
        r = self.r
        rows, space = r.fill.shape[1:]
        queries, keys, values = self.heads(s, pair)
        values_t = values.T
        r.probs_grad[...] = nt(self.both_halves(keys, HEAD_DIM**-0.5), self.widened(queries))
        parts = []
        for half in range(2):
            top, total = NEG_FILL, 0.0
            for at in range(0, rows, 64):
                here = slice(rows * half + at, rows * half + at + 64)
                scores = r.probs_grad[here] + r.fill[s, at : at + 64].astype(F32)
                r.probs_grad[here] = scores
                top = jnp.maximum(top, jnp.max(scores.reshape(8, 8, space), 0))
            top = jnp.max(top, 0, keepdims=True)
            for at in range(0, rows, 64):
                here = slice(rows * half + at, rows * half + at + 64)
                raised = jnp.exp(r.probs_grad[here] - top)
                r.probs_grad[here] = raised
                total = total + jnp.sum(raised.reshape(8, 8, space), 0)
            share = 1.0 / column_sum(total)
            lanes = slice(space * half, space * half + space)
            for at in range(0, rows, 64):
                here = slice(rows * half + at, rows * half + at + 64)
                r.pt[3 * s + pair, at : at + 64, lanes] = (r.probs_grad[here] * share).astype(BF16)
            head = values_t[HEAD_DIM * half : HEAD_DIM * half + HEAD_DIM]
            parts.append(nn(head, r.pt[3 * s + pair, :, lanes]))
        mixed = jnp.concatenate(parts, 0).T[:rows]
        r.mixed[self.rows(s), self.own_lanes(pair)] = mixed.astype(BF16)

    def out_project(self, s):
        r, p = self.r, self.p
        mixed = r.mixed[self.side(s, p)]
        sides = [nn(mixed, r.wo[side]) for side in range(2)]
        r.product[: self.slots] = jnp.concatenate(sides, 1)
        for at, rows in self.pieces(s):
            resid = r.x_all[rows].astype(F32) + r.product[at] + r.vec[2:3]
            hat, scale = normalize(resid)
            r.xhat[s, at] = hat
            r.rstd[s, at] = jnp.broadcast_to(scale, (scale.shape[0], 128))
            r.n_all[rows] = (hat * r.vec[3:4] + r.vec[4:5]).astype(BF16)

    def feed_up(self, s, lanes):
        r = self.r
        r.product[...] = nn(r.n_all[self.rows(s)], r.wup[:, lanes])
        for at, rows in self.strips(s):
            hidden, slope = gelu_both(r.product[at] + r.upb[:, lanes])
            r.hidden[rows, lanes] = hidden.astype(BF16)
            r.slope[rows, lanes] = slope.astype(BF16)

    def two(self, ref, n, side):
        return jnp.concatenate([ref[self.side(2 * n + s, side)] for s in range(2)], 0)

    def by_two(self, rows):
        return rows.reshape(2, self.slots, rows.shape[1])

    def feed_down(self, n, side, lanes):
        return self.by_two(nn(self.two(self.r.hidden, n, side), self.r.wdown[:, lanes]))

    def pieces(self, s):
        for at in range(0, self.slots, 32):
            start = (2 * s + self.p) * self.slots + at
            yield slice(at, at + 32), pl.ds(pl.multiple_of(start, 32), 32)

    def strips(self, s):
        for at in range(0, 2 * self.slots, 32):
            start = 2 * s * self.slots + at
            yield slice(at, at + 32), pl.ds(pl.multiple_of(start, 32), 32)

    def add_rows(self, vector, values):
        folded = values.reshape(values.shape[0] // 8, 8, values.shape[1])
        self.r.gacc[8 * vector : 8 * vector + 8] += jnp.sum(folded, 0)

    def finish_norm(self, s):
        r = self.r
        for at, rows in self.pieces(s):
            normed = r.xhat[s, at] * r.vec[3:4] + r.vec[4:5]
            resid = normed + r.part_own[s, at] + r.part_in[s, at].astype(F32) + r.vec[5:6]
            hat, scale = normalize(resid)
            r.final[s, at] = (hat * r.vec[6:7] + r.vec[7:8]).astype(BF16)
            grad = r.out_grad[s, at].astype(F32)
            self.add_rows(6, grad * hat)
            self.add_rows(7, grad)
            back = norm_back(grad * r.vec[6:7], hat, scale)
            r.resid_grad[s, at] = back
            low = back.astype(BF16)
            r.dd_all[rows] = low
            self.add_rows(5, low.astype(F32))

    def put_blocks(self, ref, first, result, size):
        space = ref.shape[0] // CHIPS
        low = result.astype(BF16)
        for n in range(result.shape[0] // size):
            chip = first + n
            step = (0, 1, -1, 0)[chip % 4]
            at = chip * space
            rows = pl.ds(pl.multiple_of(at + self.p * step * space, 16), size) if step else slice(at, at + size)
            ref[rows] = low[n * size : n * size + size]

    def first_down_weight_grad(self):
        r = self.r
        most = slice(0, r.hidden.shape[0] - 2 * self.slots)
        r.first_sum[...] = tn(r.hidden[most, : self.half], r.dd_all[most])

    def down_weight_grad(self, m):
        r = self.r
        at = slice(self.half * m, self.half * m + self.half)
        if m == 0:
            last = slice(r.hidden.shape[0] - 2 * self.slots, r.hidden.shape[0])
            total = r.first_sum[...] + tn(r.hidden[last, at], r.dd_all[last])
        else:
            total = tn(r.hidden[:, at], r.dd_all[...])
        self.put_blocks(r.gd, 4 * m, total, self.half // 4)

    def hidden_back(self, s):
        r = self.r
        grads = r.dd_all[self.rows(s)]
        for start in range(0, self.units, self.width):
            lanes = slice(start, start + self.width)
            r.product[...] = nt(grads, r.wdown[lanes])
            total = 0.0
            for at, rows in self.strips(s):
                low = (r.product[at] * r.slope[rows, lanes].astype(F32)).astype(BF16)
                r.slope[rows, lanes] = low
                total = total + jnp.sum(low.astype(F32).reshape(4, 8, self.width), 0)
            r.upg[:, lanes] += column_sum(total)

    def up_weight_grad(self, m, n):
        r = self.r
        at = slice(self.half * m, self.half * m + self.half)
        lanes = slice(self.width * n, self.width * n + self.width)
        self.put_blocks(r.gu.at[:, lanes], 8 * m, tn(r.n_all[:, at], r.slope[:, lanes]), self.half // 8)

    def normed_back(self, n, side):
        return self.by_two(nt(self.two(self.r.slope, n, side), self.r.wup[...]))

    def first_norm_back(self, s):
        r = self.r
        for at, rows in self.pieces(s):
            grad = r.part_own[s, at] + r.part_in[s, at].astype(F32) + r.resid_grad[s, at]
            hat = r.xhat[s, at]
            self.add_rows(3, grad * hat)
            self.add_rows(4, grad)
            back = norm_back(grad * r.vec[3:4], hat, r.rstd[s, at, 0:1])
            r.resid_grad[s, at] = back
            low = back.astype(BF16)
            r.n_all[rows] = low
            self.add_rows(2, low.astype(F32))

    def out_weight_grad(self):
        r = self.r
        own = block(self.p, self.half)
        right = r.n_all[:, own]
        for m in range(2):
            at = slice(self.half * m, self.half * m + self.half)
            self.put_blocks(r.go, 8 * m, tn(r.mixed[:, at], right), self.half // 8)

    def mixed_back(self, s):
        r = self.r
        grads = r.n_all[self.rows(s)]
        own = block(self.p, self.half)
        total = nt(grads[:, : self.half], r.wo[0, own]) + nt(grads[:, self.half :], r.wo[1, own])
        r.dm[self.rows(s)] = total.astype(BF16)

    def attend_back(self, s, pair):
        r = self.r
        scale = HEAD_DIM**-0.5
        unit = 3 * s + pair
        rows, space = r.fill.shape[1:]
        queries, keys, values = self.heads(s, pair)
        grads = r.dm[self.rows(s), 128 * pair : 128 * pair + 128]
        r.probs_grad[...] = nt(self.both_halves(values), self.widened(grads))
        for half in range(2):
            lanes = slice(space * half, space * half + space)
            total = 0.0
            for at in range(0, rows, 64):
                grad = r.probs_grad[rows * half + at : rows * half + at + 64]
                product = r.pt[unit, at : at + 64, lanes].astype(F32) * grad
                total = total + jnp.sum(product.reshape(8, 8, space), 0)
            delta = column_sum(total)
            for at in range(0, rows, 64):
                grad = r.probs_grad[rows * half + at : rows * half + at + 64]
                probs = r.pt[unit, at : at + 64, lanes].astype(F32)
                r.score_grad[at : at + 64, lanes] = (probs * (grad - delta)).astype(BF16)
        key_grad = nn(r.score_grad[...], self.both_halves(queries, scale, True))
        keys_t = keys.T * jnp.asarray(scale, BF16)
        query_parts = []
        for half in range(2):
            at = HEAD_DIM * half
            query_parts.append(
                nn(keys_t[at : at + HEAD_DIM], r.score_grad[:, space * half : space * half + space])
            )
        query_grad = jnp.concatenate(query_parts, 0).T[:rows]
        r.dqkv[pair][self.rows(s), :256] = jnp.concatenate([query_grad, key_grad], 1).astype(BF16)
        for other in ((0,), (1, 2), ())[pair]:
            grads = r.dm[self.rows(s), 128 * other : 128 * other + 128]
            value_grad = nn(r.pt[3 * s + other], self.both_halves(grads, None, True))
            r.dqkv[other][self.rows(s), 256:] = value_grad.astype(BF16)

    def project_weight_grad(self, pair):
        r = self.r
        target, right = (r.gq0, r.gq1, r.gq2)[pair], r.dqkv[pair][...]
        if pair == 1:
            right = jnp.concatenate([right, r.dqkv[2][:, 256:]], 1)
        if pair == 2:
            right = right[:, :256]
        for m in range(2):
            at = slice(self.half * m, self.half * m + self.half)
            self.put_blocks(target, 8 * m, tn(r.x_all[:, at], right), self.half // 8)

    def project_bias_grad(self, pair):
        r = self.r
        right = r.dqkv[pair]
        lanes = self.own_lanes(pair)
        r.gvec[0:1, lanes] = column_sum(right[:, :128].astype(F32))
        r.gvec[1:2, lanes] = column_sum(right[:, 256:].astype(F32))

    def token_back(self, n, side):
        r = self.r
        total = 0.0
        for pair in range(3):
            total = total + nt(self.two(r.dqkv[pair], n, side), r.wq[pair][...])
        return self.by_two(total)


def ordered(size):
    column = iota((1, 8 * size), 1)
    within = lax.rem(column, 4 * size)
    source = 2 * size * lax.div(within, size) + size * lax.div(column, 4 * size) + lax.rem(within, size)
    return iota((8 * size, 8 * size), 0) == source


def place_small(r, p):
    r.small_in[...] = jnp.zeros_like(r.small_in)
    rows = [(row, 0, vector) for row, vector in enumerate(r.vectors)] + [(0, 128, r.up_bias)]
    for row, lane, vector in rows:
        count = vector.shape[0]
        values = vector[...].reshape(1, count).astype(F32)
        for core in range(2):

            @pl.when(p == core)
            def _():
                at = 2 * row + core
                r.small_in[at : at + 1, lane : lane + count] = values


def pack_square(r, half, piece):
    at = half * piece
    for core in range(2):
        if piece == 3:
            r.stack[core, :, at : at + half] = r.out_weight[:, half * core : half * core + half].astype(F32)
            continue
        for part, weight in enumerate((r.query_weight, r.key_weight, r.value_weight)):
            lane = half * core + 128 * piece
            r.stack[core, :, at + 128 * part : at + 128 * part + 128] = weight[:, lane : lane + 128].astype(F32)


def pack_up(r, half, size):
    rows = r.up_weight.shape[0]
    groups = [r.up_weight[:, 8 * size * group : 8 * size * group + 8 * size] for group in range(CHIPS // 4)]
    stacked = jnp.concatenate([group.astype(F32) for group in groups], 0).astype(BF16)
    ordered_units = nn(stacked, ordered(size).astype(BF16))
    for group in range(CHIPS // 4):
        to = 4 * half + 4 * size * group
        for core in range(2):
            r.stack[core, :, to : to + 4 * size] = ordered_units[
                rows * group : rows * group + rows, 4 * size * core : 4 * size * core + 4 * size
            ]


def layer_kernel(r):
    k = Links()
    p = k.p
    seqs = r.tokens.shape[0]
    layer = Layer(r, p)
    half = layer.half
    width = layer.width
    per = r.stack.shape[1]
    size = r.down_weight.shape[0]
    pack = r.stack.shape[2]
    def to_other(src, dst, group, arrival):
        return pltpu.make_async_remote_copy(
            src_ref=src,
            dst_ref=dst,
            send_sem=r.pair_send.at[group],
            recv_sem=r.pair_recv.at[arrival],
            device_id=k.other(),
            device_id_type=MESH,
        )

    def local(src, dst, which):
        return pltpu.make_async_copy(src, dst, r.local_done.at[which])

    def trade_own(ref, group, base):
        return lambda s: to_other(ref.at[layer.side(s, p)], ref.at[layer.side(s, p)], group, base + s)

    def trade_slot(src, dst, group, base):
        return lambda s: to_other(src.at[s], dst.at[s], group, base + s)

    def sent(group):
        to_other(r.part_out, r.part_in, group, 0).wait_send()

    small_swap = to_other(r.small_in, r.small_theirs, 0, 0)
    share = to_other(r.wo.at[p], r.wo.at[p], 1, 1)
    sums_swap = to_other(r.sum_small, r.sum_theirs, 2, 2)
    inputs = lambda s: to_other(r.tokens.at[s, 0], r.x_all.at[layer.side(s, p)], 3, 3)
    normed = trade_own(r.n_all, 4, 4)
    down_part = trade_slot(r.part_out, r.part_in, 5, 4 + seqs)
    down_grad = trade_own(r.dd_all, 6, 4 + 2 * seqs)
    normed_part = trade_slot(r.part_out, r.part_in, 7, 4 + 3 * seqs)
    branch = trade_own(r.n_all, 8, 4 + 4 * seqs)
    token_part = trade_slot(r.part_out, r.part_in, 9, 4 + 5 * seqs)

    def mixed(s, pair):
        part = r.mixed.at[layer.rows(s), layer.own_lanes(pair)]
        return to_other(part, part, 10, 4 + 6 * seqs + s)

    def mixed_in(s):
        part = r.mixed.at[layer.rows(s), block(p, half)]
        return to_other(part, part, 10, 4 + 6 * seqs + s)

    def pack_swap(lanes):
        return to_other(r.sum_pack.at[block(1 - p, per), lanes], r.out_pack.at[p, :, lanes], 11, 4 + 7 * seqs)

    pieces = [slice(0, half), slice(half, 2 * half), slice(2 * half, 4 * half)]
    pieces += [slice(4 * half + lanes.start, 4 * half + lanes.stop) for lanes in UP_LANES]

    def piece_swap(n):
        lanes = pieces[n]
        return to_other(
            r.stack.at[1 - p, :, lanes], r.sum_pack.at[block(p, per), lanes], 12, 5 + 7 * seqs + n
        )

    def place_piece(n, target):
        lanes = pieces[n]

        def act():
            piece_swap(n).wait_recv()
            r.sum_pack[block(p, per), lanes] = r.stack[p, :, lanes]
            target[block(k.b, 2 * per)] = r.sum_pack[:, lanes].astype(BF16)

        return act

    def gather(n, ref, near_first=False):
        return Gather(k, ref, r.gather_send.at[n], r.gather_recv.at[n], near_first)

    def reduce(n, grad, land, near_first=False):
        return Reduce(k, grad, land, r.reduce_send.at[n], r.reduce_recv.at[n], near_first)

    small = gather(0, r.small_all)
    heads = [gather(1 + pair, ref) for pair, ref in enumerate((r.wq0, r.wq1, r.wq2o))]
    ups = [gather(4 + n, r.wup.at[:, lanes], first) for n, (lanes, first) in enumerate(zip(UP_LANES, UP_NEAR_FIRST))]
    downs = [
        gather(6 + n, r.wdown.at[:, lanes], first)
        for n, (lanes, first) in enumerate(zip(DOWN_LANES, DOWN_NEAR_FIRST))
    ]
    gathers = [small] + heads + ups + downs
    down_sums = [
        reduce(n, r.gd.at[:, lanes], land, first)
        for n, (lanes, land, first) in enumerate(zip(DOWN_SUM_LANES, r.land_d, DOWN_SUM_NEAR_FIRST))
    ]
    up_sums = [
        reduce(2 + n, r.gu.at[:, lanes], land, first)
        for n, (lanes, land, first) in enumerate(zip(UP_SUM_LANES, r.land_u, UP_SUM_NEAR_FIRST))
    ]
    out_sum = reduce(4, r.goq, r.land_oq)
    head_sums = [reduce(5, r.gq1, r.land_q1), reduce(6, r.gq2, r.land_q2)]
    reduces = down_sums + up_sums + [out_sum] + head_sums

    def store(one, lanes):
        def act():
            r.sum_pack[:, lanes] = one.result()
            pack_swap(lanes).start()
            r.out_pack[p, :, lanes] = r.sum_pack[block(p, per), lanes]

        return act

    def store_down(one, lanes):
        def act():
            total = one.result()
            for group in range(size // per):
                to = slice(width * group + lanes.start, width * group + lanes.stop)
                r.out_pack[2, :, to] = total[per * group : per * group + per]

        return act

    def store_last():
        total = head_sums[1].result()
        r.sum_pack[:, packs[-1]] = total[: 2 * per]
        pack_swap(packs[-1]).start()
        r.sum_small[...] = total[2 * per :]
        sums_swap.start()
        r.out_pack[p, :, packs[-1]] = r.sum_pack[block(p, per), packs[-1]]

    packs = [slice(4 * half + lanes.start, 4 * half + lanes.stop) for lanes in UP_SUM_LANES]
    packs += [slice(0, 2 * half), slice(2 * half, 3 * half + 128), slice(3 * half + 128, 4 * half)]
    stores = [store_down(one, lanes) for one, lanes in zip(down_sums, DOWN_SUM_LANES)]
    stores += [store(one, lanes) for one, lanes in zip(up_sums + [out_sum] + head_sums[:1], packs)]
    stores.append(store_last)

    def place_small_rows():
        small_swap.wait_recv()
        r.small_all[block(k.b, 16)] = r.small_in[...] + r.small_theirs[...]

    def finish_out():
        heads[2].finish()
        r.wo[p] = r.wq2o[:, half:]
        share.start()

    starts = [place_small_rows]
    starts += [place_piece(n, target) for n, target in enumerate((r.wq0, r.wq1, r.wq2o))]
    starts += [place_piece(3 + n, r.wup.at[:, lanes]) for n, lanes in enumerate(UP_LANES)]
    spreads = [one.steps() for one in gathers]
    for steps_of, start in zip(spreads, starts):
        steps_of[0] = lambda start=start, own=steps_of[0]: (start(), own())
    sums = [one.steps() + [last] for one, last in zip(reduces, stores)]
    steps = Steps(seqs, COURSE, spreads + sums)

    k.greet()
    each(seqs, lambda s: local(r.tokens.at[s, 0], r.x_all.at[layer.side(s, p)], 0).start())
    local(r.cotangent.at[:, 0], r.out_grad, 1).start()
    pack_square(r, half, 0)
    place_small(r, p)
    k.meet()
    piece_swap(0).start()
    small_swap.start()
    pack_square(r, half, 1)
    piece_swap(1).start()
    pack_square(r, half, 2)
    pack_square(r, half, 3)
    piece_swap(2).start()
    pack_up(r, half, size)
    for n in range(3, len(pieces)):
        piece_swap(n).start()
    each(seqs, lambda s: inputs(s).start())
    r.wdown[block(k.b, size)] = r.down_weight[...]
    r.gvec[...] = jnp.zeros_like(r.gvec)
    r.gacc[...] = jnp.zeros_like(r.gacc)
    r.upg[...] = jnp.zeros_like(r.upg)

    def wait_once(*copies):
        fresh = [copy for copy in copies if copy not in waited]
        waited.extend(fresh)
        return lambda s: [copy(s).wait_recv() for copy in fresh]

    waited = []

    def unpack():
        def act():
            each(seqs, layer.mask)
            small.finish()
            unpack_small(r, p)
            to_other(r.part_out, r.part_in, 3, 3).wait_recv()
            local(r.part_out, r.part_in, 0).wait()

        steps.once(act)

    def attention(pair):
        def act(s):
            layer.project(s, pair)
            layer.attend(s, pair)
            mixed(s, pair).start()

        steps.loop(act, heads[pair].finish if pair < 2 else finish_out)

    def wait_share():
        steps.once(lambda: share.wait_recv())

    def first_half():
        def act(s):
            mixed_in(s).wait_recv()
            layer.out_project(s)
            normed(s).start()

        steps.loop(act)

    def feed(n):
        wait = wait_once(normed)

        def act(s):
            wait(s)
            layer.feed_up(s, UP_LANES[n])

        steps.loop(act, ups[n].finish)

    def feed_other(n):
        lanes = DOWN_LANES[n]

        def act(two):
            at = pl.ds(2 * two, 2)
            r.part_out[at, :, lanes] = layer.feed_down(two, 1 - p, lanes).astype(BF16)
            if n == len(DOWN_LANES) - 1:
                for s in range(2):
                    down_part(2 * two + s).start()

        steps.loop(act, downs[n].finish, seqs // 2)

    def feed_own(n):
        lanes = DOWN_LANES[n]

        def act(two):
            r.part_own[pl.ds(2 * two, 2), :, lanes] = layer.feed_down(two, p, lanes)

        steps.loop(act, count=seqs // 2)

    def second_norm():
        def act(s):
            down_part(s).wait_recv()
            layer.finish_norm(s)
            down_grad(s).start()
            local(r.final.at[s], r.layer_output.at[s, 0], 2).start()

        steps.loop(act, local(r.cotangent.at[:, 0], r.out_grad, 1).wait)

    def wait_grads():
        def act():
            each(seqs - 1, lambda s: down_grad(s).wait_recv())
            layer.first_down_weight_grad()
            down_grad(seqs - 1).wait_recv()

        waited.append(down_grad)
        steps.once(act)

    def down_grads(m):
        steps.once(lambda: layer.down_weight_grad(m))

    def hidden_back():
        wait = wait_once(down_grad)

        def act(s):
            wait(s)
            layer.hidden_back(s)

        steps.loop(act)

    def up_grads(n):
        steps.once(lambda: layer.up_weight_grad(n // 2, n % 2))

    def back_other():
        def first():
            for group in (4, 5, 6):
                sent(group)

        def act(two):
            r.part_out[pl.ds(2 * two, 2)] = layer.normed_back(two, 1 - p).astype(BF16)
            for s in range(2):
                normed_part(2 * two + s).start()

        steps.loop(act, first, seqs // 2)

    def back_own():
        def act(two):
            r.part_own[pl.ds(2 * two, 2)] = layer.normed_back(two, p)

        steps.loop(act, count=seqs // 2)

    def first_norm():
        def act(s):
            normed_part(s).wait_recv()
            layer.first_norm_back(s)
            branch(s).start()

        steps.loop(act)

    def mixed_grad():
        def act(s):
            branch(s).wait_recv()
            layer.mixed_back(s)

        steps.loop(act)

    def out_grad():
        steps.once(layer.out_weight_grad)
        for one in downs:
            one.drain()

    def attention_back(pair):
        steps.loop(lambda s: layer.attend_back(s, pair))

    def head_grads(pair):
        steps.once(lambda: layer.project_weight_grad(pair))

    def pack_vectors():
        def act():
            for pair in range(3):
                layer.project_bias_grad(pair)
            pack_small(r, p)

        steps.once(act)

    def token_other():
        def act(two):
            r.part_out[pl.ds(2 * two, 2)] = layer.token_back(two, 1 - p).astype(BF16)
            for s in range(2):
                token_part(2 * two + s).start()

        steps.loop(act, lambda: sent(7), seqs // 2)

    def token_own():
        def act(two):
            r.part_own[pl.ds(2 * two, 2)] = layer.token_back(two, p)

        steps.loop(act, count=seqs // 2)

    def token_end():
        def first():
            for one in [small] + heads + ups:
                one.drain()
            for copy in (small_swap, share):
                copy.wait_send()
            to_other(r.stack.at[1 - p], r.stack.at[p], 12, 0).wait_send()
            for group in (3, 8, 10):
                sent(group)

        def act(s):
            token_part(s).wait_recv()
            total = r.part_own[s] + r.part_in[s].astype(F32) + r.resid_grad[s]
            r.token_grad[s] = total.astype(BF16)
            local(r.token_grad.at[s], r.tokens_gradient.at[s, 0], 3).start()

        steps.loop(act, first)

    def collect():
        def act():
            sums_swap.wait_recv()
            r.out_pack[2, 0:16, pack : pack + 256] = r.sum_small[...] + r.sum_theirs[...]
            whole = pack_swap(slice(0, pack))
            whole.wait()
            for one in reduces:
                one.drain()
            sums_swap.wait_send()
            sent(9)
            for outgoing in (2, 3):
                local(r.part_out, r.part_in, outgoing).wait()

        steps.once(act)

    units = dict(
        unpack=unpack,
        att=attention,
        wo=wait_share,
        out=first_half,
        up=feed,
        do=feed_other,
        dw=feed_own,
        ln2=second_norm,
        ddw=wait_grads,
        gd=down_grads,
        hb=hidden_back,
        gu=up_grads,
        no=back_other,
        nw=back_own,
        ln1=first_norm,
        mb=mixed_grad,
        go=out_grad,
        ab=attention_back,
        gq=head_grads,
        ps=pack_vectors,
        to=token_other,
        tw=token_own,
        te=token_end,
        end=collect,
    )
    for name, *which in UNITS:
        units[name](*which)
    assert not steps.waiting


def finish_kernel(r):
    p = lax.axis_index(PAIR)
    half = r.query_out.shape[1] // 2
    size = r.down_out.shape[0]
    for core in range(2):
        for pair in range(3):
            for part, target in enumerate((r.query_out, r.key_out, r.value_out)):
                place = (0, 1, 2, 6, 7, 8, 10, 11, 9)[3 * pair + part]
                at, lane = 128 * place, half * core + 128 * pair
                target[:, lane : lane + 128] = r.pack[core, :, at : at + 128]
        r.out_out[:, half * core : half * core + half] = r.pack[core, :, half : 2 * half]
    rows, width = r.query_out.shape
    groups = []
    for group in range(CHIPS // 4):
        at = 4 * half + 4 * size * group
        groups.append(jnp.concatenate([r.pack[core, :, at : at + 4 * size] for core in range(2)], 1))
    rest = jnp.concatenate(groups, 0)
    parts = []
    for _ in range(3):
        parts.append(rest.astype(BF16).astype(F32))
        rest = rest - parts[-1]
    laid = nt(jnp.concatenate(parts, 0).astype(BF16), ordered(size).astype(BF16))
    count = laid.shape[0] // 3
    laid = laid[:count] + laid[count : 2 * count] + laid[2 * count :]
    for group in range(CHIPS // 4):
        to = 8 * size * group
        r.up_out[:, to : to + 8 * size] = laid[rows * group : rows * group + rows]
    for group in range(size // rows):
        r.down_out[rows * group : rows * group + rows] = r.pack[2, :, width * group : width * group + width]
    small = r.pack[2, 0:16, 4 * half + r.up_out.shape[1] // 2 :]
    for vector, target in enumerate(r.vectors):
        row = jnp.where(p == 0, small[2 * vector : 2 * vector + 1], small[2 * vector + 1 : 2 * vector + 2])
        target[...] = row[:, : target.shape[1]]
    row = jnp.where(p == 0, small[0:1], small[1:2])
    r.up_vector[...] = row[:, 128 : 128 + size]


def call(kernel, ins, outs, scratch, semaphores, elsewhere=(), **params):
    names = list(ins) + list(outs) + list(scratch) + list(semaphores)

    def body(*refs):
        kernel(Refs(zip(names, refs)))

    def spec(name):
        return pl.BlockSpec(memory_space=pl.ANY if name in elsewhere else pltpu.VMEM)

    results = pl.pallas_call(
        body,
        out_shape=[jax.ShapeDtypeStruct(*held_as) for held_as in outs.values()],
        in_specs=[spec(name) for name in ins],
        out_specs=[spec(name) for name in outs],
        scratch_shapes=[pltpu.VMEM(*held_as) for held_as in scratch.values()] + list(semaphores.values()),
        compiler_params=pltpu.CompilerParams(**params),
        name=kernel.__name__,
    )(*ins.values())
    return Refs(zip(outs, results))


def fast(
    tokens,
    segment_ids,
    query_weight,
    query_bias,
    key_weight,
    value_weight,
    value_bias,
    out_weight,
    out_bias,
    first_gain,
    first_shift,
    up_weight,
    up_bias,
    down_weight,
    down_bias,
    second_gain,
    second_shift,
    cotangent,
):
    seqs, _, slots, width = tokens.shape
    units = up_weight.shape[1] // 2
    per = up_weight.shape[0]
    half = width // 2
    size = units // CHIPS
    rows = 2 * slots
    space = -(-rows // 128) * 128
    ins = dict(
        tokens=tokens,
        cotangent=cotangent,
        segment_ids=segment_ids,
        query_weight=query_weight,
        key_weight=key_weight,
        value_weight=value_weight,
        out_weight=out_weight,
        up_weight=up_weight,
        down_weight=down_weight,
        query_bias=query_bias,
        value_bias=value_bias,
        out_bias=out_bias,
        first_gain=first_gain,
        first_shift=first_shift,
        down_bias=down_bias,
        second_gain=second_gain,
        second_shift=second_shift,
        up_bias=up_bias,
    )
    pack = 4 * half + units
    outs = dict(
        layer_output=(tokens.shape, BF16),
        tokens_gradient=(tokens.shape, BF16),
        out_pack=((3, per, pack + 256), F32),
    )
    all_rows = seqs * rows
    held = dict(
        stack=((2, per, pack), F32),
        sum_pack=((2 * per, pack), F32),
        small_in=((16, 256), F32),
        small_theirs=((16, 256), F32),
        sum_theirs=((16, 256), F32),
        sum_small=((16, 256), F32),
        small_all=((CHIPS * 16, 256), F32),
        vec=((8, width), F32),
        upb=((1, units), F32),
        gvec=((8, width), F32),
        gacc=((64, width), F32),
        upg=((1, units), F32),
        fill=((seqs, rows, space), BF16),
        probs_grad=((2 * rows, space), F32),
        product=((rows, width), F32),
        score_grad=((rows, 2 * space), BF16),
        x_all=((all_rows, width), BF16),
        wq0=((width, half), BF16),
        wq1=((width, half), BF16),
        wq2o=((width, width), BF16),
        wo=((2, width, half), BF16),
        wup=((width, units), BF16),
        wdown=((units, width), BF16),
        qkv=((3, all_rows, half), BF16),
        pt=((3 * seqs, rows, 2 * space), BF16),
        mixed=((all_rows, width), BF16),
        xhat=((seqs, slots, width), F32),
        rstd=((seqs, slots, 128), F32),
        n_all=((all_rows, width), BF16),
        hidden=((all_rows, units), BF16),
        slope=((all_rows, units), BF16),
        part_own=((seqs, slots, width), F32),
        part_out=((seqs, slots, width), BF16),
        part_in=((seqs, slots, width), BF16),
        out_grad=((seqs, slots, width), BF16),
        final=((seqs, slots, width), BF16),
        token_grad=((seqs, slots, width), BF16),
        resid_grad=((seqs, slots, width), F32),
        dd_all=((all_rows, width), BF16),
        gd=((units, width), BF16),
        first_sum=((half, width), F32),
        land_d0=((Reduce.SLOTS * size, DOWN_SUM_LANES[0].stop), BF16),
        land_d1=((Reduce.SLOTS * size, width - DOWN_SUM_LANES[0].stop), BF16),
        land_u0=((Reduce.SLOTS * 2 * per, UP_SUM_LANES[0].stop), BF16),
        land_u1=((Reduce.SLOTS * 2 * per, units - UP_SUM_LANES[0].stop), BF16),
        land_oq=((Reduce.SLOTS * 2 * per, width), BF16),
        land_q1=((Reduce.SLOTS * 2 * per, half + 128), BF16),
        land_q2=((Reduce.SLOTS * (2 * per + 16), half - 128), BF16),
    )
    dma = pltpu.SemaphoreType.DMA
    semaphores = dict(
        pair_send=dma((13,)),
        pair_recv=dma((9 + 7 * seqs + len(UP_LANES),)),
        gather_send=dma((8,)),
        gather_recv=dma((8, Gather.ARRIVALS)),
        local_done=dma((4,)),
        reduce_send=dma((7,)),
        reduce_recv=dma((7, Reduce.ARRIVALS)),
    )

    def layer(r):
        r.gu = r.hidden.at[0:width]
        last = width + 16 * CHIPS
        r.goq = r.slope.at[0:width, 0 : 2 * half]
        split = 3 * half + 128
        r.gq0 = r.slope.at[0:width, 0:half]
        r.gq1 = r.slope.at[0:width, 2 * half : split]
        r.gq2 = r.slope.at[0:last, split : 4 * half]
        r.go = r.slope.at[0:width, half : 2 * half]
        r.wq = [r.wq0, r.wq1, r.wq2o.at[:, 0:half]]
        r.dqkv = [r.wdown.at[0:all_rows, 0:half], r.wdown.at[0:all_rows, half:width], r.dd_all.at[:, 0:half]]
        r.dm = r.dd_all.at[:, half:width]
        r.land_d = [r.land_d0, r.land_d1]
        r.land_u = [r.land_u0, r.land_u1]
        r.vectors = [
            r.query_bias,
            r.value_bias,
            r.out_bias,
            r.first_gain,
            r.first_shift,
            r.down_bias,
            r.second_gain,
            r.second_shift,
        ]
        layer_kernel(r)

    elsewhere = dict(tokens=1, cotangent=1, layer_output=1, tokens_gradient=1)
    done = call(
        layer, ins, outs, held, semaphores, elsewhere, vmem_limit_bytes=VMEM_BYTES, collective_id=0, has_side_effects=True
    )

    square = ((per, width), F32)
    line = ((1, per), F32)
    finals = dict(
        query_out=square,
        query_vector=line,
        key_out=square,
        value_out=square,
        value_vector=line,
        out_out=square,
        out_vector=line,
        gain_vector=line,
        shift_vector=line,
        up_out=(up_weight.shape, F32),
        up_vector=((1, size), F32),
        down_out=(down_weight.shape, F32),
        down_vector=line,
        last_gain_vector=line,
        last_shift_vector=line,
    )

    def finish(r):
        r.vectors = [
            r.query_vector,
            r.value_vector,
            r.out_vector,
            r.gain_vector,
            r.shift_vector,
            r.down_vector,
            r.last_gain_vector,
            r.last_shift_vector,
        ]
        finish_kernel(r)

    final = call(finish, dict(pack=done.out_pack), finals, {}, {}, vmem_limit_bytes=16 * 1024 * 1024)
    flat = [value[0] if value.shape[0] == 1 else value for value in final.values()]
    return (done.layer_output, done.tokens_gradient, *flat)


def solution(mesh):
    in_specs = (
        P(BATCH, PAIR, None, None),
        P(BATCH, None, None),
        P(AXES, None),
        P(AXES),
        P(AXES, None),
        P(AXES, None),
        P(AXES),
        P(AXES, None),
        P(AXES),
        P(AXES),
        P(AXES),
        P(AXES, None),
        P(AXES),
        P(AXES, None),
        P(AXES),
        P(AXES),
        P(AXES),
        P(BATCH, PAIR, None, None),
    )
    out_specs = (
        P(BATCH, PAIR, None, None),
        P(BATCH, PAIR, None, None),
        P(AXES, None),
        P(AXES),
        P(AXES, None),
        P(AXES, None),
        P(AXES),
        P(AXES, None),
        P(AXES),
        P(AXES),
        P(AXES),
        P(AXES, None),
        P(AXES),
        P(AXES, None),
        P(AXES),
        P(AXES),
        P(AXES),
    )
    small_slice = dict(mesh.shape) == {BATCH: CHIPS, PAIR: 2}
    part = fast if small_slice else local
    return jax.shard_map(part, mesh=mesh, in_specs=in_specs, out_specs=out_specs, check_vma=False)
```
